256 devices in a mesh: wide: 32 (over z, x), narrow: 8 (over y, core).
Axes of the slice: x: 4, y: 4, z: 8, core: 2. Of those that a mesh axis runs over, the one named last changes fastest.
Arguments:
- feats: bfloat16 [256, 262144], P('narrow', 'wide'), may hold values from -6 to 6
- hilbert_pos: int32 [262144], P('wide'), may hold values from 0 to 262143, as said below
- ln_attn: float32 [256], replicated, may hold values from 0.25 to 1.75
- w_qkv: bfloat16 [3, 256, 256], P(None, None, 'narrow'), may hold values from -3.375 to 3.375
- w_proj: bfloat16 [256, 256], P('narrow'), may hold values from -0.375 to 0.375
- ln_pool: float32 [256], replicated, may hold values from 0.25 to 1.75
- w_pool: bfloat16 [256, 512], P(None, 'narrow'), may hold values from -0.375 to 0.375
- cell_of: int32 [262144], P('wide'), may hold values from 0 to 65535, as said below
Outputs:
- block_out: bfloat16 [256, 262144], P('narrow', 'wide')
- coarse: bfloat16 [512, 65536], P('narrow', 'wide')
- unpooled: bfloat16 [512, 262144], P('narrow', 'wide')
The draws below stay inside these ranges and needn't reach their ends.
Inputs may be any that keep to these rules, and one draw needn't show every extreme that they name: A permutation: the point at z-order position i (on device i // 8192 of wide) moves to Hilbert position hilbert_pos[i], on device hilbert_pos[i] // 8192. Every device receives exactly 8192 points; a device sends at most 512 points to any one device, and exactly 512 to some device. The point at Hilbert position i pools into cell cell_of[i], owned by device cell_of[i] // 2048. Every owner receives exactly 8192 points; a device sends at most 384 points to any one owner, and exactly 384 to some owner. The live cells of an owner are the first 1024 to 2048 of its range, each with one point or more; the last owner has all 2048 live.
All inputs are finite; a program needn't handle non-finite values.
Results may differ from the reference program's by a relative error of at most 0.009.
The reference program's roundings to bfloat16 on the way (of `ordered`, `normed`, `projections`, `probs`, `attended`, `pool_normed` and `projected`) count: a program that leaves them out, or rounds other values in their place, can miss the bound.
Values may be sent and summed in bfloat16 or wider, within the bound.
A program may use at most 128 MiB of HBM per device.

```python
import jax
import jax.numpy as jnp
from jax import lax

C = 256
C2 = 512
HD = 16
PATCH = 1024
P_DEV = 8192
HEADS = 16
POINTS = 262144
CAP = 512
PCAP = 384
CELLS_DEV = 2048
CELLS = 65536
N_WIDE = 32


def shuffle_rows(sub_key):
    return jax.random.permutation(sub_key, P_DEV).astype(jnp.int32)


def route_rows(key, capacity):
    parts = jax.random.split(key, 5)
    devices_wide = N_WIDE
    perm_rows = jax.random.permutation(parts[0], devices_wide).astype(jnp.int32)
    perm_cols = jax.random.permutation(parts[1], devices_wide).astype(jnp.int32)
    latin_square = (perm_rows[:, None] + perm_cols[None, :]) % devices_wide
    remaining = P_DEV - capacity
    quotient = remaining // (devices_wide - 1)
    leftover = remaining - quotient * (devices_wide - 1)
    jitter_range = max(1, min(quotient, capacity - quotient - 1) * 4 // 5)
    jitter = jax.random.randint(parts[2], (devices_wide - 1,), 0, jitter_range).astype(jnp.int32)
    base_load = quotient + (jnp.arange(devices_wide - 1) < leftover).astype(jnp.int32)
    tail_load = (base_load + jitter - jnp.roll(jitter, 1)).astype(jnp.int32)
    load_levels = jnp.concatenate([jnp.full((1,), capacity, jnp.int32), tail_load])
    counts = load_levels[latin_square]
    send_end = jnp.cumsum(counts, axis=1)
    send_start = send_end - counts
    recv_offset = jnp.cumsum(counts, axis=0) - counts
    ranks_all = jnp.arange(P_DEV, dtype=jnp.int32)
    targets = jnp.sum((ranks_all[None, :, None] >= send_end[:, None, :]).astype(jnp.int32), axis=2)
    within = ranks_all[None, :] - jnp.take_along_axis(send_start, targets, axis=1)
    arrival = jnp.take_along_axis(recv_offset, targets, axis=1) + within
    shuffles = jax.vmap(shuffle_rows)(jax.random.split(parts[3], devices_wide))
    landing = shuffles[targets, arrival]
    orders = jax.vmap(shuffle_rows)(jax.random.split(parts[4], devices_wide))
    device_ids = jnp.arange(devices_wide, dtype=jnp.int32)[:, None]
    target_rows = jnp.zeros((devices_wide, P_DEV), jnp.int32).at[device_ids, orders].set(targets)
    landing_rows = jnp.zeros((devices_wide, P_DEV), jnp.int32).at[device_ids, orders].set(landing)
    return (target_rows, landing_rows)


def draw_hilbert_pos(key, part):
    key = jax.random.fold_in(key, 11)
    owners, landing = route_rows(key, CAP)
    return (owners * P_DEV + landing).reshape(-1).astype(jnp.int32)


def draw_cell_of(key, part):
    key = jax.random.fold_in(key, 23)
    route_key, live_key, pick_key, spill_key = jax.random.split(key, 4)
    owners, landing = route_rows(route_key, PCAP)
    live_cells = jax.random.randint(live_key, (N_WIDE,), CELLS_DEV // 2, CELLS_DEV + 1).astype(jnp.int32)
    live_cells = live_cells.at[jax.random.randint(pick_key, (), 0, N_WIDE)].set(CELLS_DEV)
    live_cells = live_cells.at[N_WIDE - 1].set(CELLS_DEV)
    owner_live = live_cells[owners]
    spill = jax.random.randint(spill_key, owners.shape, 0, 1 << 20).astype(jnp.int32) % owner_live
    local_cell = jnp.where(landing < owner_live, landing, spill)
    return (owners * CELLS_DEV + local_cell).reshape(-1).astype(jnp.int32)


def draw_w_qkv(key, part):
    key = jax.random.fold_in(key, 37)
    normal_key = jax.random.fold_in(key, 0)
    matrix = jnp.clip(jax.random.normal(normal_key, (3, C, C), jnp.float32), -6.0, 6.0) * C ** (-0.5)
    return matrix.astype(jnp.bfloat16)


def shard_levels(rng, dims, shards, least, largest):
    level = 1.0
    for axis_at, shards_of in shards:
        steps = jax.random.uniform(jax.random.fold_in(jax.random.fold_in(rng, 6), axis_at), (shards_of,), jnp.float32, least / len(shards), largest / len(shards))
        level = level * jnp.repeat(jnp.exp(steps), dims[axis_at] // shards_of).reshape((-1,) + (1,) * (len(dims) - 1 - axis_at))
    return level


def bell_draw(stream_key, shape, deviation, reach, cuts=(), kind=jnp.bfloat16):
    loudness = shard_levels(stream_key, shape, cuts, -0.22, 0.18) if cuts else 1.0
    values = jax.random.normal(stream_key, shape, jnp.float32) * deviation * loudness
    return jnp.minimum(jnp.maximum(values, -reach), reach).astype(kind)


def setup_inputs(seed: int = 0) -> dict:
    key_of = jax.random.split(jax.random.key(seed), 9)
    return {
        "feats": bell_draw(key_of[0], (C, POINTS), 1.0, 6.0, ((0, 8), (1, 32))),
        "hilbert_pos": draw_hilbert_pos(jax.random.fold_in(key_of[8], 71), 0),
        "ln_attn": jnp.clip(1.0 + 0.15 * jax.random.normal(key_of[2], (C,), jnp.float32), 0.25, 1.75),
        "w_qkv": draw_w_qkv(jax.random.fold_in(key_of[8], 71), 0),
        "w_proj": bell_draw(key_of[4], (C, C), C ** -0.5, 0.375, ((0, 8),)),
        "ln_pool": jnp.clip(1.0 + 0.15 * jax.random.normal(key_of[5], (C,), jnp.float32), 0.25, 1.75),
        "w_pool": bell_draw(key_of[6], (C, C2), C ** -0.5, 0.375, ((1, 8),)),
        "cell_of": draw_cell_of(jax.random.fold_in(key_of[8], 71), 0),
    }


def layer_norm(values, gain_row):
    widened = values.astype(jnp.float32)
    average = lax.optimization_barrier(jnp.mean(widened, axis=0, keepdims=True))
    centred = widened - average
    spread = lax.optimization_barrier(jnp.mean(centred * centred, axis=0, keepdims=True))
    return (centred * lax.rsqrt(spread + 1e-05) * gain_row[:, None]).astype(jnp.bfloat16)

def reference(feats, hilbert_pos, ln_attn, w_qkv, w_proj, ln_pool, w_pool, cell_of):
    ordered = jnp.zeros_like(feats).at[:, hilbert_pos].set(feats)
    normed = layer_norm(ordered, ln_attn)
    projections = jnp.einsum('tco,cp->top', w_qkv.astype(jnp.float32), normed.astype(jnp.float32)).astype(jnp.bfloat16)
    queries = projections[0].reshape(HEADS, HD, POINTS)
    key_rows = projections[1].reshape(HEADS, HD, POINTS)
    value_rows = projections[2].reshape(HEADS, HD, POINTS)
    score_scale = HD ** (-0.5)

    def one_patch(patch_id):
        patch_start = patch_id * PATCH
        query_part = lax.dynamic_slice_in_dim(queries, patch_start, PATCH, 2).astype(jnp.float32)
        key_part = lax.dynamic_slice_in_dim(key_rows, patch_start, PATCH, 2).astype(jnp.float32)
        value_part = lax.dynamic_slice_in_dim(value_rows, patch_start, PATCH, 2).astype(jnp.float32)
        scores = jnp.einsum('hdi,hdj->hij', query_part, key_part) * score_scale
        row_max = lax.optimization_barrier(jnp.max(scores, axis=-1, keepdims=True))
        expo = jnp.exp(scores - row_max)
        probs = (expo / lax.optimization_barrier(jnp.sum(expo, axis=-1, keepdims=True))).astype(jnp.bfloat16)
        return jnp.einsum('hij,hdj->hdi', probs.astype(jnp.float32), value_part).astype(jnp.bfloat16)
    blocks = lax.map(one_patch, jnp.arange(POINTS // PATCH, dtype=jnp.int32))
    attended = jnp.transpose(blocks, (1, 2, 0, 3)).reshape(C, POINTS)
    attn_sum = jnp.dot(w_proj.T, attended, preferred_element_type=jnp.float32)
    block_out = (ordered.astype(jnp.float32) + attn_sum).astype(jnp.bfloat16)
    pool_normed = layer_norm(block_out, ln_pool)
    projected = jnp.dot(w_pool.T, pool_normed, preferred_element_type=jnp.float32).astype(jnp.bfloat16)
    cell_sums = jnp.zeros((C2, CELLS), jnp.float32).at[:, cell_of].add(projected.astype(jnp.float32))
    cell_counts = jnp.zeros((CELLS,), jnp.float32).at[cell_of].add(1.0)
    pooled = cell_sums / jnp.maximum(cell_counts, 1.0)
    coarse = jax.nn.gelu(pooled, approximate=False).astype(jnp.bfloat16)
    unpooled = coarse[:, cell_of]
    return (block_out, coarse, unpooled)
```

```python
import functools

import jax
import jax.numpy as jnp
import numpy as np
from jax import lax
from jax.experimental import pallas as pl
from jax.experimental.pallas import tpu as pltpu
from jax.sharding import PartitionSpec as P

HD = 16
HEADS = 16
C = 256
C2 = 512
PATCH = 1024
POINTS = 8192
GROUPS = 32
BANDS = 8
CH = C // BANDS
CH2 = C2 // BANDS
LO = 8
HROWS = 64
PROWS = 48
CELLS = 2048
CHI = CELLS // LO
BF = jnp.bfloat16
F32 = jnp.float32
NT = (((1,), (1,)), ((), ()))
PARAMS = pltpu.CompilerParams(vmem_limit_bytes=56 * 1024 * 1024)
SCORE = float(HD**-0.5 * np.log2(np.e))


def call(kernel, out_shape, scratch=()):
    return pl.pallas_call(
        kernel, out_shape=out_shape, scratch_shapes=list(scratch), compiler_params=PARAMS
    )


def shape(dims, dtype):
    return jax.ShapeDtypeStruct(dims, dtype)


def one_hot(row, first, count):
    numbers = lax.broadcasted_iota(jnp.int32, (count, row.shape[1]), 0)
    return jnp.where(numbers == row - first, 1.0, 0.0).astype(BF)


def spread(values, low):
    wide = values.astype(F32)
    return jnp.concatenate([jnp.where(low == l, wide, 0.0).astype(BF) for l in range(LO)], axis=0)


def gather_low(product, low, channels):
    total = jnp.where(low == 0, product[:channels], 0.0)
    for l in range(1, LO):
        total += jnp.where(low == l, product[l * channels : (l + 1) * channels], 0.0)
    return total


def slots_kernel(rows, shift, goal_ref, value_ref, row_ref, low_ref, table_ref):
    k = 512
    before = lax.broadcasted_iota(jnp.int32, (k, k), 0) < lax.broadcasted_iota(jnp.int32, (k, k), 1)
    before = jnp.where(before, 1.0, 0.0).astype(BF)
    carry = jnp.zeros((GROUPS, 1), F32)
    table = jnp.zeros((GROUPS * LO, 2 * rows), F32)
    for j in range(POINTS // k):
        at = slice(j * k % PATCH, j * k % PATCH + k)
        of = slice(j * k // PATCH, j * k // PATCH + 1)
        goal = goal_ref[of, at]
        member = lax.broadcasted_iota(jnp.int32, (GROUPS, k), 0) == goal
        hot = jnp.where(member, 1.0, 0.0)
        running = jnp.dot(hot.astype(BF), before, preferred_element_type=F32) + carry
        carry = carry + jnp.sum(hot, axis=1, keepdims=True)
        rank = jnp.sum(hot * running, axis=0, keepdims=True).astype(jnp.int32)
        low = jnp.zeros_like(rank)
        for l in range(1, LO):
            low += jnp.where(rank >= l * rows, 1, 0)
        high = rank - low * rows
        row_ref[of, at] = goal * rows + high
        low_ref[of, at] = low
        value = value_ref[of, at] + 1
        which = lax.broadcasted_iota(jnp.int32, (rows, k), 0) == high
        parts = [
            jnp.where(which, part.astype(F32), 0.0) for part in (value >> shift, value & ((1 << shift) - 1))
        ]
        marks = jnp.concatenate(parts, axis=0).astype(BF)
        table += lax.dot_general(
            one_hot(goal * LO + low, 0, GROUPS * LO), marks, NT, preferred_element_type=F32
        )
    table_ref[...] = (table[:, :rows] * (1 << shift) + table[:, rows:]).astype(jnp.int32) - 1


def slots(goals, values, rows):
    kinds = [shape((BANDS, PATCH), jnp.int32)] * 2 + [shape((GROUPS * LO, rows), jnp.int32)]
    return call(functools.partial(slots_kernel, rows, 7), kinds)(
        goals.reshape(BANDS, PATCH), values.reshape(BANDS, PATCH)
    )


def place(row_of, spread_ref, out_ref, block, k):
    steps = spread_ref.shape[1] // k

    def one_block(b, _):
        total = jnp.zeros((block, spread_ref.shape[0]), F32)
        for j in range(steps):
            total += lax.dot_general(
                one_hot(row_of(j), b * block, block),
                spread_ref[:, j * k : (j + 1) * k],
                NT,
                preferred_element_type=F32,
            )
        out_ref[pl.ds(pl.multiple_of(b * block, block), block), :] = total.astype(out_ref.dtype)
        return 0

    lax.fori_loop(0, out_ref.shape[0] // block, one_block, 0)


def send_kernel(feats_ref, row_ref, low_ref, out_ref, spread_ref):
    for j in range(BANDS):
        at = slice(j * PATCH, (j + 1) * PATCH)
        values = feats_ref[:, at] if len(feats_ref.shape) == 2 else feats_ref[j]
        spread_ref[:, at] = spread(values, low_ref[j : j + 1, :])
    place(lambda j: row_ref[j : j + 1, :], spread_ref, out_ref, 512, PATCH)


def send(values, row, low, rows):
    return call(
        send_kernel,
        shape((GROUPS * rows, LO * CH), BF),
        [pltpu.VMEM((LO * CH, POINTS), BF)],
    )(values, row, low)


def receive_kernel(in_ref, landing_ref, out_ref, spread_ref):
    turned = in_ref[...].T
    k = in_ref.shape[0]
    for l in range(LO):
        landing = landing_ref[l : l + 1, :]
        spread_ref[:, l * k : (l + 1) * k] = spread(
            turned[l * CH : (l + 1) * CH], (landing >> 7) & 7
        )

    def row_of(j):
        landing = landing_ref[j : j + 1, :]
        return (landing >> 10) * 128 + (landing & 127)

    place(row_of, spread_ref, out_ref, 512, k)


def receive(arrived, landing):
    k = arrived.shape[0]
    return call(
        receive_kernel,
        shape((POINTS // LO, LO * CH), BF),
        [pltpu.VMEM((LO * CH, LO * k), BF)],
    )(arrived, landing)


def normalise(wide, gain_ref):
    average = jnp.mean(wide, axis=0, keepdims=True)
    centred = wide - average
    spread_of = jnp.mean(centred * centred, axis=0, keepdims=True)
    return (centred * lax.rsqrt(spread_of + 1e-05) * gain_ref[...]).astype(BF)


def block_kernel(in_ref, weights_ref, gain_ref, gain2_ref, out_ref, x_ref, q_ref, k_ref, v_ref, km_ref, vm_ref, att_ref):
    for n in range(BANDS):
        turned = in_ref[n].T
        for l in range(LO):
            x_ref[n * CH : (n + 1) * CH, l * 128 : (l + 1) * 128] = turned[l * CH : (l + 1) * CH]
    normed = normalise(x_ref[...].astype(F32), gain_ref)

    def weight(first):
        return jnp.concatenate([weights_ref[n, first : first + CH, :] for n in range(BANDS)], axis=0)

    def project(t):
        return jnp.dot(weight(t * CH), normed, preferred_element_type=F32).astype(BF)

    q_ref[...] = project(0).T
    k_ref[...] = project(1)
    v_ref[...] = project(2).T
    att_ref[...] = jnp.zeros_like(att_ref)
    rows = 256

    def one_head(h, _):
        dims = lax.broadcasted_iota(jnp.int32, (C, PATCH), 0) // HD
        km_ref[...] = jnp.where(dims == h, k_ref[...].astype(F32), 0.0).astype(BF)
        lanes = lax.broadcasted_iota(jnp.int32, (PATCH, C), 1) // HD
        vm_ref[...] = jnp.where(lanes == h, v_ref[...].astype(F32), 1.0).astype(BF)
        lane = lax.broadcasted_iota(jnp.int32, (rows, C), 1)
        other = lax.rem(h * HD + C // 2, C)
        for b in range(PATCH // rows):
            at = slice(b * rows, (b + 1) * rows)
            scores = jnp.dot(q_ref[at, :], km_ref[...], preferred_element_type=F32)
            top = jnp.max(scores, axis=1, keepdims=True)
            expo = jnp.exp2((scores - top) * SCORE).astype(BF)
            sums = jnp.dot(expo, vm_ref[...], preferred_element_type=F32)
            whole = jnp.sum(jnp.where(lane == other, sums, 0.0), axis=1, keepdims=True)
            att_ref[at, :] += jnp.where(lane // HD == h, sums * (1.0 / whole), 0.0)
        return 0

    lax.fori_loop(0, HEADS, one_head, 0)
    added = lax.dot_general(
        weight(3 * CH).T, att_ref[...].astype(BF), NT, preferred_element_type=F32
    )
    block = (x_ref[...].astype(F32) + added).astype(BF)
    pooled = normalise(block.astype(F32), gain2_ref)
    for n in range(BANDS):
        out_ref[n, :CH, :] = block[n * CH : (n + 1) * CH]
        out_ref[n, CH:, :] = pooled[n * CH : (n + 1) * CH]


def block(arrived, weights, gain, gain2):
    return call(
        block_kernel,
        shape((BANDS, 2 * CH, PATCH), BF),
        [
            pltpu.VMEM((C, PATCH), BF),
            pltpu.VMEM((PATCH, C), BF),
            pltpu.VMEM((C, PATCH), BF),
            pltpu.VMEM((PATCH, C), BF),
            pltpu.VMEM((C, PATCH), BF),
            pltpu.VMEM((PATCH, C), BF),
            pltpu.VMEM((PATCH, C), F32),
        ],
    )(arrived, weights, gain.reshape(C, 1), gain2.reshape(C, 1))


def pool_kernel(in_ref, cell_ref, out_ref):
    turned = in_ref[...].T
    sums = jnp.zeros((CHI, LO * CH), F32)
    counts = jnp.zeros((CHI, LO * CH), F32)
    for l in range(LO):
        cell = cell_ref[l : l + 1, :]
        low = cell >> 8
        hot = one_hot(cell & (CHI - 1), 0, CHI)
        sums += lax.dot_general(
            hot, spread(turned[l * CH : (l + 1) * CH], low), NT, preferred_element_type=F32
        )
        ones = jnp.ones((CH, cell.shape[1]), F32)
        counts += lax.dot_general(hot, spread(ones, low), NT, preferred_element_type=F32)
    out_ref[...] = (sums / jnp.maximum(counts, 1.0)).T


def pool(arrived, cells):
    return call(pool_kernel, shape((LO * CH, CHI), F32))(arrived, cells)


def coarse_kernel(mean_ref, weights_ref, out_ref):
    mean = mean_ref[...]
    upper = mean.astype(BF)
    lower = (mean - upper.astype(F32)).astype(BF)
    for n in range(BANDS):
        weight = weights_ref[n, 4 * CH :, :]
        value = jnp.dot(weight, upper, preferred_element_type=F32) + jnp.dot(
            weight, lower, preferred_element_type=F32
        )
        out_ref[n] = (value * (1.0 + lax.erf(value * (0.5**0.5))) * 0.5).astype(BF)


def coarse_cells(mean, weights):
    return call(coarse_kernel, shape((BANDS, CH2, CHI), BF))(mean, weights)


def give_kernel(table_ref, cell_ref, out_ref, turned_ref):
    table = table_ref[...]
    for l in range(LO):
        cell = cell_ref[l : l + 1, :]
        product = jnp.dot(table, one_hot(cell & (CHI - 1), 0, CHI), preferred_element_type=F32)
        turned_ref[l * CH2 : (l + 1) * CH2, :] = gather_low(product, cell >> 8, CH2).astype(BF)
    out_ref[...] = turned_ref[...].T


def give(table, cells):
    rows = GROUPS * PROWS
    return call(
        give_kernel,
        shape((rows, LO * CH2), BF),
        [pltpu.VMEM((LO * CH2, rows), BF)],
    )(table, cells)


def take_kernel(in_ref, row_ref, low_ref, out_ref, turned_ref):
    turned_ref[...] = in_ref[...].T
    rows = in_ref.shape[0]
    for j in range(BANDS):
        product = jnp.dot(
            turned_ref[...], one_hot(row_ref[j : j + 1, :], 0, rows), preferred_element_type=F32
        )
        out_ref[:, j * PATCH : (j + 1) * PATCH] = gather_low(
            product, low_ref[j : j + 1, :], CH2
        ).astype(BF)


def take(arrived, row, low):
    rows = GROUPS * PROWS
    return call(
        take_kernel,
        shape((CH2, POINTS), BF),
        [pltpu.VMEM((LO * CH2, rows), BF)],
    )(arrived, row, low)


def exchange(values, axis):
    return lax.all_to_all(values, axis, split_axis=0, concat_axis=0, tiled=True)


def by_low(table, rows):
    return exchange(table, "wide").reshape(GROUPS, LO, rows).transpose(1, 0, 2).reshape(LO, -1)


def on_device(feats, hilbert_pos, ln_attn, w_qkv, w_proj, ln_pool, w_pool, cell_of):
    own = jnp.concatenate([w_qkv.transpose(0, 2, 1).reshape(-1, C), w_proj, w_pool.T], axis=0)
    weights = lax.all_gather(own, "narrow", axis=0)
    row, low, landing = slots(hilbert_pos // POINTS, hilbert_pos % POINTS, HROWS)
    landing = by_low(landing, HROWS)
    arrived = exchange(send(feats, row, low, HROWS), "wide")
    p_row, p_low, cells = slots(cell_of // CELLS, cell_of % CELLS, PROWS)
    cells = by_low(cells, PROWS)
    patch = exchange(receive(arrived, landing), "narrow").reshape(BANDS, PATCH // LO, LO * CH)
    both = exchange(block(patch, weights, ln_attn, ln_pool), "narrow")
    block_out = both[:, :CH].transpose(1, 0, 2).reshape(CH, POINTS)
    incoming = exchange(send(both[:, CH:], p_row, p_low, PROWS), "wide")
    mean = exchange(pool(incoming, cells), "narrow")
    table = exchange(coarse_cells(mean, weights), "narrow")
    coarse = table.transpose(1, 0, 2).reshape(CH2, CELLS)
    came_back = exchange(give(table.reshape(BANDS * CH2, CHI), cells), "wide")
    unpooled = take(came_back, p_row, p_low)
    return (block_out, coarse, unpooled)


def solution(mesh):
    in_specs = (
        P("narrow", "wide"),
        P("wide"),
        P(),
        P(None, None, "narrow"),
        P("narrow", None),
        P(),
        P(None, "narrow"),
        P("wide"),
    )
    out_specs = (P("narrow", "wide"), P("narrow", "wide"), P("narrow", "wide"))
    return jax.shard_map(
        on_device, mesh=mesh, in_specs=in_specs, out_specs=out_specs, check_vma=False
    )
```

```python
import jax
import jax.numpy as jnp
import numpy as np
from jax import lax
from jax.experimental import pallas as pl
from jax.experimental.pallas import tpu as pltpu
from jax.sharding import PartitionSpec as P

HD = 16
HEADS = 16
C = 256
C2 = 512
PATCH = 1024
POINTS = 8192
GROUPS = 32
BANDS = 8
CH = C // BANDS
CH2 = C2 // BANDS
LO = 8
TAB = 128
HROWS = 64
PROWS = 48
CELLS = 2048
CHI = CELLS // LO
BF = jnp.bfloat16
F32 = jnp.float32
NT = (((1,), (1,)), ((), ()))
SCORE = float(HD**-0.5 * np.log2(np.e))


def shape(dims, dtype):
    return jax.ShapeDtypeStruct(dims, dtype)


def one_hot(row, first, count):
    numbers = lax.broadcasted_iota(jnp.int32, (count, row.shape[1]), 0)
    return jnp.where(numbers == row - first, 1.0, 0.0).astype(BF)


def spread(values, low):
    wide = values.astype(F32)
    return jnp.concatenate([jnp.where(low == l, wide, 0.0).astype(BF) for l in range(LO)], axis=0)


def gather_low(product, low, channels):
    total = jnp.where(low == 0, product[:channels], 0.0)
    for l in range(1, LO):
        total += jnp.where(low == l, product[l * channels : (l + 1) * channels], 0.0)
    return total


def make_slots(rows, goals, values, row_ref, low_ref, table_ref):
    k = 512
    before = lax.broadcasted_iota(jnp.int32, (k, k), 0) < lax.broadcasted_iota(jnp.int32, (k, k), 1)
    before = jnp.where(before, 1.0, 0.0).astype(BF)
    carry = jnp.zeros((GROUPS, 1), F32)
    table = jnp.zeros((GROUPS * LO, 2 * TAB), F32)
    for j in range(POINTS // k):
        at = slice(j * k % PATCH, j * k % PATCH + k)
        of = slice(j * k // PATCH, j * k // PATCH + 1)
        goal = goals[of, at]
        member = lax.broadcasted_iota(jnp.int32, (GROUPS, k), 0) == goal
        hot = jnp.where(member, 1.0, 0.0)
        running = jnp.dot(hot.astype(BF), before, preferred_element_type=F32) + carry
        carry = carry + jnp.sum(hot, axis=1, keepdims=True)
        rank = jnp.sum(hot * running, axis=0, keepdims=True).astype(jnp.int32)
        low = jnp.zeros_like(rank)
        for l in range(1, LO):
            low += jnp.where(rank >= l * rows, 1, 0)
        high = rank - low * rows
        row_ref[of, at] = goal * rows + high
        low_ref[of, at] = low
        value = values[of, at] + 1
        which = lax.broadcasted_iota(jnp.int32, (TAB, k), 0) == high
        parts = [
            jnp.where(which, part.astype(F32), 0.0) for part in (value >> 7, value & 127)
        ]
        marks = jnp.concatenate(parts, axis=0).astype(BF)
        table += lax.dot_general(
            one_hot(goal * LO + low, 0, GROUPS * LO), marks, NT, preferred_element_type=F32
        )
    table = (table[:, :TAB] * 128.0 + table[:, TAB:]).astype(jnp.int32) - 1
    table_ref[...] = table.reshape(GROUPS, LO, TAB)


def place(row_ref, spread_ref, first, count):
    total = jnp.zeros((count, spread_ref.shape[0]), F32)
    for j in range(BANDS):
        total += lax.dot_general(
            one_hot(row_ref[j : j + 1, :], first, count),
            spread_ref[:, j * PATCH : (j + 1) * PATCH],
            NT,
            preferred_element_type=F32,
        )
    return total


def normalise(wide, gain_ref):
    average = jnp.mean(wide, axis=0, keepdims=True)
    centred = wide - average
    spread_of = jnp.mean(centred * centred, axis=0, keepdims=True)
    return (centred * lax.rsqrt(spread_of + 1e-05) * gain_ref[...]).astype(BF)


def remote(src, dst, send_sem, recv_sem, wide, narrow):
    return pltpu.make_async_remote_copy(
        src_ref=src,
        dst_ref=dst,
        send_sem=send_sem,
        recv_sem=recv_sem,
        device_id={"wide": wide, "narrow": narrow},
        device_id_type=pl.DeviceIdType.MESH,
    )


class Wide:
    def __init__(self, src, dst, send_sem, recv_sem, sign):
        self.src, self.dst, self.send_sem, self.recv_sem, self.sign = src, dst, send_sem, recv_sem, sign

    def copy(self, t):
        goal = (lax.axis_index("wide") + self.sign * t + GROUPS) % GROUPS
        return remote(
            self.src.at[t],
            self.dst.at[t],
            self.send_sem.at[t],
            self.recv_sem.at[t],
            goal,
            lax.axis_index("narrow"),
        )

    def start(self, group):
        @pl.when(group == 0)
        def _():
            self.dst[0] = self.src[0]

        def one(i, _):
            t = group * 8 + i

            @pl.when(t > 0)
            def _():
                self.copy(t).start()

            return 0

        lax.fori_loop(0, 8, one, 0)

    def wait(self, group):
        def one(i, _):
            t = group * 8 + i

            @pl.when(t > 0)
            def _():
                self.copy(t).wait_recv()

            return 0

        lax.fori_loop(0, 8, one, 0)

    def finish(self):
        lax.fori_loop(1, GROUPS, lambda t, _: self.copy(t).wait_send() or 0, 0)


class Narrow:
    def __init__(self, src, dst, send_sem, recv_sem, whole=False):
        self.src, self.dst, self.send_sem, self.recv_sem = src, dst, send_sem, recv_sem
        self.whole = whole

    def copy(self, step):
        me = lax.axis_index("narrow")
        goal = (me + step) % BANDS
        return remote(
            self.src if self.whole else self.src.at[goal],
            self.dst.at[me],
            self.send_sem.at[step],
            self.recv_sem.at[step],
            lax.axis_index("wide"),
            goal,
        )

    def start(self):
        me = lax.axis_index("narrow")
        lax.fori_loop(1, BANDS, lambda s, _: self.copy(s).start() or 0, 0)
        self.dst[me] = self.src[...] if self.whole else self.src[me]

    def wait(self):
        me = lax.axis_index("narrow")

        def one(step, _):
            landed = self.dst.at[(me - step + BANDS) % BANDS]
            remote(
                landed,
                landed,
                self.send_sem.at[step],
                self.recv_sem.at[step],
                lax.axis_index("wide"),
                me,
            ).wait_recv()
            return 0

        lax.fori_loop(1, BANDS, one, 0)

    def finish(self):
        lax.fori_loop(1, BANDS, lambda s, _: self.copy(s).wait_send() or 0, 0)


def attend(x_ref, q_ref, k_ref, v_ref, km_ref, vm_ref, att_ref):
    att_ref[...] = jnp.zeros_like(att_ref)
    rows = 256

    def one_head(h, _):
        dims = lax.broadcasted_iota(jnp.int32, (C, PATCH), 0) // HD
        km_ref[...] = jnp.where(dims == h, k_ref[...].astype(F32), 0.0).astype(BF)
        lanes = lax.broadcasted_iota(jnp.int32, (PATCH, C), 1) // HD
        vm_ref[...] = jnp.where(lanes == h, v_ref[...].astype(F32), 1.0).astype(BF)
        lane = lax.broadcasted_iota(jnp.int32, (rows, C), 1)
        other = lax.rem(h * HD + C // 2, C)
        for b in range(PATCH // rows):
            at = slice(b * rows, (b + 1) * rows)
            scores = jnp.dot(q_ref[at, :], km_ref[...], preferred_element_type=F32)
            top = jnp.max(scores, axis=1, keepdims=True)
            expo = jnp.exp2((scores - top) * SCORE).astype(BF)
            sums = jnp.dot(expo, vm_ref[...], preferred_element_type=F32)
            whole = jnp.sum(jnp.where(lane == other, sums, 0.0), axis=1, keepdims=True)
            att_ref[at, :] += jnp.where(lane // HD == h, sums * (1.0 / whole), 0.0)
        return 0

    lax.fori_loop(0, HEADS, one_head, 0)


def lanes_of(table_ref, group, rows):
    return jnp.concatenate([table_ref[group * 8 + i, :, :rows] for i in range(8)], axis=1)


def kernel(
    feats_ref, hilbert_ref, cell_ref, own_ref, gain_ref, gain2_ref,
    block_ref, coarse_ref, unpooled_ref,
    row_ref, low_ref, p_row_ref, p_low_ref,
    land_out, land_in, cell_out, cell_in,
    spread_ref, first_out, first_in, acc_ref,
    patch_out, patch_in, weights_ref,
    x_ref, q_ref, k_ref, v_ref, km_ref, vm_ref, att_ref,
    both_out, both_in, second_out, second_in,
    sum_ref, count_ref, mean_out, mean_in, table_out, table_in,
    turned_ref, back_out, back_in,
    wide_send, wide_recv, narrow_send, narrow_recv,
):
    me = lax.axis_index("wide")
    mine = lax.axis_index("narrow")

    def wide(number, src, dst, sign=1):
        return Wide(src, dst, wide_send.at[number], wide_recv.at[number], sign)

    def narrow(number, src, dst, whole=False):
        return Narrow(src, dst, narrow_send.at[number], narrow_recv.at[number], whole)

    landings = wide(0, land_out, land_in)
    first = wide(1, first_out, first_in)
    cells = wide(2, cell_out, cell_in)
    second = wide(3, second_out, second_in)
    back = wide(4, back_out, back_in, -1)
    gather = narrow(0, own_ref, weights_ref, True)
    patches = narrow(1, patch_out, patch_in)
    boths = narrow(2, both_out, both_in)
    means = narrow(3, mean_out, mean_in)
    tables = narrow(4, table_out, table_in)

    barrier = pltpu.get_barrier_semaphore()

    def greet_wide(t, _):
        pl.semaphore_signal(
            barrier,
            inc=1,
            device_id={"wide": (me + t) % GROUPS, "narrow": mine},
            device_id_type=pl.DeviceIdType.MESH,
        )
        return 0

    def greet_narrow(t, _):
        pl.semaphore_signal(
            barrier,
            inc=1,
            device_id={"wide": me, "narrow": (mine + t) % BANDS},
            device_id_type=pl.DeviceIdType.MESH,
        )
        return 0

    lax.fori_loop(1, GROUPS, greet_wide, 0)
    lax.fori_loop(1, BANDS, greet_narrow, 0)

    position = hilbert_ref[...]
    make_slots(
        HROWS, ((position >> 13) - me) & (GROUPS - 1), position & (POINTS - 1), row_ref, low_ref, land_out
    )
    for j in range(BANDS):
        at = slice(j * PATCH, (j + 1) * PATCH)
        spread_ref[:, at] = spread(feats_ref[:, at], low_ref[j : j + 1, :])
    pl.semaphore_wait(barrier, GROUPS + BANDS - 2)
    gather.start()
    for g in range(4):
        landings.start(g)

    def first_block(g, _):
        chunk = place(row_ref, spread_ref, g * 512, 512).astype(BF)
        first_out[pl.ds(g * 8, 8)] = chunk.reshape(8, HROWS, LO * CH)
        first.start(g)
        return 0

    lax.fori_loop(0, 4, first_block, 0)

    cell = cell_ref[...]
    make_slots(
        PROWS, ((cell >> 11) - me) & (GROUPS - 1), cell & (CELLS - 1), p_row_ref, p_low_ref, cell_out
    )
    for g in range(4):
        cells.start(g)

    def first_group(g, _):
        landings.wait(g)
        first.wait(g)
        k = 8 * HROWS
        turned = first_in[pl.ds(g * 8, 8)].reshape(k, LO * CH).T
        landing = lanes_of(land_in, g, HROWS)
        for l in range(LO):
            spread_ref[:, l * k : (l + 1) * k] = spread(
                turned[l * CH : (l + 1) * CH], (landing[l : l + 1] >> 7) & 7
            )
        rows = (landing >> 10) * 128 + (landing & 127)
        for m in range(2):
            total = jnp.zeros((512, LO * CH), F32)
            for l in range(LO):
                total += lax.dot_general(
                    one_hot(rows[l : l + 1], m * 512, 512),
                    spread_ref[:, l * k : (l + 1) * k],
                    NT,
                    preferred_element_type=F32,
                )
            at = slice(m * 512, (m + 1) * 512)
            acc_ref[at, :] = jnp.where(g == 0, total, total + acc_ref[at, :])
        return 0

    lax.fori_loop(0, 4, first_group, 0)
    patch_out[...] = acc_ref[...].astype(BF).reshape(BANDS, PATCH // LO, LO * CH)
    patches.start()
    gather.wait()
    patches.wait()

    for n in range(BANDS):
        turned = patch_in[n].T
        for l in range(LO):
            x_ref[n * CH : (n + 1) * CH, l * 128 : (l + 1) * 128] = turned[l * CH : (l + 1) * CH]
    normed = normalise(x_ref[...].astype(F32), gain_ref)

    def weight(start):
        return jnp.concatenate([weights_ref[n, start : start + CH, :] for n in range(BANDS)], axis=0)

    def project(t):
        return jnp.dot(weight(t * CH), normed, preferred_element_type=F32).astype(BF)

    q_ref[...] = project(0).T
    k_ref[...] = project(1)
    v_ref[...] = project(2).T
    attend(x_ref, q_ref, k_ref, v_ref, km_ref, vm_ref, att_ref)
    added = lax.dot_general(
        weight(3 * CH).T, att_ref[...].astype(BF), NT, preferred_element_type=F32
    )
    block = (x_ref[...].astype(F32) + added).astype(BF)
    pooled = normalise(block.astype(F32), gain2_ref)
    for n in range(BANDS):
        both_out[n, :CH, :] = pooled[n * CH : (n + 1) * CH]
        both_out[n, CH:, :] = block[n * CH : (n + 1) * CH]
    boths.start()
    boths.wait()

    for j in range(BANDS):
        at = slice(j * PATCH, (j + 1) * PATCH)
        spread_ref[:, at] = spread(both_in[j, :CH, :], p_low_ref[j : j + 1, :])

    def second_block(g, _):
        chunk = place(p_row_ref, spread_ref, g * 384, 384).astype(BF)
        second_out[pl.ds(g * 8, 8)] = chunk.reshape(8, PROWS, LO * CH)
        second.start(g)
        return 0

    lax.fori_loop(0, 4, second_block, 0)
    for j in range(BANDS):
        block_ref[:, j * PATCH : (j + 1) * PATCH] = both_in[j, CH:, :]
    sum_ref[...] = jnp.zeros_like(sum_ref)
    count_ref[...] = jnp.zeros_like(count_ref)
    k = 8 * PROWS

    def count_group(g, _):
        cells.wait(g)
        cell = lanes_of(cell_in, g, PROWS)
        ones = jnp.ones((CH, k), F32)
        for l in range(LO):
            count_ref[...] += lax.dot_general(
                one_hot(cell[l : l + 1] & (CHI - 1), 0, CHI),
                spread(ones, cell[l : l + 1] >> 8),
                NT,
                preferred_element_type=F32,
            )
        return 0

    lax.fori_loop(0, 4, count_group, 0)

    def second_group(g, _):
        second.wait(g)
        turned = second_in[pl.ds(g * 8, 8)].reshape(k, LO * CH).T
        cell = lanes_of(cell_in, g, PROWS)
        for l in range(LO):
            sum_ref[...] += lax.dot_general(
                one_hot(cell[l : l + 1] & (CHI - 1), 0, CHI),
                spread(turned[l * CH : (l + 1) * CH], cell[l : l + 1] >> 8),
                NT,
                preferred_element_type=F32,
            )
        return 0

    lax.fori_loop(0, 4, second_group, 0)
    mean_out[...] = (sum_ref[...] / jnp.maximum(count_ref[...], 1.0)).T.reshape(BANDS, CH, CHI)
    means.start()
    means.wait()

    mean = mean_in[...].reshape(C, CHI)
    upper = mean.astype(BF)
    lower = (mean - upper.astype(F32)).astype(BF)
    for n in range(BANDS):
        weight_n = weights_ref[n, 4 * CH :, :]
        value = jnp.dot(weight_n, upper, preferred_element_type=F32) + jnp.dot(
            weight_n, lower, preferred_element_type=F32
        )
        table_out[n] = (value * (1.0 + lax.erf(value * (0.5**0.5))) * 0.5).astype(BF)
    tables.start()
    tables.wait()

    table = table_in[...].reshape(BANDS * CH2, CHI)

    def give_group(g, _):
        cell = lanes_of(cell_in, g, PROWS)
        for l in range(LO):
            product = jnp.dot(
                table, one_hot(cell[l : l + 1] & (CHI - 1), 0, CHI), preferred_element_type=F32
            )
            turned_ref[l * CH2 : (l + 1) * CH2, :] = gather_low(
                product, cell[l : l + 1] >> 8, CH2
            ).astype(BF)
        back_out[pl.ds(g * 8, 8)] = turned_ref[...].T.reshape(8, PROWS, LO * CH2)
        back.start(g)
        return 0

    lax.fori_loop(0, 4, give_group, 0)
    for n in range(BANDS):
        coarse_ref[:, n * CHI : (n + 1) * CHI] = table_in[n]
    unpooled_ref[...] = jnp.zeros_like(unpooled_ref)

    def take_group(g, _):
        back.wait(g)
        turned_ref[...] = back_in[pl.ds(g * 8, 8)].reshape(k, LO * CH2).T
        for j in range(BANDS):
            at = slice(j * PATCH, (j + 1) * PATCH)
            product = jnp.dot(
                turned_ref[...], one_hot(p_row_ref[j : j + 1, :], g * k, k), preferred_element_type=F32
            )
            part = gather_low(product, p_low_ref[j : j + 1, :], CH2)
            unpooled_ref[:, at] = (unpooled_ref[:, at].astype(F32) + part).astype(BF)
        return 0

    lax.fori_loop(0, 4, take_group, 0)
    for each in (landings, first, cells, second, back, gather, patches, boths, means, tables):
        each.finish()


def on_device(feats, hilbert_pos, ln_attn, w_qkv, w_proj, ln_pool, w_pool, cell_of):
    own = jnp.concatenate([w_qkv.transpose(0, 2, 1).reshape(-1, C), w_proj, w_pool.T], axis=0)
    small = lambda: pltpu.VMEM((BANDS, PATCH), jnp.int32)
    table = lambda: pltpu.VMEM((GROUPS, LO, TAB), jnp.int32)
    half = lambda *dims: pltpu.VMEM(dims, BF)
    full = lambda *dims: pltpu.VMEM(dims, F32)
    return tuple(
        pl.pallas_call(
            kernel,
            out_shape=[
                jax.ShapeDtypeStruct((CH, POINTS), BF),
                jax.ShapeDtypeStruct((CH2, CELLS), BF),
                jax.ShapeDtypeStruct((CH2, POINTS), BF),
            ],
            in_specs=[pl.BlockSpec(memory_space=pltpu.VMEM)] * 6,
            out_specs=[pl.BlockSpec(memory_space=pltpu.VMEM)] * 3,
            scratch_shapes=[
                small(), small(), small(), small(),
                table(), table(), table(), table(),
                half(LO * CH, POINTS),
                half(GROUPS, HROWS, LO * CH), half(GROUPS, HROWS, LO * CH),
                full(PATCH, LO * CH),
                half(BANDS, PATCH // LO, LO * CH), half(BANDS, PATCH // LO, LO * CH),
                half(BANDS, 6 * CH, C),
                half(C, PATCH), half(PATCH, C), half(C, PATCH), half(PATCH, C),
                half(C, PATCH), half(PATCH, C), full(PATCH, C),
                half(BANDS, 2 * CH, PATCH), half(BANDS, 2 * CH, PATCH),
                half(GROUPS, PROWS, LO * CH), half(GROUPS, PROWS, LO * CH),
                full(CHI, LO * CH), full(CHI, LO * CH),
                full(BANDS, CH, CHI), full(BANDS, CH, CHI),
                half(BANDS, CH2, CHI), half(BANDS, CH2, CHI),
                half(LO * CH2, 8 * PROWS),
                half(GROUPS, PROWS, LO * CH2), half(GROUPS, PROWS, LO * CH2),
                pltpu.SemaphoreType.DMA((5, GROUPS)), pltpu.SemaphoreType.DMA((5, GROUPS)),
                pltpu.SemaphoreType.DMA((5, BANDS)), pltpu.SemaphoreType.DMA((5, BANDS)),
            ],
            compiler_params=pltpu.CompilerParams(
                collective_id=0, has_side_effects=True, vmem_limit_bytes=56 * 1024 * 1024
            ),
        )(
            feats,
            hilbert_pos.reshape(BANDS, PATCH),
            cell_of.reshape(BANDS, PATCH),
            own,
            ln_attn.reshape(C, 1),
            ln_pool.reshape(C, 1),
        )
    )


def solution(mesh):
    in_specs = (
        P("narrow", "wide"),
        P("wide"),
        P(),
        P(None, None, "narrow"),
        P("narrow", None),
        P(),
        P(None, "narrow"),
        P("wide"),
    )
    out_specs = (P("narrow", "wide"), P("narrow", "wide"), P("narrow", "wide"))
    return jax.shard_map(
        on_device, mesh=mesh, in_specs=in_specs, out_specs=out_specs, check_vma=False
    )
```

```python
import jax
import jax.numpy as jnp
import numpy as np
from jax import lax
from jax.experimental import pallas as pl
from jax.experimental.pallas import tpu as pltpu
from jax.sharding import PartitionSpec as P

HD = 16
HEADS = 16
C = 256
C2 = 512
PATCH = 1024
POINTS = 8192
GROUPS = 32
BANDS = 8
CH = C // BANDS
CH2 = C2 // BANDS
LO = 8
TAB = 128
OWN = 1
COLS = 512
HROWS = 64
PROWS = 48
CELLS = 2048
CHI = CELLS // LO
BF = jnp.bfloat16
F32 = jnp.float32
NT = (((1,), (1,)), ((), ()))
SCORE = float(HD**-0.5 * np.log2(np.e))


def shape(dims, dtype):
    return jax.ShapeDtypeStruct(dims, dtype)


def one_hot(row, first, count):
    numbers = lax.broadcasted_iota(jnp.int32, (count, row.shape[1]), 0)
    return jnp.where(numbers == row - first, 1.0, 0.0).astype(BF)


def spread(values, low):
    wide = values.astype(F32)
    return jnp.concatenate([jnp.where(low == l, wide, 0.0).astype(BF) for l in range(LO)], axis=0)


def gather_low(product, low, channels):
    total = jnp.where(low == 0, product[:channels], 0.0)
    for l in range(1, LO):
        total += jnp.where(low == l, product[l * channels : (l + 1) * channels], 0.0)
    return total


def slot_of(goal):
    me = lax.axis_index("wide")
    up = ((goal >> 2) - (me >> 2)) & 7
    across = ((goal & 3) - (me & 3)) & 3
    back = jnp.where((up == 0) | (up > 4), 1, 0)
    return jnp.where(up == 0, 0, jnp.abs(up - 4)) * 8 + across * 2 + back


def partner(t, sign):
    me = lax.axis_index("wide")
    group, across, back = t // 8, t % 8 // 2, t % 2
    up = (1 - back) * (4 - group) + back * ((group + 3) // 4 * 4 + group)
    return (me // 4 + sign * up + 8) % 8 * 4 + (me % 4 + sign * across + 4) % 4


def rank_points(rows, bits, goal_ref, row_ref, low_ref):
    k = 512
    before = lax.broadcasted_iota(jnp.int32, (k, k), 0) < lax.broadcasted_iota(jnp.int32, (k, k), 1)
    before = jnp.where(before, 1.0, 0.0).astype(BF)
    carry = jnp.zeros((GROUPS, 1), F32)
    for j in range(POINTS // k):
        at = slice(j * k % PATCH, j * k % PATCH + k)
        of = slice(j * k // PATCH, j * k // PATCH + 1)
        goal = slot_of(goal_ref[:, j * k : (j + 1) * k] >> bits)
        member = lax.broadcasted_iota(jnp.int32, (GROUPS, k), 0) == goal
        hot = jnp.where(member, 1.0, 0.0)
        running = jnp.dot(hot.astype(BF), before, preferred_element_type=F32) + carry
        carry = carry + jnp.sum(hot, axis=1, keepdims=True)
        rank = jnp.sum(hot * running, axis=0, keepdims=True).astype(jnp.int32)
        low = jnp.zeros_like(rank)
        for l in range(1, LO):
            low += jnp.where(rank >= l * rows, 1, 0)
        row_ref[of, at] = goal * rows + rank - low * rows
        low_ref[of, at] = low


def make_table(rows, bits, value_ref, row_ref, low_ref, table_ref):
    k = 512
    table = jnp.zeros((GROUPS * LO, 2 * TAB), F32)
    for j in range(POINTS // k):
        at = slice(j * k % PATCH, j * k % PATCH + k)
        of = slice(j * k // PATCH, j * k // PATCH + 1)
        values = value_ref[:, j * k : (j + 1) * k]
        goal = slot_of(values >> bits)
        value = (values & ((1 << bits) - 1)) + 1
        which = lax.broadcasted_iota(jnp.int32, (TAB, k), 0) == row_ref[of, at] - goal * rows
        parts = [
            jnp.where(which, part.astype(F32), 0.0) for part in (value >> 7, value & 127)
        ]
        marks = jnp.concatenate(parts, axis=0).astype(BF)
        table += lax.dot_general(
            one_hot(goal * LO + low_ref[of, at], 0, GROUPS * LO),
            marks,
            NT,
            preferred_element_type=F32,
        )
    table = (table[:, :TAB] * 128.0 + table[:, TAB:]).astype(jnp.int32) - 1
    table_ref[...] = table.reshape(GROUPS, LO, TAB)


def place(row_ref, spread_ref, first, count):
    total = jnp.zeros((count, spread_ref.shape[0]), F32)
    for j in range(BANDS):
        total += lax.dot_general(
            one_hot(row_ref[j : j + 1, :], first, count),
            spread_ref[:, j * PATCH : (j + 1) * PATCH],
            NT,
            preferred_element_type=F32,
        )
    return total


def statistics(wide):
    average = jnp.mean(wide, axis=0, keepdims=True)
    centred = wide - average
    spread_of = jnp.mean(centred * centred, axis=0, keepdims=True)
    return average, lax.rsqrt(spread_of + 1e-05)


def normalise(wide, average, scale, gain):
    return ((wide - average) * scale * gain).astype(BF)


def remote(src, dst, send_sem, recv_sem, wide, narrow):
    return pltpu.make_async_remote_copy(
        src_ref=src,
        dst_ref=dst,
        send_sem=send_sem,
        recv_sem=recv_sem,
        device_id={"wide": wide, "narrow": narrow},
        device_id_type=pl.DeviceIdType.MESH,
    )


class Wide:
    def __init__(self, src, dst, send_sem, recv_sem, sign):
        self.src, self.dst, self.send_sem, self.recv_sem, self.sign = src, dst, send_sem, recv_sem, sign

    def each(self, first, count, act):
        def one(i, _):
            t = first + i

            @pl.when(t != OWN)
            def _():
                act(
                    remote(
                        self.src.at[t],
                        self.dst.at[t],
                        self.send_sem.at[t],
                        self.recv_sem.at[t],
                        partner(t, self.sign),
                        lax.axis_index("narrow"),
                    )
                )

            return 0

        lax.fori_loop(0, count, one, 0)

    def start(self, group):
        self.each(group * 8, 8, lambda copy: copy.start())

        @pl.when(group == OWN // 8)
        def _():
            self.dst[OWN] = self.src[OWN]

    def wait(self, group):
        self.each(group * 8, 8, lambda copy: copy.wait_recv())

    def finish(self):
        self.each(0, GROUPS, lambda copy: copy.wait_send())


class Narrow:
    def __init__(self, src, dst, send_sem, recv_sem, whole=False):
        self.src, self.dst, self.send_sem, self.recv_sem = src, dst, send_sem, recv_sem
        self.whole = whole

    def copy(self, step):
        me = lax.axis_index("narrow")
        goal = (me + step) % BANDS
        return remote(
            self.src if self.whole else self.src.at[goal],
            self.dst.at[me],
            self.send_sem.at[step],
            self.recv_sem.at[step],
            lax.axis_index("wide"),
            goal,
        )

    def start(self):
        me = lax.axis_index("narrow")
        lax.fori_loop(1, BANDS, lambda s, _: self.copy(s).start() or 0, 0)
        self.dst[me] = self.src[...] if self.whole else self.src[me]

    def wait(self):
        me = lax.axis_index("narrow")

        def one(step, _):
            landed = self.dst.at[(me - step + BANDS) % BANDS]
            remote(
                landed,
                landed,
                self.send_sem.at[step],
                self.recv_sem.at[step],
                lax.axis_index("wide"),
                me,
            ).wait_recv()
            return 0

        lax.fori_loop(1, BANDS, one, 0)

    def finish(self):
        lax.fori_loop(1, BANDS, lambda s, _: self.copy(s).wait_send() or 0, 0)


def attend(q_ref, k_ref, v_ref, att_ref, key_ref, query_ref, value_ref, score_ref, top_ref, prob_ref):
    key_ref[...] = k_ref[...].T
    query_ref[...] = jnp.zeros_like(query_ref)
    value_ref[...] = jnp.ones_like(value_ref)
    parts = PATCH // COLS

    def head_rows(h):
        return pl.ds(pl.multiple_of(h * HD, HD), HD)

    def score(h, part, slot):
        if part == 0:
            query_ref[h % 2, head_rows((h + HEADS - 2) % HEADS), :] = jnp.zeros((HD, PATCH), BF)
            query_ref[h % 2, head_rows(h), :] = q_ref[head_rows(h), :]
        scores = jnp.dot(
            key_ref[...],
            query_ref[h % 2, :, part * COLS : (part + 1) * COLS],
            preferred_element_type=F32,
        )
        score_ref[slot] = scores
        top_ref[slot] = jnp.broadcast_to(jnp.max(scores, axis=0, keepdims=True), (8, COLS))

    score(0, 0, 0)

    def two_heads(pair, _):
        for unit in range(2 * parts):
            h, part, slot = pair * 2 + unit // parts, unit % parts, unit % 2
            after = unit + 1
            score(jnp.minimum(pair * 2 + after // parts, HEADS - 1), after % parts, after % 2)
            prob_ref[slot] = jnp.exp2((score_ref[slot] - top_ref[slot][:1]) * SCORE).astype(BF)
            value_ref[h % 2, :HD, :] = v_ref[head_rows(h), :]
            sums = jnp.dot(value_ref[h % 2], prob_ref[slot], preferred_element_type=F32)
            att_ref[head_rows(h), part * COLS : (part + 1) * COLS] = (sums[:HD] / sums[HD:]).astype(BF)
        return 0

    lax.fori_loop(0, HEADS // 2, two_heads, 0)


def lanes_of(table_ref, group, rows):
    return jnp.concatenate([table_ref[group * 8 + i, :, :rows] for i in range(8)], axis=1)


def kernel(
    feats_ref, hilbert_ref, cell_ref, own_ref, gain_ref, gain2_ref,
    block_ref, coarse_ref, unpooled_ref,
    row_ref, low_ref, p_row_ref, p_low_ref,
    land_out, land_in, cell_out, cell_in,
    spread_ref, first_out, first_in, acc_ref,
    patch_out, patch_in, weights_ref,
    x_ref, q_ref, k_ref, v_ref, att_ref, key_ref, query_ref, value_ref, score_ref, top_ref, prob_ref,
    block_out, block_in, stat_out, stat_in, second_out, second_in,
    sum_ref, count_ref, mean_out, mean_in, table_out, table_in,
    turned_ref, back_out, back_in,
    wide_send, wide_recv, narrow_send, narrow_recv,
):
    me = lax.axis_index("wide")
    mine = lax.axis_index("narrow")

    def wide(number, src, dst, sign=1):
        return Wide(src, dst, wide_send.at[number], wide_recv.at[number], sign)

    def narrow(number, src, dst, whole=False):
        return Narrow(src, dst, narrow_send.at[number], narrow_recv.at[number], whole)

    landings = wide(0, land_out, land_in)
    first = wide(1, first_out, first_in)
    cells = wide(2, cell_out, cell_in)
    second = wide(3, second_out, second_in)
    back = wide(4, back_out, back_in, -1)
    gather = narrow(0, own_ref, weights_ref, True)
    patches = narrow(1, patch_out, patch_in)
    blocks = narrow(2, block_out, block_in)
    stats = narrow(5, stat_out, stat_in, True)
    means = narrow(3, mean_out, mean_in)
    tables = narrow(4, table_out, table_in)

    barrier = pltpu.get_barrier_semaphore()

    def greet_wide(t, _):
        pl.semaphore_signal(
            barrier,
            inc=1,
            device_id={"wide": (me + t) % GROUPS, "narrow": mine},
            device_id_type=pl.DeviceIdType.MESH,
        )
        return 0

    def greet_narrow(t, _):
        pl.semaphore_signal(
            barrier,
            inc=1,
            device_id={"wide": me, "narrow": (mine + t) % BANDS},
            device_id_type=pl.DeviceIdType.MESH,
        )
        return 0

    lax.fori_loop(1, GROUPS, greet_wide, 0)
    lax.fori_loop(1, BANDS, greet_narrow, 0)

    rank_points(HROWS, 13, hilbert_ref, row_ref, low_ref)
    for j in range(BANDS):
        at = slice(j * PATCH, (j + 1) * PATCH)
        spread_ref[:, at] = spread(feats_ref[:, at], low_ref[j : j + 1, :])

    def first_block(g, _):
        chunk = place(row_ref, spread_ref, g * 512, 512).astype(BF)
        first_out[pl.ds(g * 8, 8)] = chunk.reshape(8, HROWS, LO * CH)

        @pl.when(g == 0)
        def _():
            pl.semaphore_wait(barrier, GROUPS + BANDS - 2)

        first.start(g)

        @pl.when(g == 0)
        def _():
            make_table(HROWS, 13, hilbert_ref, row_ref, low_ref, land_out)
            lax.fori_loop(0, 4, lambda i, _: landings.start(i) or 0, 0)

        return 0

    lax.fori_loop(0, 4, first_block, 0)
    gather.start()
    rank_points(PROWS, 11, cell_ref, p_row_ref, p_low_ref)
    make_table(PROWS, 11, cell_ref, p_row_ref, p_low_ref, cell_out)
    lax.fori_loop(0, 4, lambda i, _: cells.start(i) or 0, 0)

    def first_group(g, _):
        landings.wait(g)
        first.wait(g)
        k = 8 * HROWS
        turned = first_in[pl.ds(g * 8, 8)].reshape(k, LO * CH).T
        landing = lanes_of(land_in, g, HROWS)
        for l in range(LO):
            spread_ref[:, l * k : (l + 1) * k] = spread(
                turned[l * CH : (l + 1) * CH], (landing[l : l + 1] >> 7) & 7
            )
        rows = (landing >> 10) * 128 + (landing & 127)
        for m in range(2):
            total = jnp.zeros((512, LO * CH), F32)
            for l in range(LO):
                total += lax.dot_general(
                    one_hot(rows[l : l + 1], m * 512, 512),
                    spread_ref[:, l * k : (l + 1) * k],
                    NT,
                    preferred_element_type=F32,
                )
            at = slice(m * 512, (m + 1) * 512)
            acc_ref[at, :] = jnp.where(g == 0, total, total + acc_ref[at, :])
        return 0

    lax.fori_loop(0, 4, first_group, 0)
    patch_out[...] = acc_ref[...].astype(BF).reshape(BANDS, PATCH // LO, LO * CH)
    patches.start()
    gather.wait()
    patches.wait()

    for n in range(BANDS):
        turned = patch_in[n].T
        for l in range(LO):
            x_ref[n * CH : (n + 1) * CH, l * 128 : (l + 1) * 128] = turned[l * CH : (l + 1) * CH]
    gains = jnp.broadcast_to(gain_ref[...], (8, C)).T[:, :1]
    wide_x = x_ref[...].astype(F32)
    normed = normalise(wide_x, *statistics(wide_x), gains)

    def weight(start):
        return jnp.concatenate([weights_ref[n, start : start + CH, :] for n in range(BANDS)], axis=0)

    def project(t):
        return jnp.dot(weight(t * CH), normed, preferred_element_type=F32).astype(BF)

    q_ref[...] = project(0)
    k_ref[...] = project(1)
    v_ref[...] = project(2)
    attend(
        q_ref, k_ref, v_ref, att_ref, key_ref, query_ref, value_ref, score_ref, top_ref, prob_ref
    )
    added = jnp.dot(weight(3 * CH).T, att_ref[...], preferred_element_type=F32)
    block = (x_ref[...].astype(F32) + added).astype(BF)
    block_out[...] = block.reshape(BANDS, CH, PATCH)
    blocks.start()
    average, scale = statistics(block.astype(F32))
    stat_out[:1, :] = average
    stat_out[1:, :] = scale
    stats.start()
    stats.wait()
    blocks.wait()

    gains2 = jnp.broadcast_to(gain2_ref[...], (8, C)).T[:, :1].reshape(BANDS, CH, 1)
    gain2 = jnp.zeros((CH, 1), F32)
    for n in range(BANDS):
        gain2 = jnp.where(mine == n, gains2[n], gain2)
    for j in range(BANDS):
        at = slice(j * PATCH, (j + 1) * PATCH)
        pooled = normalise(
            block_in[j].astype(F32), stat_in[j, :1, :], stat_in[j, 1:, :], gain2
        )
        spread_ref[:, at] = spread(pooled, p_low_ref[j : j + 1, :])

    def second_block(g, _):
        chunk = place(p_row_ref, spread_ref, g * 384, 384).astype(BF)
        second_out[pl.ds(g * 8, 8)] = chunk.reshape(8, PROWS, LO * CH)
        second.start(g)
        return 0

    lax.fori_loop(0, 4, second_block, 0)
    for j in range(BANDS):
        block_ref[:, j * PATCH : (j + 1) * PATCH] = block_in[j]
    sum_ref[...] = jnp.zeros_like(sum_ref)
    count_ref[...] = jnp.zeros_like(count_ref)
    k = 8 * PROWS

    def count_group(g, _):
        cells.wait(g)
        cell = lanes_of(cell_in, g, PROWS)
        ones = jnp.ones((CH, k), F32)
        for l in range(LO):
            count_ref[...] += lax.dot_general(
                one_hot(cell[l : l + 1] & (CHI - 1), 0, CHI),
                spread(ones, cell[l : l + 1] >> 8),
                NT,
                preferred_element_type=F32,
            )
        return 0

    lax.fori_loop(0, 4, count_group, 0)

    def second_group(g, _):
        second.wait(g)
        turned = second_in[pl.ds(g * 8, 8)].reshape(k, LO * CH).T
        cell = lanes_of(cell_in, g, PROWS)
        for l in range(LO):
            sum_ref[...] += lax.dot_general(
                one_hot(cell[l : l + 1] & (CHI - 1), 0, CHI),
                spread(turned[l * CH : (l + 1) * CH], cell[l : l + 1] >> 8),
                NT,
                preferred_element_type=F32,
            )
        return 0

    lax.fori_loop(0, 4, second_group, 0)
    mean_out[...] = (sum_ref[...] / jnp.maximum(count_ref[...], 1.0)).T.reshape(BANDS, CH, CHI)
    means.start()
    means.wait()

    mean = mean_in[...].reshape(C, CHI)
    upper = mean.astype(BF)
    lower = (mean - upper.astype(F32)).astype(BF)
    for n in range(BANDS):
        weight_n = weights_ref[n, 4 * CH :, :]
        value = jnp.dot(weight_n, upper, preferred_element_type=F32) + jnp.dot(
            weight_n, lower, preferred_element_type=F32
        )
        table_out[n] = (value * (1.0 + lax.erf(value * (0.5**0.5))) * 0.5).astype(BF)
    tables.start()
    tables.wait()

    table = table_in[...].reshape(BANDS * CH2, CHI)

    def give_group(g, _):
        cell = lanes_of(cell_in, g, PROWS)
        for l in range(LO):
            product = jnp.dot(
                table, one_hot(cell[l : l + 1] & (CHI - 1), 0, CHI), preferred_element_type=F32
            )
            turned_ref[l * CH2 : (l + 1) * CH2, :] = gather_low(
                product, cell[l : l + 1] >> 8, CH2
            ).astype(BF)
        back_out[pl.ds(g * 8, 8)] = turned_ref[...].T.reshape(8, PROWS, LO * CH2)
        back.start(g)
        return 0

    lax.fori_loop(0, 4, give_group, 0)
    for n in range(BANDS):
        coarse_ref[:, n * CHI : (n + 1) * CHI] = table_in[n]
    unpooled_ref[...] = jnp.zeros_like(unpooled_ref)

    def take_group(g, _):
        back.wait(g)
        turned_ref[...] = back_in[pl.ds(g * 8, 8)].reshape(k, LO * CH2).T
        for j in range(BANDS):
            at = slice(j * PATCH, (j + 1) * PATCH)
            product = jnp.dot(
                turned_ref[...], one_hot(p_row_ref[j : j + 1, :], g * k, k), preferred_element_type=F32
            )
            part = gather_low(product, p_low_ref[j : j + 1, :], CH2)
            unpooled_ref[:, at] = (unpooled_ref[:, at].astype(F32) + part).astype(BF)
        return 0

    lax.fori_loop(0, 4, take_group, 0)
    for each in (landings, first, cells, second, back, gather, patches, blocks, stats, means, tables):
        each.finish()


def on_device(feats, hilbert_pos, ln_attn, w_qkv, w_proj, ln_pool, w_pool, cell_of):
    own = jnp.concatenate([w_qkv.transpose(0, 2, 1).reshape(-1, C), w_proj, w_pool.T], axis=0)
    small = lambda: pltpu.VMEM((BANDS, PATCH), jnp.int32)
    table = lambda: pltpu.VMEM((GROUPS, LO, TAB), jnp.int32)
    half = lambda *dims: pltpu.VMEM(dims, BF)
    full = lambda *dims: pltpu.VMEM(dims, F32)
    return tuple(
        pl.pallas_call(
            kernel,
            out_shape=[
                jax.ShapeDtypeStruct((CH, POINTS), BF),
                jax.ShapeDtypeStruct((CH2, CELLS), BF),
                jax.ShapeDtypeStruct((CH2, POINTS), BF),
            ],
            in_specs=[pl.BlockSpec(memory_space=pltpu.VMEM)] * 6,
            out_specs=[pl.BlockSpec(memory_space=pltpu.VMEM)] * 3,
            scratch_shapes=[
                small(), small(), small(), small(),
                table(), table(), table(), table(),
                half(LO * CH, POINTS),
                half(GROUPS, HROWS, LO * CH), half(GROUPS, HROWS, LO * CH),
                full(PATCH, LO * CH),
                half(BANDS, PATCH // LO, LO * CH), half(BANDS, PATCH // LO, LO * CH),
                half(BANDS, 6 * CH, C),
                half(C, PATCH), half(C, PATCH), half(C, PATCH), half(C, PATCH), half(C, PATCH),
                half(PATCH, C), half(2, C, PATCH), half(2, 2 * HD, PATCH),
                full(2, PATCH, COLS), full(2, 8, COLS), half(2, PATCH, COLS),
                half(BANDS, CH, PATCH), half(BANDS, CH, PATCH),
                full(2, PATCH), full(BANDS, 2, PATCH),
                half(GROUPS, PROWS, LO * CH), half(GROUPS, PROWS, LO * CH),
                full(CHI, LO * CH), full(CHI, LO * CH),
                full(BANDS, CH, CHI), full(BANDS, CH, CHI),
                half(BANDS, CH2, CHI), half(BANDS, CH2, CHI),
                half(LO * CH2, 8 * PROWS),
                half(GROUPS, PROWS, LO * CH2), half(GROUPS, PROWS, LO * CH2),
                pltpu.SemaphoreType.DMA((5, GROUPS)), pltpu.SemaphoreType.DMA((5, GROUPS)),
                pltpu.SemaphoreType.DMA((6, BANDS)), pltpu.SemaphoreType.DMA((6, BANDS)),
            ],
            compiler_params=pltpu.CompilerParams(
                collective_id=0, has_side_effects=True, vmem_limit_bytes=56 * 1024 * 1024
            ),
        )(
            feats,
            hilbert_pos.reshape(1, POINTS),
            cell_of.reshape(1, POINTS),
            own,
            ln_attn.reshape(1, C),
            ln_pool.reshape(1, C),
        )
    )


def solution(mesh):
    in_specs = (
        P("narrow", "wide"),
        P("wide"),
        P(),
        P(None, None, "narrow"),
        P("narrow", None),
        P(),
        P(None, "narrow"),
        P("wide"),
    )
    out_specs = (P("narrow", "wide"), P("narrow", "wide"), P("narrow", "wide"))
    return jax.shard_map(
        on_device, mesh=mesh, in_specs=in_specs, out_specs=out_specs, check_vma=False
    )
```

```python
import jax
import jax.numpy as jnp
import numpy as np
from jax import lax
from jax.experimental import pallas as pl
from jax.experimental.pallas import tpu as pltpu
from jax.sharding import PartitionSpec as P

HD = 16
HEADS = 16
C = 256
C2 = 512
PATCH = 1024
POINTS = 8192
GROUPS = 32
BANDS = 8
CH = C // BANDS
CH2 = C2 // BANDS
LO = 8
TAB = 128
OWN = 1
RELAYED = (2, 6)
ANY = pl.BlockSpec(memory_space=pl.ANY)
INSIDE = pl.BlockSpec(memory_space=pltpu.VMEM)
COLS = 512
HROWS = 64
PROWS = 48
CELLS = 2048
CHI = CELLS // LO
BF = jnp.bfloat16
F32 = jnp.float32
NT = (((1,), (1,)), ((), ()))
SCORE = float(HD**-0.5 * np.log2(np.e))


def shape(dims, dtype):
    return jax.ShapeDtypeStruct(dims, dtype)


def one_hot(row, first, count):
    numbers = lax.broadcasted_iota(jnp.int32, (count, row.shape[1]), 0)
    return jnp.where(numbers == row - first, 1.0, 0.0).astype(BF)


def spread(values, low):
    wide = values.astype(F32)
    return jnp.concatenate([jnp.where(low == l, wide, 0.0).astype(BF) for l in range(LO)], axis=0)


def gather_low(product, low, channels):
    total = jnp.where(low == 0, product[:channels], 0.0)
    for l in range(1, LO):
        total += jnp.where(low == l, product[l * channels : (l + 1) * channels], 0.0)
    return total


def slot_of(goal):
    me = lax.axis_index("wide")
    up = ((goal >> 2) - (me >> 2)) & 7
    across = ((goal & 3) - (me & 3)) & 3
    back = jnp.where((up == 0) | (up > 4), 1, 0)
    return jnp.where(up == 0, 0, jnp.abs(up - 4)) * 8 + across * 2 + back


def partner(t, sign):
    me = lax.axis_index("wide")
    group, across, back = t // 8, t % 8 // 2, t % 2
    up = (1 - back) * (4 - group) + back * ((group + 3) // 4 * 4 + group)
    return (me // 4 + sign * up + 8) % 8 * 4 + (me % 4 + sign * across + 4) % 4


def rank_points(rows, bits, goal_ref, row_ref, low_ref):
    k = 512
    before = lax.broadcasted_iota(jnp.int32, (k, k), 0) < lax.broadcasted_iota(jnp.int32, (k, k), 1)
    before = jnp.where(before, 1.0, 0.0).astype(BF)
    carry = jnp.zeros((GROUPS, 1), F32)
    for j in range(POINTS // k):
        at = slice(j * k % PATCH, j * k % PATCH + k)
        of = slice(j * k // PATCH, j * k // PATCH + 1)
        goal = slot_of(goal_ref[:, j * k : (j + 1) * k] >> bits)
        member = lax.broadcasted_iota(jnp.int32, (GROUPS, k), 0) == goal
        hot = jnp.where(member, 1.0, 0.0)
        running = jnp.dot(hot.astype(BF), before, preferred_element_type=F32) + carry
        carry = carry + jnp.sum(hot, axis=1, keepdims=True)
        rank = jnp.sum(hot * running, axis=0, keepdims=True).astype(jnp.int32)
        low = jnp.zeros_like(rank)
        for l in range(1, LO):
            low += jnp.where(rank >= l * rows, 1, 0)
        row_ref[of, at] = goal * rows + rank - low * rows
        low_ref[of, at] = low


def make_table(rows, bits, value_ref, row_ref, low_ref, table_ref):
    k = 512
    table = jnp.zeros((GROUPS * LO, 2 * TAB), F32)
    for j in range(POINTS // k):
        at = slice(j * k % PATCH, j * k % PATCH + k)
        of = slice(j * k // PATCH, j * k // PATCH + 1)
        values = value_ref[:, j * k : (j + 1) * k]
        goal = slot_of(values >> bits)
        value = (values & ((1 << bits) - 1)) + 1
        which = lax.broadcasted_iota(jnp.int32, (TAB, k), 0) == row_ref[of, at] - goal * rows
        parts = [
            jnp.where(which, part.astype(F32), 0.0) for part in (value >> 7, value & 127)
        ]
        marks = jnp.concatenate(parts, axis=0).astype(BF)
        table += lax.dot_general(
            one_hot(goal * LO + low_ref[of, at], 0, GROUPS * LO),
            marks,
            NT,
            preferred_element_type=F32,
        )
    table = (table[:, :TAB] * 128.0 + table[:, TAB:]).astype(jnp.int32) - 1
    table_ref[...] = table.reshape(GROUPS, LO, TAB)


def place(row_ref, spread_ref, first, count):
    total = jnp.zeros((count, spread_ref.shape[0]), F32)
    for j in range(BANDS):
        total += lax.dot_general(
            one_hot(row_ref[j : j + 1, :], first, count),
            spread_ref[:, j * PATCH : (j + 1) * PATCH],
            NT,
            preferred_element_type=F32,
        )
    return total


def statistics(wide):
    average = jnp.mean(wide, axis=0, keepdims=True)
    centred = wide - average
    spread_of = jnp.mean(centred * centred, axis=0, keepdims=True)
    return average, lax.rsqrt(spread_of + 1e-05)


def normalise(wide, average, scale, gain):
    return ((wide - average) * scale * gain).astype(BF)


def remote(src, dst, send_sem, recv_sem, wide, narrow):
    return pltpu.make_async_remote_copy(
        src_ref=src,
        dst_ref=dst,
        send_sem=send_sem,
        recv_sem=recv_sem,
        device_id={"wide": wide, "narrow": narrow},
        device_id_type=pl.DeviceIdType.MESH,
    )


class Wide:
    def __init__(self, src, dst, send_sem, recv_sem, sign, relay=None, relay_send=None, relay_recv=None):
        self.src, self.dst, self.send_sem, self.recv_sem, self.sign = src, dst, send_sem, recv_sem, sign
        self.relay, self.relay_send, self.relay_recv = relay, relay_send, relay_recv

    def copy(self, t):
        return remote(
            self.src.at[t],
            self.dst.at[t],
            self.send_sem.at[t],
            self.recv_sem.at[t],
            partner(t, self.sign),
            lax.axis_index("narrow"),
        )

    def hop(self, k):
        me = lax.axis_index("wide")
        return remote(
            self.src.at[RELAYED[k]],
            self.relay.at[k],
            self.send_sem.at[RELAYED[k]],
            self.relay_recv.at[k],
            (me // 4 + 7) % 8 * 4 + me % 4,
            lax.axis_index("narrow"),
        )

    def second_hop(self, k):
        me = lax.axis_index("wide")
        across = RELAYED[k] // 2
        return remote(
            self.relay.at[k],
            self.dst.at[RELAYED[k]],
            self.relay_send.at[k],
            self.recv_sem.at[RELAYED[k]],
            (me // 4 + 5) % 8 * 4 + (me % 4 + self.sign * across + 4) % 4,
            lax.axis_index("narrow"),
        )

    def each(self, first, count, act, skip=()):
        def one(i, _):
            t = first + i
            takes = t != OWN
            for other in skip:
                takes = takes & (t != other)

            @pl.when(takes)
            def _():
                act(self.copy(t))

            return 0

        lax.fori_loop(0, count, one, 0)

    def start(self, group):
        relayed = RELAYED if self.relay is not None else ()

        @pl.when(group == 0)
        def _():
            for k in range(len(relayed)):
                self.hop(k).start()
            self.dst[OWN] = self.src[OWN]

        self.each(group * 8, 8, lambda copy: copy.start(), relayed)

    def forward(self):
        for k in range(len(RELAYED)):
            self.hop(k).wait_recv()
            self.second_hop(k).start()

    def wait(self, group):
        self.each(group * 8, 8, lambda copy: copy.wait_recv())

    def finish(self):
        self.each(0, GROUPS, lambda copy: copy.wait_send())
        if self.relay is not None:
            for k in range(len(RELAYED)):
                self.second_hop(k).wait_send()


def arrival(i):
    return i // 3 * 3 + (1 - i // 3) * ((i + 1) % 3)


class Narrow:
    def __init__(self, src, dst, send_sem, recv_sem, whole=False):
        self.src, self.dst, self.send_sem, self.recv_sem = src, dst, send_sem, recv_sem
        self.whole = whole

    def copy(self, step):
        me = lax.axis_index("narrow")
        goal = (me + step) % BANDS
        return remote(
            self.src if self.whole else self.src.at[goal],
            self.dst.at[me],
            self.send_sem.at[step],
            self.recv_sem.at[step],
            lax.axis_index("wide"),
            goal,
        )

    def start(self):
        me = lax.axis_index("narrow")
        lax.fori_loop(1, BANDS, lambda s, _: self.copy(s).start() or 0, 0)
        self.dst[me] = self.src[...] if self.whole else self.src[me]

    def start_half(self, half):
        me = lax.axis_index("narrow")

        def one(i, _):
            step = (half * 4 + i - me + BANDS) % BANDS

            @pl.when(step != 0)
            def _():
                self.copy(step).start()

            return 0

        lax.fori_loop(0, 4, one, 0)

        @pl.when(me // 4 == half)
        def _():
            self.dst[me] = self.src[me]

    def wait(self):
        me = lax.axis_index("narrow")

        def one(step, _):
            landed = self.dst.at[(me - step + BANDS) % BANDS]
            remote(
                landed,
                landed,
                self.send_sem.at[step],
                self.recv_sem.at[step],
                lax.axis_index("wide"),
                me,
            ).wait_recv()
            return 0

        lax.fori_loop(1, BANDS, one, 0)

    def finish(self):
        lax.fori_loop(1, BANDS, lambda s, _: self.copy(s).wait_send() or 0, 0)


def attend(part, q_ref, k_ref, v_ref, att_ref, key_ref, query_ref, value_ref, score_ref, top_ref, prob_ref):
    columns = slice(part * COLS, (part + 1) * COLS)

    def head_rows(h):
        return pl.ds(pl.multiple_of(h * HD, HD), HD)

    def score(h, slot):
        query_ref[slot, head_rows((h + HEADS - 2) % HEADS), :] = jnp.zeros((HD, COLS), BF)
        query_ref[slot, head_rows(h), :] = q_ref[head_rows(h), columns]
        scores = jnp.dot(key_ref[...], query_ref[slot], preferred_element_type=F32)
        score_ref[slot] = scores
        top_ref[slot] = jnp.broadcast_to(jnp.max(scores, axis=0, keepdims=True), (8, COLS))

    query_ref[...] = jnp.zeros_like(query_ref)
    score(0, 0)

    def four_heads(quad, _):
        for unit in range(4):
            h, slot = quad * 4 + unit, unit % 2
            score(jnp.minimum(h + 1, HEADS - 1), 1 - slot)
            prob_ref[slot] = jnp.exp2((score_ref[slot] - top_ref[slot][:1]) * SCORE).astype(BF)
            value_ref[slot, :HD, :] = v_ref[head_rows(h), :]
            sums = jnp.dot(value_ref[slot], prob_ref[slot], preferred_element_type=F32)
            att_ref[head_rows(h), columns] = (sums[:HD] / sums[HD:]).astype(BF)
        return 0

    lax.fori_loop(0, HEADS // 4, four_heads, 0)


def lanes_of(table_ref, group, rows):
    return jnp.concatenate([table_ref[group * 8 + i, :, :rows] for i in range(8)], axis=1)


def kernel(
    feats_ref, hilbert_ref, cell_ref, qkv_ref, proj_ref, pool_ref, gain_ref, gain2_ref,
    block_goal, coarse_goal, unpooled_goal,
    block_ref, coarse_ref, unpooled_ref, own_ref,
    row_ref, low_ref, p_row_ref, p_low_ref,
    land_out, land_in, cell_out, cell_in,
    spread_ref, first_out, first_in, acc_ref,
    patch_out, patch_in, weights_ref,
    x_ref, q_ref, k_ref, v_ref, att_ref, key_ref, query_ref, value_ref, score_ref, top_ref, prob_ref,
    block_out, block_in, stat_out, stat_in, second_out, second_in,
    sum_ref, count_ref, mean_out, mean_in, table_out, table_in,
    turned_ref, back_out, back_in,
    first_relay, second_relay, back_relay, relay_send, relay_recv,
    wide_send, wide_recv, narrow_send, narrow_recv, goal_sem,
):
    me = lax.axis_index("wide")
    mine = lax.axis_index("narrow")

    def wide(number, src, dst, sign=1, relay=None):
        return Wide(
            src, dst, wide_send.at[number], wide_recv.at[number], sign,
            relay, relay_send.at[number], relay_recv.at[number],
        )

    def narrow(number, src, dst, whole=False):
        return Narrow(src, dst, narrow_send.at[number], narrow_recv.at[number], whole)

    landings = wide(0, land_out, land_in)
    first = wide(1, first_out, first_in, 1, first_relay)
    cells = wide(2, cell_out, cell_in)
    second = wide(3, second_out, second_in, 1, second_relay)
    back = wide(4, back_out, back_in, -1, back_relay)
    gather = narrow(0, own_ref, weights_ref, True)
    patches = narrow(1, patch_out, patch_in)
    blocks = [narrow(2 + i, block_out.at[i], block_in.at[i]) for i in range(2)]
    stats = [narrow(6 + i, stat_out.at[i], stat_in.at[i], True) for i in range(2)]
    means = narrow(4, mean_out, mean_in)
    tables = narrow(5, table_out, table_in)

    barrier = pltpu.get_barrier_semaphore()

    def greet_wide(t, _):
        pl.semaphore_signal(
            barrier,
            inc=1,
            device_id={"wide": (me + t) % GROUPS, "narrow": mine},
            device_id_type=pl.DeviceIdType.MESH,
        )
        return 0

    def greet_narrow(t, _):
        pl.semaphore_signal(
            barrier,
            inc=1,
            device_id={"wide": me, "narrow": (mine + t) % BANDS},
            device_id_type=pl.DeviceIdType.MESH,
        )
        return 0

    lax.fori_loop(1, GROUPS, greet_wide, 0)
    lax.fori_loop(1, BANDS, greet_narrow, 0)

    own_ref[: 3 * CH, :] = qkv_ref[...]
    own_ref[3 * CH : 4 * CH, :] = proj_ref[...]
    own_ref[4 * CH :, :] = pool_ref[...]

    rank_points(HROWS, 13, hilbert_ref, row_ref, low_ref)
    for j in range(BANDS):
        at = slice(j * PATCH, (j + 1) * PATCH)
        spread_ref[:, at] = spread(feats_ref[:, at], low_ref[j : j + 1, :])

    def first_block(g, _):
        chunk = place(row_ref, spread_ref, g * 512, 512).astype(BF)
        first_out[pl.ds(g * 8, 8)] = chunk.reshape(8, HROWS, LO * CH)

        @pl.when(g == 0)
        def _():
            pl.semaphore_wait(barrier, GROUPS + BANDS - 2)

        @pl.when(g == 2)
        def _():
            first.forward()

        first.start(g)

        @pl.when(g == 0)
        def _():
            make_table(HROWS, 13, hilbert_ref, row_ref, low_ref, land_out)
            lax.fori_loop(0, 4, lambda i, _: landings.start(i) or 0, 0)

        return 0

    lax.fori_loop(0, 4, first_block, 0)
    gather.start()
    rank_points(PROWS, 11, cell_ref, p_row_ref, p_low_ref)
    make_table(PROWS, 11, cell_ref, p_row_ref, p_low_ref, cell_out)
    lax.fori_loop(0, 4, lambda i, _: cells.start(i) or 0, 0)

    def first_group(i, _):
        g = arrival(i)
        landings.wait(g)
        first.wait(g)
        k = 8 * HROWS
        turned = first_in[pl.ds(g * 8, 8)].reshape(k, LO * CH).T
        landing = lanes_of(land_in, g, HROWS)
        for l in range(LO):
            spread_ref[:, l * k : (l + 1) * k] = spread(
                turned[l * CH : (l + 1) * CH], (landing[l : l + 1] >> 7) & 7
            )
        rows = (landing >> 10) * 128 + (landing & 127)
        for m in range(2):
            total = jnp.zeros((512, LO * CH), F32)
            for l in range(LO):
                total += lax.dot_general(
                    one_hot(rows[l : l + 1], m * 512, 512),
                    spread_ref[:, l * k : (l + 1) * k],
                    NT,
                    preferred_element_type=F32,
                )
            at = slice(m * 512, (m + 1) * 512)
            total = jnp.where(i == 0, total, total + acc_ref[at, :])
            acc_ref[at, :] = total

            @pl.when(i == 3)
            def _():
                patch_out[m * 4 : (m + 1) * 4] = total.astype(BF).reshape(4, PATCH // LO, LO * CH)
                patches.start_half(m)

        return 0

    lax.fori_loop(0, 4, first_group, 0)
    gather.wait()
    patches.wait()

    for n in range(BANDS):
        turned = patch_in[n].T
        for l in range(LO):
            x_ref[n * CH : (n + 1) * CH, l * 128 : (l + 1) * 128] = turned[l * CH : (l + 1) * CH]
    gains = jnp.broadcast_to(gain_ref[...], (8, C)).T[:, :1]
    wide_x = x_ref[...].astype(F32)
    normed = normalise(wide_x, *statistics(wide_x), gains)

    def weight(start):
        return jnp.concatenate([weights_ref[n, start : start + CH, :] for n in range(BANDS)], axis=0)

    def project(t):
        return jnp.dot(weight(t * CH), normed, preferred_element_type=F32).astype(BF)

    q_ref[...] = project(0)
    k_ref[...] = project(1)
    v_ref[...] = project(2)
    key_ref[...] = k_ref[...].T
    value_ref[...] = jnp.ones_like(value_ref)
    proj = weight(3 * CH).T
    for part in range(2):
        attend(
            part, q_ref, k_ref, v_ref, att_ref, key_ref, query_ref, value_ref, score_ref, top_ref, prob_ref
        )
        columns = slice(part * COLS, (part + 1) * COLS)
        added = jnp.dot(proj, att_ref[:, columns], preferred_element_type=F32)
        block = (x_ref[:, columns].astype(F32) + added).astype(BF)
        block_out[part] = block.reshape(BANDS, CH, COLS)
        blocks[part].start()
        average, scale = statistics(block.astype(F32))
        stat_out[part, :1, :] = average
        stat_out[part, 1:, :] = scale
        stats[part].start()

    gains2 = jnp.broadcast_to(gain2_ref[...], (8, C)).T[:, :1].reshape(BANDS, CH, 1)
    gain2 = jnp.zeros((CH, 1), F32)
    for n in range(BANDS):
        gain2 = jnp.where(mine == n, gains2[n], gain2)
    for part in range(2):
        stats[part].wait()
        blocks[part].wait()
        for j in range(BANDS):
            at = slice(j * PATCH + part * COLS, j * PATCH + (part + 1) * COLS)
            pooled = normalise(
                block_in[part, j].astype(F32), stat_in[part, j, :1, :], stat_in[part, j, 1:, :], gain2
            )
            spread_ref[:, at] = spread(pooled, p_low_ref[j : j + 1, part * COLS : (part + 1) * COLS])

    def second_block(g, _):
        chunk = place(p_row_ref, spread_ref, g * 384, 384).astype(BF)
        second_out[pl.ds(g * 8, 8)] = chunk.reshape(8, PROWS, LO * CH)

        @pl.when(g == 2)
        def _():
            second.forward()

        second.start(g)
        return 0

    lax.fori_loop(0, 4, second_block, 0)
    for j in range(BANDS):
        for part in range(2):
            at = slice(j * PATCH + part * COLS, j * PATCH + (part + 1) * COLS)
            block_ref[:, at] = block_in[part, j]
    block_leaves = pltpu.make_async_copy(block_ref, block_goal, goal_sem.at[0])
    block_leaves.start()
    sum_ref[...] = jnp.zeros_like(sum_ref)
    count_ref[...] = jnp.zeros_like(count_ref)
    k = 8 * PROWS

    def count_group(g, _):
        cells.wait(g)
        cell = lanes_of(cell_in, g, PROWS)
        ones = jnp.ones((CH, k), F32)
        for l in range(LO):
            count_ref[...] += lax.dot_general(
                one_hot(cell[l : l + 1] & (CHI - 1), 0, CHI),
                spread(ones, cell[l : l + 1] >> 8),
                NT,
                preferred_element_type=F32,
            )
        return 0

    lax.fori_loop(0, 4, count_group, 0)

    def second_group(i, _):
        g = arrival(i)
        second.wait(g)
        turned = second_in[pl.ds(g * 8, 8)].reshape(k, LO * CH).T
        cell = lanes_of(cell_in, g, PROWS)
        for l in range(LO):
            sum_ref[...] += lax.dot_general(
                one_hot(cell[l : l + 1] & (CHI - 1), 0, CHI),
                spread(turned[l * CH : (l + 1) * CH], cell[l : l + 1] >> 8),
                NT,
                preferred_element_type=F32,
            )
        return 0

    lax.fori_loop(0, 4, second_group, 0)
    mean_out[...] = (sum_ref[...] / jnp.maximum(count_ref[...], 1.0)).T.reshape(BANDS, CH, CHI)
    means.start()
    means.wait()

    mean = mean_in[...].reshape(C, CHI)
    upper = mean.astype(BF)
    lower = (mean - upper.astype(F32)).astype(BF)
    for n in range(BANDS):
        weight_n = weights_ref[n, 4 * CH :, :]
        value = jnp.dot(weight_n, upper, preferred_element_type=F32) + jnp.dot(
            weight_n, lower, preferred_element_type=F32
        )
        table_out[n] = (value * (1.0 + lax.erf(value * (0.5**0.5))) * 0.5).astype(BF)
    tables.start()
    tables.wait()

    table = table_in[...].reshape(BANDS * CH2, CHI)

    def give_group(g, _):
        cell = lanes_of(cell_in, g, PROWS)
        for l in range(LO):
            product = jnp.dot(
                table, one_hot(cell[l : l + 1] & (CHI - 1), 0, CHI), preferred_element_type=F32
            )
            turned_ref[l * CH2 : (l + 1) * CH2, :] = gather_low(
                product, cell[l : l + 1] >> 8, CH2
            ).astype(BF)
        back_out[pl.ds(g * 8, 8)] = turned_ref[...].T.reshape(8, PROWS, LO * CH2)

        @pl.when(g == 2)
        def _():
            back.forward()

        back.start(g)
        return 0

    lax.fori_loop(0, 4, give_group, 0)
    for n in range(BANDS):
        coarse_ref[:, n * CHI : (n + 1) * CHI] = table_in[n]
    coarse_leaves = pltpu.make_async_copy(coarse_ref, coarse_goal, goal_sem.at[1])
    coarse_leaves.start()
    unpooled_ref[...] = jnp.zeros_like(unpooled_ref)

    def take_group(i, _):
        g = arrival(i)
        back.wait(g)
        turned_ref[...] = back_in[pl.ds(g * 8, 8)].reshape(k, LO * CH2).T
        for j in range(BANDS):
            at = slice(j * PATCH, (j + 1) * PATCH)
            product = jnp.dot(
                turned_ref[...], one_hot(p_row_ref[j : j + 1, :], g * k, k), preferred_element_type=F32
            )
            part = gather_low(product, p_low_ref[j : j + 1, :], CH2)
            unpooled_ref[:, at] = (unpooled_ref[:, at].astype(F32) + part).astype(BF)
        return 0

    lax.fori_loop(0, 4, take_group, 0)
    unpooled_leaves = pltpu.make_async_copy(unpooled_ref, unpooled_goal, goal_sem.at[2])
    unpooled_leaves.start()
    for each in (landings, first, cells, second, back, gather, patches, *blocks, *stats, means, tables):
        each.finish()
    block_leaves.wait()
    coarse_leaves.wait()
    unpooled_leaves.wait()


def settle_kernel(a_ref, b_ref, c_ref, a_out, b_out, c_out, sem):
    copies = [
        pltpu.make_async_copy(a_ref, a_out, sem.at[0]),
        pltpu.make_async_copy(b_ref, b_out, sem.at[1]),
        pltpu.make_async_copy(c_ref, c_out, sem.at[2]),
    ]
    for copy in copies:
        copy.start()
    for copy in copies:
        copy.wait()


def on_device(feats, hilbert_pos, ln_attn, w_qkv, w_proj, ln_pool, w_pool, cell_of):
    small = lambda: pltpu.VMEM((BANDS, PATCH), jnp.int32)
    table = lambda: pltpu.VMEM((GROUPS, LO, TAB), jnp.int32)
    half = lambda *dims: pltpu.VMEM(dims, BF)
    full = lambda *dims: pltpu.VMEM(dims, F32)
    results = [
        jax.ShapeDtypeStruct((CH, POINTS), BF),
        jax.ShapeDtypeStruct((CH2, CELLS), BF),
        jax.ShapeDtypeStruct((CH2, POINTS), BF),
    ]
    settle = pl.pallas_call(
        settle_kernel,
        out_shape=results,
        in_specs=[ANY] * 3,
        out_specs=[ANY] * 3,
        scratch_shapes=[pltpu.SemaphoreType.DMA((3,))],
        compiler_params=pltpu.CompilerParams(vmem_limit_bytes=60 * 1024 * 1024),
    )
    return tuple(
        settle(*pl.pallas_call(
            kernel,
            out_shape=results,
            in_specs=[INSIDE] * 8,
            out_specs=[ANY] * 3,
            scratch_shapes=[
                half(CH, POINTS), half(CH2, CELLS), half(CH2, POINTS), half(6 * CH, C),
                small(), small(), small(), small(),
                table(), table(), table(), table(),
                half(LO * CH, POINTS),
                half(GROUPS, HROWS, LO * CH), half(GROUPS, HROWS, LO * CH),
                full(PATCH, LO * CH),
                half(BANDS, PATCH // LO, LO * CH), half(BANDS, PATCH // LO, LO * CH),
                half(BANDS, 6 * CH, C),
                half(C, PATCH), half(C, PATCH), half(C, PATCH), half(C, PATCH), half(C, PATCH),
                half(PATCH, C), half(2, C, COLS), half(2, 2 * HD, PATCH),
                full(2, PATCH, COLS), full(2, 8, COLS), half(2, PATCH, COLS),
                half(2, BANDS, CH, COLS), half(2, BANDS, CH, COLS),
                full(2, 2, COLS), full(2, BANDS, 2, COLS),
                half(GROUPS, PROWS, LO * CH), half(GROUPS, PROWS, LO * CH),
                full(CHI, LO * CH), full(CHI, LO * CH),
                full(BANDS, CH, CHI), full(BANDS, CH, CHI),
                half(BANDS, CH2, CHI), half(BANDS, CH2, CHI),
                half(LO * CH2, 8 * PROWS),
                half(GROUPS, PROWS, LO * CH2), half(GROUPS, PROWS, LO * CH2),
                half(2, HROWS, LO * CH), half(2, PROWS, LO * CH), half(2, PROWS, LO * CH2),
                pltpu.SemaphoreType.DMA((5, 2)), pltpu.SemaphoreType.DMA((5, 2)),
                pltpu.SemaphoreType.DMA((5, GROUPS)), pltpu.SemaphoreType.DMA((5, GROUPS)),
                pltpu.SemaphoreType.DMA((8, BANDS)), pltpu.SemaphoreType.DMA((8, BANDS)),
                pltpu.SemaphoreType.DMA((3,)),
            ],
            compiler_params=pltpu.CompilerParams(
                collective_id=0, has_side_effects=True, vmem_limit_bytes=56 * 1024 * 1024
            ),
        )(
            feats,
            hilbert_pos.reshape(1, POINTS),
            cell_of.reshape(1, POINTS),
            w_qkv.transpose(0, 2, 1).reshape(-1, C),
            w_proj,
            w_pool.T,
            ln_attn.reshape(1, C),
            ln_pool.reshape(1, C),
        ))
    )


def solution(mesh):
    in_specs = (
        P("narrow", "wide"),
        P("wide"),
        P(),
        P(None, None, "narrow"),
        P("narrow", None),
        P(),
        P(None, "narrow"),
        P("wide"),
    )
    out_specs = (P("narrow", "wide"), P("narrow", "wide"), P("narrow", "wide"))
    return jax.shard_map(
        on_device, mesh=mesh, in_specs=in_specs, out_specs=out_specs, check_vma=False
    )
```

```python
import jax
import jax.numpy as jnp
import numpy as np
from jax import lax
from jax.experimental import pallas as pl
from jax.experimental.pallas import tpu as pltpu
from jax.sharding import PartitionSpec as P

HD = 16
HEADS = 16
C = 256
C2 = 512
PATCH = 1024
POINTS = 8192
GROUPS = 32
BANDS = 8
CH = C // BANDS
CH2 = C2 // BANDS
LO = 8
TAB = 128
OWN = 1
INSIDE = pl.BlockSpec(memory_space=pltpu.VMEM)
COLS = 512
HROWS = 64
PROWS = 48
CELLS = 2048
CHI = CELLS // LO
BF = jnp.bfloat16
F32 = jnp.float32
NT = (((1,), (1,)), ((), ()))
SCORE = float(HD**-0.5 * np.log2(np.e))


def shape(dims, dtype):
    return jax.ShapeDtypeStruct(dims, dtype)


def one_hot(row, first, count):
    numbers = lax.broadcasted_iota(jnp.int32, (count, row.shape[1]), 0)
    return jnp.where(numbers == row - first, 1.0, 0.0).astype(BF)


def spread(values, low):
    wide = values.astype(F32)
    return jnp.concatenate([jnp.where(low == l, wide, 0.0).astype(BF) for l in range(LO)], axis=0)


def gather_low(product, low, channels):
    total = jnp.where(low == 0, product[:channels], 0.0)
    for l in range(1, LO):
        total += jnp.where(low == l, product[l * channels : (l + 1) * channels], 0.0)
    return total


def slot_of(goal):
    me = lax.axis_index("wide")
    up = ((goal >> 2) - (me >> 2)) & 7
    across = ((goal & 3) - (me & 3)) & 3
    back = jnp.where((up == 0) | (up > 4), 1, 0)
    return jnp.where(up == 0, 0, jnp.abs(up - 4)) * 8 + across * 2 + back


def partner(t, sign):
    me = lax.axis_index("wide")
    group, across, back = t // 8, t % 8 // 2, t % 2
    up = (1 - back) * (4 - group) + back * ((group + 3) // 4 * 4 + group)
    return (me // 4 + sign * up + 8) % 8 * 4 + (me % 4 + sign * across + 4) % 4


def rank_points(rows, bits, goal_ref, row_ref, low_ref):
    k = 512
    before = lax.broadcasted_iota(jnp.int32, (k, k), 0) < lax.broadcasted_iota(jnp.int32, (k, k), 1)
    before = jnp.where(before, 1.0, 0.0).astype(BF)
    carry = jnp.zeros((GROUPS, 1), F32)
    for j in range(POINTS // k):
        at = slice(j * k % PATCH, j * k % PATCH + k)
        of = slice(j * k // PATCH, j * k // PATCH + 1)
        goal = slot_of(goal_ref[:, j * k : (j + 1) * k] >> bits)
        member = lax.broadcasted_iota(jnp.int32, (GROUPS, k), 0) == goal
        hot = jnp.where(member, 1.0, 0.0)
        running = jnp.dot(hot.astype(BF), before, preferred_element_type=F32) + carry
        carry = carry + jnp.sum(hot, axis=1, keepdims=True)
        rank = jnp.sum(hot * running, axis=0, keepdims=True).astype(jnp.int32)
        low = jnp.zeros_like(rank)
        for l in range(1, LO):
            low += jnp.where(rank >= l * rows, 1, 0)
        row_ref[of, at] = goal * rows + rank - low * rows
        low_ref[of, at] = low


def make_table(rows, bits, value_ref, row_ref, low_ref, table_ref):
    k = 512
    table = jnp.zeros((GROUPS * LO, 2 * TAB), F32)
    for j in range(POINTS // k):
        at = slice(j * k % PATCH, j * k % PATCH + k)
        of = slice(j * k // PATCH, j * k // PATCH + 1)
        values = value_ref[:, j * k : (j + 1) * k]
        goal = slot_of(values >> bits)
        value = (values & ((1 << bits) - 1)) + 1
        which = lax.broadcasted_iota(jnp.int32, (TAB, k), 0) == row_ref[of, at] - goal * rows
        parts = [
            jnp.where(which, part.astype(F32), 0.0) for part in (value >> 7, value & 127)
        ]
        marks = jnp.concatenate(parts, axis=0).astype(BF)
        table += lax.dot_general(
            one_hot(goal * LO + low_ref[of, at], 0, GROUPS * LO),
            marks,
            NT,
            preferred_element_type=F32,
        )
    table = (table[:, :TAB] * 128.0 + table[:, TAB:]).astype(jnp.int32) - 1
    table_ref[...] = table.reshape(GROUPS, LO, TAB)


def place(row_ref, spread_ref, first, count):
    total = jnp.zeros((count, spread_ref.shape[0]), F32)
    for j in range(BANDS):
        total += lax.dot_general(
            one_hot(row_ref[j : j + 1, :], first, count),
            spread_ref[:, j * PATCH : (j + 1) * PATCH],
            NT,
            preferred_element_type=F32,
        )
    return total


def statistics(wide):
    average = jnp.mean(wide, axis=0, keepdims=True)
    centred = wide - average
    spread_of = jnp.mean(centred * centred, axis=0, keepdims=True)
    return average, lax.rsqrt(spread_of + 1e-05)


def normalise(wide, average, scale, gain):
    return ((wide - average) * scale * gain).astype(BF)


def remote(src, dst, send_sem, recv_sem, wide, narrow):
    return pltpu.make_async_remote_copy(
        src_ref=src,
        dst_ref=dst,
        send_sem=send_sem,
        recv_sem=recv_sem,
        device_id={"wide": wide, "narrow": narrow},
        device_id_type=pl.DeviceIdType.MESH,
    )


class Wide:
    def __init__(self, src, dst, send_sem, recv_sem, sign):
        self.src, self.dst, self.send_sem, self.recv_sem, self.sign = src, dst, send_sem, recv_sem, sign

    def each(self, first, count, act):
        def one(i, _):
            t = first + i

            @pl.when(t != OWN)
            def _():
                act(
                    remote(
                        self.src.at[t],
                        self.dst.at[t],
                        self.send_sem.at[t],
                        self.recv_sem.at[t],
                        partner(t, self.sign),
                        lax.axis_index("narrow"),
                    )
                )

            return 0

        lax.fori_loop(0, count, one, 0)

    def start(self, group):
        self.each(group * 8, 8, lambda copy: copy.start())

        @pl.when(group == OWN // 8)
        def _():
            self.dst[OWN] = self.src[OWN]

    def wait(self, group):
        self.each(group * 8, 8, lambda copy: copy.wait_recv())

    def finish(self):
        self.each(0, GROUPS, lambda copy: copy.wait_send())


class Narrow:
    def __init__(self, src, dst, send_sem, recv_sem, whole=False):
        self.src, self.dst, self.send_sem, self.recv_sem = src, dst, send_sem, recv_sem
        self.whole = whole

    def copy(self, step):
        me = lax.axis_index("narrow")
        goal = (me + step) % BANDS
        return remote(
            self.src if self.whole else self.src.at[goal],
            self.dst.at[me],
            self.send_sem.at[step],
            self.recv_sem.at[step],
            lax.axis_index("wide"),
            goal,
        )

    def start(self):
        me = lax.axis_index("narrow")
        lax.fori_loop(1, BANDS, lambda s, _: self.copy(s).start() or 0, 0)
        self.dst[me] = self.src[...] if self.whole else self.src[me]

    def start_half(self, half):
        me = lax.axis_index("narrow")

        def one(i, _):
            step = (half * 4 + i - me + BANDS) % BANDS

            @pl.when(step != 0)
            def _():
                self.copy(step).start()

            return 0

        lax.fori_loop(0, 4, one, 0)

        @pl.when(me // 4 == half)
        def _():
            self.dst[me] = self.src[me]

    def wait(self):
        me = lax.axis_index("narrow")

        def one(step, _):
            landed = self.dst.at[(me - step + BANDS) % BANDS]
            remote(
                landed,
                landed,
                self.send_sem.at[step],
                self.recv_sem.at[step],
                lax.axis_index("wide"),
                me,
            ).wait_recv()
            return 0

        lax.fori_loop(1, BANDS, one, 0)

    def finish(self):
        lax.fori_loop(1, BANDS, lambda s, _: self.copy(s).wait_send() or 0, 0)


def attend(q_ref, k_ref, v_ref, att_ref, key_ref, query_ref, value_ref, score_ref, top_ref, prob_ref):
    key_ref[...] = k_ref[...].T
    query_ref[...] = jnp.zeros_like(query_ref)
    value_ref[...] = jnp.ones_like(value_ref)
    parts = PATCH // COLS

    def head_rows(h):
        return pl.ds(pl.multiple_of(h * HD, HD), HD)

    def score(h, part, slot):
        if part == 0:
            query_ref[h % 2, head_rows((h + HEADS - 2) % HEADS), :] = jnp.zeros((HD, PATCH), BF)
            query_ref[h % 2, head_rows(h), :] = q_ref[head_rows(h), :]
        scores = jnp.dot(
            key_ref[...],
            query_ref[h % 2, :, part * COLS : (part + 1) * COLS],
            preferred_element_type=F32,
        )
        score_ref[slot] = scores
        top_ref[slot] = jnp.broadcast_to(jnp.max(scores, axis=0, keepdims=True), (8, COLS))

    score(0, 0, 0)

    def two_heads(pair, _):
        for unit in range(2 * parts):
            h, part, slot = pair * 2 + unit // parts, unit % parts, unit % 2
            after = unit + 1
            score(jnp.minimum(pair * 2 + after // parts, HEADS - 1), after % parts, after % 2)
            prob_ref[slot] = jnp.exp2((score_ref[slot] - top_ref[slot][:1]) * SCORE).astype(BF)
            value_ref[h % 2, :HD, :] = v_ref[head_rows(h), :]
            sums = jnp.dot(value_ref[h % 2], prob_ref[slot], preferred_element_type=F32)
            att_ref[head_rows(h), part * COLS : (part + 1) * COLS] = (sums[:HD] / sums[HD:]).astype(BF)
        return 0

    lax.fori_loop(0, HEADS // 2, two_heads, 0)


def gelu(value):
    return (value * (1.0 + lax.erf(value * (0.5**0.5))) * 0.5).astype(BF)


def lanes_of(table_ref, group, rows):
    return jnp.concatenate([table_ref[group * 8 + i, :, :rows] for i in range(8)], axis=1)


def kernel(
    feats_ref, hilbert_ref, cell_ref, qkv_ref, proj_ref, pool_ref, gain_ref, gain2_ref,
    block_in, table_in, result_in,
    own_ref,
    row_ref, low_ref, p_row_ref, p_low_ref,
    land_out, land_in, cell_out, cell_in,
    spread_ref, first_out, first_in, acc_ref,
    patch_out, patch_in, weights_ref,
    x_ref, q_ref, k_ref, v_ref, att_ref, key_ref, query_ref, value_ref, score_ref, top_ref, prob_ref,
    block_out, stat_out, stat_in, second_out, second_in,
    sum_ref, count_ref, mean_ref, mean_in, table_out,
    turned_ref, back_out, back_in, point_out, point_in, result_out,
    wide_send, wide_recv, narrow_send, narrow_recv,
):
    me = lax.axis_index("wide")
    mine = lax.axis_index("narrow")

    def wide(number, src, dst, sign=1):
        return Wide(src, dst, wide_send.at[number], wide_recv.at[number], sign)

    def narrow(number, src, dst, whole=False):
        return Narrow(src, dst, narrow_send.at[number], narrow_recv.at[number], whole)

    landings = wide(0, land_out, land_in)
    first = wide(1, first_out, first_in)
    cells = wide(2, cell_out, cell_in)
    second = wide(3, second_out, second_in)
    back = wide(4, back_out, back_in, -1)
    gather = narrow(0, own_ref, weights_ref, True)
    patches = narrow(1, patch_out, patch_in)
    blocks = narrow(2, block_out, block_in)
    stats = narrow(5, stat_out, stat_in, True)
    points = narrow(6, point_out, point_in)
    results = narrow(7, result_out, result_in)
    means = narrow(3, mean_ref, mean_in)
    tables = narrow(4, table_out, table_in)

    barrier = pltpu.get_barrier_semaphore()

    def greet_wide(t, _):
        pl.semaphore_signal(
            barrier,
            inc=1,
            device_id={"wide": (me + t) % GROUPS, "narrow": mine},
            device_id_type=pl.DeviceIdType.MESH,
        )
        return 0

    def greet_narrow(t, _):
        pl.semaphore_signal(
            barrier,
            inc=1,
            device_id={"wide": me, "narrow": (mine + t) % BANDS},
            device_id_type=pl.DeviceIdType.MESH,
        )
        return 0

    lax.fori_loop(1, GROUPS, greet_wide, 0)
    lax.fori_loop(1, BANDS, greet_narrow, 0)

    own_ref[: 3 * CH, :] = qkv_ref[...]
    own_ref[3 * CH : 4 * CH, :] = proj_ref[...]
    own_ref[4 * CH :, :] = pool_ref[...]

    rank_points(HROWS, 13, hilbert_ref, row_ref, low_ref)
    for j in range(BANDS):
        at = slice(j * PATCH, (j + 1) * PATCH)
        spread_ref[:, at] = spread(feats_ref[:, at], low_ref[j : j + 1, :])

    def first_block(g, _):
        chunk = place(row_ref, spread_ref, g * 512, 512).astype(BF)
        first_out[pl.ds(g * 8, 8)] = chunk.reshape(8, HROWS, LO * CH)

        @pl.when(g == 0)
        def _():
            pl.semaphore_wait(barrier, GROUPS + BANDS - 2)

        first.start(g)

        @pl.when(g == 0)
        def _():
            make_table(HROWS, 13, hilbert_ref, row_ref, low_ref, land_out)
            lax.fori_loop(0, 4, lambda i, _: landings.start(i) or 0, 0)

        return 0

    lax.fori_loop(0, 4, first_block, 0)
    gather.start()
    rank_points(PROWS, 11, cell_ref, p_row_ref, p_low_ref)
    make_table(PROWS, 11, cell_ref, p_row_ref, p_low_ref, cell_out)
    lax.fori_loop(0, 4, lambda i, _: cells.start(i) or 0, 0)

    def first_group(g, _):
        landings.wait(g)
        first.wait(g)
        k = 8 * HROWS
        turned = first_in[pl.ds(g * 8, 8)].reshape(k, LO * CH).T
        landing = lanes_of(land_in, g, HROWS)
        for l in range(LO):
            spread_ref[:, l * k : (l + 1) * k] = spread(
                turned[l * CH : (l + 1) * CH], (landing[l : l + 1] >> 7) & 7
            )
        rows = (landing >> 10) * 128 + (landing & 127)
        for m in range(2):
            total = jnp.zeros((512, LO * CH), F32)
            for l in range(LO):
                total += lax.dot_general(
                    one_hot(rows[l : l + 1], m * 512, 512),
                    spread_ref[:, l * k : (l + 1) * k],
                    NT,
                    preferred_element_type=F32,
                )
            at = slice(m * 512, (m + 1) * 512)
            total = jnp.where(g == 0, total, total + acc_ref[at, :])
            acc_ref[at, :] = total

            @pl.when(g == 3)
            def _():
                patch_out[m * 4 : (m + 1) * 4] = total.astype(BF).reshape(4, PATCH // LO, LO * CH)
                patches.start_half(m)

        return 0

    lax.fori_loop(0, 4, first_group, 0)
    gather.wait()
    patches.wait()

    for n in range(BANDS):
        turned = patch_in[n].T
        for l in range(LO):
            x_ref[n * CH : (n + 1) * CH, l * 128 : (l + 1) * 128] = turned[l * CH : (l + 1) * CH]
    gains = jnp.broadcast_to(gain_ref[...], (8, C)).T[:, :1]
    wide_x = x_ref[...].astype(F32)
    normed = normalise(wide_x, *statistics(wide_x), gains)

    def weight(start):
        return jnp.concatenate([weights_ref[n, start : start + CH, :] for n in range(BANDS)], axis=0)

    def project(t):
        return jnp.dot(weight(t * CH), normed, preferred_element_type=F32).astype(BF)

    q_ref[...] = project(0)
    k_ref[...] = project(1)
    v_ref[...] = project(2)
    attend(
        q_ref, k_ref, v_ref, att_ref, key_ref, query_ref, value_ref, score_ref, top_ref, prob_ref
    )
    added = jnp.dot(weight(3 * CH).T, att_ref[...], preferred_element_type=F32)
    block = (x_ref[...].astype(F32) + added).astype(BF)
    block_out[...] = block.reshape(BANDS, CH, PATCH)
    blocks.start()
    average, scale = statistics(block.astype(F32))
    stat_out[:1, :] = average
    stat_out[1:, :] = scale
    stats.start()
    stats.wait()
    blocks.wait()

    gains2 = jnp.broadcast_to(gain2_ref[...], (8, C)).T[:, :1].reshape(BANDS, CH, 1)
    gain2 = jnp.zeros((CH, 1), F32)
    for n in range(BANDS):
        gain2 = jnp.where(mine == n, gains2[n], gain2)
    for j in range(BANDS):
        at = slice(j * PATCH, (j + 1) * PATCH)
        pooled = normalise(
            block_in[j].astype(F32), stat_in[j, :1, :], stat_in[j, 1:, :], gain2
        )
        spread_ref[:, at] = spread(pooled, p_low_ref[j : j + 1, :])

    def second_block(g, _):
        chunk = place(p_row_ref, spread_ref, g * 384, 384).astype(BF)
        second_out[pl.ds(g * 8, 8)] = chunk.reshape(8, PROWS, LO * CH)
        second.start(g)
        return 0

    lax.fori_loop(0, 4, second_block, 0)
    sum_ref[...] = jnp.zeros_like(sum_ref)
    count_ref[...] = jnp.zeros_like(count_ref)
    k = 8 * PROWS

    def count_group(g, _):
        cells.wait(g)
        cell = lanes_of(cell_in, g, PROWS)
        ones = jnp.ones((CH, k), F32)
        for l in range(LO):
            count_ref[...] += lax.dot_general(
                one_hot(cell[l : l + 1] & (CHI - 1), 0, CHI),
                spread(ones, cell[l : l + 1] >> 8),
                NT,
                preferred_element_type=F32,
            )
        return 0

    lax.fori_loop(0, 4, count_group, 0)

    def second_group(g, _):
        second.wait(g)
        turned = second_in[pl.ds(g * 8, 8)].reshape(k, LO * CH).T
        cell = lanes_of(cell_in, g, PROWS)
        for l in range(LO):
            sum_ref[...] += lax.dot_general(
                one_hot(cell[l : l + 1] & (CHI - 1), 0, CHI),
                spread(turned[l * CH : (l + 1) * CH], cell[l : l + 1] >> 8),
                NT,
                preferred_element_type=F32,
            )
        return 0

    lax.fori_loop(0, 4, second_group, 0)
    mean = (sum_ref[...] / jnp.maximum(count_ref[...], 1.0)).T.astype(BF)
    mean_ref[...] = mean.reshape(BANDS, CH, CHI)

    def give_group(g, _):
        cell = lanes_of(cell_in, g, PROWS)
        means_of = mean_ref[...].reshape(C, CHI)
        for l in range(LO):
            product = jnp.dot(
                means_of, one_hot(cell[l : l + 1] & (CHI - 1), 0, CHI), preferred_element_type=F32
            )
            turned_ref[l * CH : (l + 1) * CH, :] = gather_low(
                product, cell[l : l + 1] >> 8, CH
            ).astype(BF)
        back_out[pl.ds(g * 8, 8)] = turned_ref[...].T.reshape(8, PROWS, LO * CH)
        back.start(g)
        return 0

    lax.fori_loop(0, 4, give_group, 0)
    means.start()
    means.wait()

    for n in range(BANDS):
        table_out[n] = gelu(
            jnp.dot(weights_ref[n, 4 * CH :, :], mean_in[...].reshape(C, CHI), preferred_element_type=F32)
        )
    tables.start()

    def take_group(g, _):
        back.wait(g)
        turned_ref[...] = back_in[pl.ds(g * 8, 8)].reshape(k, LO * CH).T
        for half_of in range(2):
            for j in range(half_of * 4, half_of * 4 + 4):
                product = jnp.dot(
                    turned_ref[...],
                    one_hot(p_row_ref[j : j + 1, :], g * k, k),
                    preferred_element_type=F32,
                )
                part = gather_low(product, p_low_ref[j : j + 1, :], CH)
                before = jnp.where(g == 0, 0.0, point_out[j].astype(F32))
                point_out[j] = (before + part).astype(BF)

            @pl.when(g == 3)
            def _():
                points.start_half(half_of)

        return 0

    point_out[...] = jnp.zeros_like(point_out)
    lax.fori_loop(0, 4, take_group, 0)
    points.wait()

    def project_for(step, _):
        n = (mine + step) % BANDS
        result_out[n] = gelu(
            jnp.dot(
                weights_ref[n, 4 * CH :, :],
                point_in[...].reshape(C, PATCH),
                preferred_element_type=F32,
            )
        )

        @pl.when(step != BANDS)
        def _():
            results.copy(step).start()

        return 0

    lax.fori_loop(1, BANDS + 1, project_for, 0)
    result_in[mine] = result_out[mine]
    results.wait()
    tables.wait()
    for each in (landings, first, cells, second, back):
        each.finish()
    for each in (gather, patches, blocks, stats, means, tables, points, results):
        each.finish()


def settle_kernel(block_in, table_in, result_in, block_ref, coarse_ref, unpooled_ref):
    for n in range(BANDS):
        block_ref[:, n * PATCH : (n + 1) * PATCH] = block_in[n]
        coarse_ref[:, n * CHI : (n + 1) * CHI] = table_in[n]
        unpooled_ref[:, n * PATCH : (n + 1) * PATCH] = result_in[n]


def on_device(feats, hilbert_pos, ln_attn, w_qkv, w_proj, ln_pool, w_pool, cell_of):
    small = lambda: pltpu.VMEM((BANDS, PATCH), jnp.int32)
    table = lambda: pltpu.VMEM((GROUPS, LO, TAB), jnp.int32)
    half = lambda *dims: pltpu.VMEM(dims, BF)
    full = lambda *dims: pltpu.VMEM(dims, F32)
    settle = pl.pallas_call(
        settle_kernel,
        out_shape=[
            jax.ShapeDtypeStruct((CH, POINTS), BF),
            jax.ShapeDtypeStruct((CH2, CELLS), BF),
            jax.ShapeDtypeStruct((CH2, POINTS), BF),
        ],
        in_specs=[INSIDE] * 3,
        out_specs=[INSIDE] * 3,
        compiler_params=pltpu.CompilerParams(vmem_limit_bytes=16 * 1024 * 1024),
    )
    return tuple(
        settle(*pl.pallas_call(
            kernel,
            out_shape=[
                jax.ShapeDtypeStruct((BANDS, CH, PATCH), BF),
                jax.ShapeDtypeStruct((BANDS, CH2, CHI), BF),
                jax.ShapeDtypeStruct((BANDS, CH2, PATCH), BF),
            ],
            in_specs=[INSIDE] * 8,
            out_specs=[INSIDE] * 3,
            scratch_shapes=[
                half(6 * CH, C),
                small(), small(), small(), small(),
                table(), table(), table(), table(),
                half(LO * CH, POINTS),
                half(GROUPS, HROWS, LO * CH), half(GROUPS, HROWS, LO * CH),
                full(PATCH, LO * CH),
                half(BANDS, PATCH // LO, LO * CH), half(BANDS, PATCH // LO, LO * CH),
                half(BANDS, 6 * CH, C),
                half(C, PATCH), half(C, PATCH), half(C, PATCH), half(C, PATCH), half(C, PATCH),
                half(PATCH, C), half(2, C, PATCH), half(2, 2 * HD, PATCH),
                full(2, PATCH, COLS), full(2, 8, COLS), half(2, PATCH, COLS),
                half(BANDS, CH, PATCH), full(2, PATCH), full(BANDS, 2, PATCH),
                half(GROUPS, PROWS, LO * CH), half(GROUPS, PROWS, LO * CH),
                full(CHI, LO * CH), full(CHI, LO * CH),
                half(BANDS, CH, CHI), half(BANDS, CH, CHI), half(BANDS, CH2, CHI),
                half(LO * CH, 8 * PROWS),
                half(GROUPS, PROWS, LO * CH), half(GROUPS, PROWS, LO * CH),
                half(BANDS, CH, PATCH), half(BANDS, CH, PATCH), half(BANDS, CH2, PATCH),
                pltpu.SemaphoreType.DMA((5, GROUPS)), pltpu.SemaphoreType.DMA((5, GROUPS)),
                pltpu.SemaphoreType.DMA((8, BANDS)), pltpu.SemaphoreType.DMA((8, BANDS)),
            ],
            compiler_params=pltpu.CompilerParams(
                collective_id=0, has_side_effects=True, vmem_limit_bytes=56 * 1024 * 1024
            ),
        )(
            feats,
            hilbert_pos.reshape(1, POINTS),
            cell_of.reshape(1, POINTS),
            w_qkv.transpose(0, 2, 1).reshape(-1, C),
            w_proj,
            w_pool.T,
            ln_attn.reshape(1, C),
            ln_pool.reshape(1, C),
        ))
    )


def solution(mesh):
    in_specs = (
        P("narrow", "wide"),
        P("wide"),
        P(),
        P(None, None, "narrow"),
        P("narrow", None),
        P(),
        P(None, "narrow"),
        P("wide"),
    )
    out_specs = (P("narrow", "wide"), P("narrow", "wide"), P("narrow", "wide"))
    return jax.shard_map(
        on_device, mesh=mesh, in_specs=in_specs, out_specs=out_specs, check_vma=False
    )
```

```python
import jax
import jax.numpy as jnp
import numpy as np
from jax import lax
from jax.experimental import pallas as pl
from jax.experimental.pallas import tpu as pltpu
from jax.sharding import PartitionSpec as P

HD = 16
HEADS = 16
C = 256
C2 = 512
PATCH = 1024
POINTS = 8192
GROUPS = 32
BANDS = 8
CH = C // BANDS
CH2 = C2 // BANDS
LO = 8
TAB = 128
OWN = 1
INSIDE = pl.BlockSpec(memory_space=pltpu.VMEM)
COLS = 512
HROWS = 64
PROWS = 48
CELLS = 2048
CHI = CELLS // LO
BF = jnp.bfloat16
F32 = jnp.float32
NT = (((1,), (1,)), ((), ()))
SCORE = float(HD**-0.5 * np.log2(np.e))


def shape(dims, dtype):
    return jax.ShapeDtypeStruct(dims, dtype)


def one_hot(row, first, count):
    numbers = lax.broadcasted_iota(jnp.int32, (count, row.shape[1]), 0)
    return jnp.where(numbers == row - first, 1.0, 0.0).astype(BF)


def spread(values, low):
    wide = values.astype(F32)
    return jnp.concatenate([jnp.where(low == l, wide, 0.0).astype(BF) for l in range(LO)], axis=0)


def gather_low(product, low, channels):
    total = jnp.where(low == 0, product[:channels], 0.0)
    for l in range(1, LO):
        total += jnp.where(low == l, product[l * channels : (l + 1) * channels], 0.0)
    return total


def slot_of(goal):
    me = lax.axis_index("wide")
    up = ((goal >> 2) - (me >> 2)) & 7
    across = ((goal & 3) - (me & 3)) & 3
    back = jnp.where((up == 0) | (up > 4), 1, 0)
    return jnp.where(up == 0, 0, jnp.abs(up - 4)) * 8 + across * 2 + back


def partner(t, sign):
    me = lax.axis_index("wide")
    group, across, back = t // 8, t % 8 // 2, t % 2
    up = (1 - back) * (4 - group) + back * ((group + 3) // 4 * 4 + group)
    return (me // 4 + sign * up + 8) % 8 * 4 + (me % 4 + sign * across + 4) % 4


def rank_points(rows, bits, goal_ref, row_ref, low_ref):
    k = 512
    before = lax.broadcasted_iota(jnp.int32, (k, k), 0) < lax.broadcasted_iota(jnp.int32, (k, k), 1)
    before = jnp.where(before, 1.0, 0.0).astype(BF)
    goals = [slot_of(goal_ref[:, j * k : (j + 1) * k] >> bits) for j in range(POINTS // k)]
    hot = jnp.concatenate([one_hot(goal, 0, GROUPS) for goal in goals], axis=0)
    running = jnp.dot(hot, before, preferred_element_type=F32)
    carry = jnp.zeros((GROUPS, 1), F32)
    for j, goal in enumerate(goals):
        at = slice(j * k % PATCH, j * k % PATCH + k)
        of = slice(j * k // PATCH, j * k // PATCH + 1)
        member = lax.broadcasted_iota(jnp.int32, (GROUPS, k), 0) == goal
        ranks = running[j * GROUPS : (j + 1) * GROUPS]
        rank = jnp.sum(jnp.where(member, ranks + carry, 0.0), axis=0, keepdims=True).astype(jnp.int32)
        carry = carry + ranks[:, k - 1 :] + jnp.where(member[:, k - 1 :], 1.0, 0.0)
        low = jnp.zeros_like(rank)
        for l in range(1, LO):
            low += jnp.where(rank >= l * rows, 1, 0)
        row_ref[of, at] = goal * rows + rank - low * rows
        low_ref[of, at] = low


def make_table(rows, bits, value_ref, row_ref, low_ref, table_ref):
    k = 512
    table = jnp.zeros((GROUPS * 4, 2 * TAB), F32)
    for j in range(POINTS // k):
        at = slice(j * k % PATCH, j * k % PATCH + k)
        of = slice(j * k // PATCH, j * k // PATCH + 1)
        values = value_ref[:, j * k : (j + 1) * k]
        goal, low = slot_of(values >> bits), low_ref[of, at]
        value = (values & ((1 << bits) - 1)) + 1
        lane = row_ref[of, at] - goal * rows + (low & 1) * (TAB // 2)
        which = lax.broadcasted_iota(jnp.int32, (TAB, k), 0) == lane
        parts = [
            jnp.where(which, part.astype(F32), 0.0) for part in (value >> 7, value & 127)
        ]
        marks = jnp.concatenate(parts, axis=0).astype(BF)
        table += lax.dot_general(
            one_hot(goal * 4 + (low >> 1), 0, GROUPS * 4), marks, NT, preferred_element_type=F32
        )
    table = (table[:, :TAB] * 128.0 + table[:, TAB:]).astype(jnp.int32) - 1
    for t in range(GROUPS):
        table_ref[t] = table[t * 4 : (t + 1) * 4]


def place(row_ref, spread_ref, first, count):
    total = jnp.zeros((count, spread_ref.shape[0]), F32)
    for j in range(BANDS):
        total += lax.dot_general(
            one_hot(row_ref[j : j + 1, :], first, count),
            spread_ref[:, j * PATCH : (j + 1) * PATCH],
            NT,
            preferred_element_type=F32,
        )
    return total


def statistics(wide):
    average = jnp.mean(wide, axis=0, keepdims=True)
    centred = wide - average
    spread_of = jnp.mean(centred * centred, axis=0, keepdims=True)
    return average, lax.rsqrt(spread_of + 1e-05)


def normalise(wide, average, scale, gain):
    return ((wide - average) * scale * gain).astype(BF)


def remote(src, dst, send_sem, recv_sem, wide, narrow):
    return pltpu.make_async_remote_copy(
        src_ref=src,
        dst_ref=dst,
        send_sem=send_sem,
        recv_sem=recv_sem,
        device_id={"wide": wide, "narrow": narrow},
        device_id_type=pl.DeviceIdType.MESH,
    )


class Wide:
    def __init__(self, src, dst, send_sem, recv_sem, sign):
        self.src, self.dst, self.send_sem, self.recv_sem, self.sign = src, dst, send_sem, recv_sem, sign

    def each(self, first, count, act):
        def one(i, _):
            t = first + i

            @pl.when(t != OWN)
            def _():
                act(
                    remote(
                        self.src.at[t],
                        self.dst.at[t],
                        self.send_sem.at[t],
                        self.recv_sem.at[t],
                        partner(t, self.sign),
                        lax.axis_index("narrow"),
                    )
                )

            return 0

        lax.fori_loop(0, count, one, 0)

    def start(self, group):
        self.each(group * 8, 8, lambda copy: copy.start())

        @pl.when(group == OWN // 8)
        def _():
            self.dst[OWN] = self.src[OWN]

    def wait(self, group):
        self.each(group * 8, 8, lambda copy: copy.wait_recv())

    def finish(self):
        self.each(0, GROUPS, lambda copy: copy.wait_send())


class Narrow:
    def __init__(self, src, dst, send_sem, recv_sem, whole=False):
        self.src, self.dst, self.send_sem, self.recv_sem = src, dst, send_sem, recv_sem
        self.whole = whole

    def copy(self, step):
        me = lax.axis_index("narrow")
        goal = (me + step) % BANDS
        return remote(
            self.src if self.whole else self.src.at[goal],
            self.dst.at[me],
            self.send_sem.at[step],
            self.recv_sem.at[step],
            lax.axis_index("wide"),
            goal,
        )

    def start(self):
        me = lax.axis_index("narrow")
        lax.fori_loop(1, BANDS, lambda s, _: self.copy(s).start() or 0, 0)
        self.dst[me] = self.src[...] if self.whole else self.src[me]

    def start_half(self, half):
        me = lax.axis_index("narrow")

        def one(i, _):
            step = (half * 4 + i - me + BANDS) % BANDS

            @pl.when(step != 0)
            def _():
                self.copy(step).start()

            return 0

        lax.fori_loop(0, 4, one, 0)

        @pl.when(me // 4 == half)
        def _():
            self.dst[me] = self.src[me]

    def wait(self):
        me = lax.axis_index("narrow")

        def one(step, _):
            landed = self.dst.at[(me - step + BANDS) % BANDS]
            remote(
                landed,
                landed,
                self.send_sem.at[step],
                self.recv_sem.at[step],
                lax.axis_index("wide"),
                me,
            ).wait_recv()
            return 0

        lax.fori_loop(1, BANDS, one, 0)

    def finish(self):
        lax.fori_loop(1, BANDS, lambda s, _: self.copy(s).wait_send() or 0, 0)


def attend(q_ref, k_ref, v_ref, att_ref, key_ref, query_ref, value_ref, score_ref, top_ref, prob_ref):
    key_ref[...] = k_ref[...].T
    query_ref[...] = jnp.zeros_like(query_ref)
    value_ref[...] = jnp.ones_like(value_ref)
    parts = PATCH // COLS

    def head_rows(h):
        return pl.ds(pl.multiple_of(h * HD, HD), HD)

    def score(h, part, slot):
        if part == 0:
            query_ref[h % 2, head_rows((h + HEADS - 2) % HEADS), :] = jnp.zeros((HD, PATCH), BF)
            query_ref[h % 2, head_rows(h), :] = q_ref[head_rows(h), :]
        scores = jnp.dot(
            key_ref[...],
            query_ref[h % 2, :, part * COLS : (part + 1) * COLS],
            preferred_element_type=F32,
        )
        score_ref[slot] = scores
        top_ref[slot] = jnp.broadcast_to(jnp.max(scores, axis=0, keepdims=True), (8, COLS))

    score(0, 0, 0)

    def two_heads(pair, _):
        for unit in range(2 * parts):
            h, part, slot = pair * 2 + unit // parts, unit % parts, unit % 2
            after = unit + 1
            score(jnp.minimum(pair * 2 + after // parts, HEADS - 1), after % parts, after % 2)
            prob_ref[slot] = jnp.exp2((score_ref[slot] - top_ref[slot][:1]) * SCORE).astype(BF)
            value_ref[h % 2, :HD, :] = v_ref[head_rows(h), :]
            sums = jnp.dot(value_ref[h % 2], prob_ref[slot], preferred_element_type=F32)
            att_ref[head_rows(h), part * COLS : (part + 1) * COLS] = (sums[:HD] / sums[HD:]).astype(BF)
        return 0

    lax.fori_loop(0, HEADS // 2, two_heads, 0)


def gelu(value):
    return (value * (1.0 + lax.erf(value * (0.5**0.5))) * 0.5).astype(BF)


def lanes_of(table_ref, group, rows):
    halves = [
        jnp.concatenate([table_ref[group * 8 + i][:, at : at + rows] for i in range(8)], axis=1)
        for at in (0, TAB // 2)
    ]
    return [halves[l % 2][l // 2 : l // 2 + 1] for l in range(LO)]


def kernel(
    feats_ref, hilbert_ref, cell_ref, qkv_ref, proj_ref, pool_ref, gain_ref, gain2_ref,
    block_in, table_in, result_in,
    own_ref,
    row_ref, low_ref, p_row_ref, p_low_ref,
    land_out, land_in, cell_out, cell_in,
    spread_ref, first_out, first_in, acc_ref,
    patch_out, patch_in, weights_ref,
    x_ref, q_ref, k_ref, v_ref, att_ref, key_ref, query_ref, value_ref, score_ref, top_ref, prob_ref,
    block_out, stat_out, stat_in, second_out, second_in,
    sum_ref, count_ref, mean_ref, mean_in, table_out,
    turned_ref, back_out, back_in, point_out, point_in, result_out,
    wide_send, wide_recv, narrow_send, narrow_recv,
):
    me = lax.axis_index("wide")
    mine = lax.axis_index("narrow")

    def wide(number, src, dst, sign=1):
        return Wide(src, dst, wide_send.at[number], wide_recv.at[number], sign)

    def narrow(number, src, dst, whole=False):
        return Narrow(src, dst, narrow_send.at[number], narrow_recv.at[number], whole)

    landings = wide(0, land_out, land_in)
    first = wide(1, first_out, first_in)
    cells = wide(2, cell_out, cell_in)
    second = wide(3, second_out, second_in)
    back = wide(4, back_out, back_in, -1)
    gather = narrow(0, own_ref, weights_ref, True)
    patches = narrow(1, patch_out, patch_in)
    blocks = narrow(2, block_out, block_in)
    stats = narrow(5, stat_out, stat_in, True)
    points = narrow(6, point_out, point_in)
    results = narrow(7, result_out, result_in)
    means = narrow(3, mean_ref, mean_in)
    tables = narrow(4, table_out, table_in)

    barrier = pltpu.get_barrier_semaphore()

    def greet_wide(t, _):
        pl.semaphore_signal(
            barrier,
            inc=1,
            device_id={"wide": (me + t) % GROUPS, "narrow": mine},
            device_id_type=pl.DeviceIdType.MESH,
        )
        return 0

    def greet_narrow(t, _):
        pl.semaphore_signal(
            barrier,
            inc=1,
            device_id={"wide": me, "narrow": (mine + t) % BANDS},
            device_id_type=pl.DeviceIdType.MESH,
        )
        return 0

    lax.fori_loop(1, GROUPS, greet_wide, 0)
    lax.fori_loop(1, BANDS, greet_narrow, 0)

    own_ref[: 3 * CH, :] = qkv_ref[...]
    own_ref[3 * CH : 4 * CH, :] = proj_ref[...]
    own_ref[4 * CH :, :] = pool_ref[...]

    rank_points(HROWS, 13, hilbert_ref, row_ref, low_ref)
    for j in range(BANDS):
        at = slice(j * PATCH, (j + 1) * PATCH)
        spread_ref[:, at] = spread(feats_ref[:, at], low_ref[j : j + 1, :])

    def first_block(g, _):
        chunk = place(row_ref, spread_ref, g * 512, 512).astype(BF)
        first_out[pl.ds(g * 8, 8)] = chunk.reshape(8, HROWS, LO * CH)

        @pl.when(g == 0)
        def _():
            pl.semaphore_wait(barrier, GROUPS + BANDS - 2)

        first.start(g)

        @pl.when(g == 0)
        def _():
            make_table(HROWS, 13, hilbert_ref, row_ref, low_ref, land_out)
            lax.fori_loop(0, 4, lambda i, _: landings.start(i) or 0, 0)

        return 0

    lax.fori_loop(0, 4, first_block, 0)
    gather.start()
    rank_points(PROWS, 11, cell_ref, p_row_ref, p_low_ref)
    make_table(PROWS, 11, cell_ref, p_row_ref, p_low_ref, cell_out)

    def first_group(g, _):
        landings.wait(g)
        first.wait(g)
        k = 8 * HROWS
        turned = first_in[pl.ds(g * 8, 8)].reshape(k, LO * CH).T
        landing = lanes_of(land_in, g, HROWS)
        for l in range(LO):
            spread_ref[:, l * k : (l + 1) * k] = spread(
                turned[l * CH : (l + 1) * CH], (landing[l] >> 7) & 7
            )
        rows = [(each >> 10) * 128 + (each & 127) for each in landing]
        for m in range(2):
            total = jnp.zeros((512, LO * CH), F32)
            for l in range(LO):
                total += lax.dot_general(
                    one_hot(rows[l], m * 512, 512),
                    spread_ref[:, l * k : (l + 1) * k],
                    NT,
                    preferred_element_type=F32,
                )
            at = slice(m * 512, (m + 1) * 512)
            total = jnp.where(g == 0, total, total + acc_ref[at, :])
            acc_ref[at, :] = total

            @pl.when(g == 3)
            def _():
                patch_out[m * 4 : (m + 1) * 4] = total.astype(BF).reshape(4, PATCH // LO, LO * CH)
                patches.start_half(m)

        return 0

    lax.fori_loop(0, 4, first_group, 0)
    lax.fori_loop(0, 4, lambda i, _: cells.start(i) or 0, 0)
    gather.wait()
    patches.wait()

    for n in range(BANDS):
        turned = patch_in[n].T
        for l in range(LO):
            x_ref[n * CH : (n + 1) * CH, l * 128 : (l + 1) * 128] = turned[l * CH : (l + 1) * CH]
    gains = jnp.broadcast_to(gain_ref[...], (8, C)).T[:, :1]
    wide_x = x_ref[...].astype(F32)
    normed = normalise(wide_x, *statistics(wide_x), gains)

    def weight(start):
        return jnp.concatenate([weights_ref[n, start : start + CH, :] for n in range(BANDS)], axis=0)

    def project(t):
        return jnp.dot(weight(t * CH), normed, preferred_element_type=F32).astype(BF)

    q_ref[...] = project(0)
    k_ref[...] = project(1)
    v_ref[...] = project(2)
    attend(
        q_ref, k_ref, v_ref, att_ref, key_ref, query_ref, value_ref, score_ref, top_ref, prob_ref
    )
    added = jnp.dot(weight(3 * CH).T, att_ref[...], preferred_element_type=F32)
    block = (x_ref[...].astype(F32) + added).astype(BF)
    block_out[...] = block.reshape(BANDS, CH, PATCH)
    blocks.start()
    average, scale = statistics(block.astype(F32))
    stat_out[:1, :] = average
    stat_out[1:, :] = scale
    stats.start()
    stats.wait()
    blocks.wait()

    gains2 = jnp.broadcast_to(gain2_ref[...], (8, C)).T[:, :1].reshape(BANDS, CH, 1)
    gain2 = jnp.zeros((CH, 1), F32)
    for n in range(BANDS):
        gain2 = jnp.where(mine == n, gains2[n], gain2)
    for j in range(BANDS):
        at = slice(j * PATCH, (j + 1) * PATCH)
        pooled = normalise(
            block_in[j].astype(F32), stat_in[j, :1, :], stat_in[j, 1:, :], gain2
        )
        spread_ref[:, at] = spread(pooled, p_low_ref[j : j + 1, :])

    def second_block(g, _):
        chunk = place(p_row_ref, spread_ref, g * 384, 384).astype(BF)
        second_out[pl.ds(g * 8, 8)] = chunk.reshape(8, PROWS, LO * CH)
        second.start(g)
        return 0

    lax.fori_loop(0, 4, second_block, 0)
    sum_ref[...] = jnp.zeros_like(sum_ref)
    count_ref[...] = jnp.zeros_like(count_ref)
    k = 8 * PROWS

    def count_group(g, _):
        cells.wait(g)
        cell = lanes_of(cell_in, g, PROWS)
        ones = jnp.ones((CH, k), F32)
        for l in range(LO):
            count_ref[...] += lax.dot_general(
                one_hot(cell[l] & (CHI - 1), 0, CHI),
                spread(ones, cell[l] >> 8),
                NT,
                preferred_element_type=F32,
            )
        return 0

    lax.fori_loop(0, 4, count_group, 0)

    def second_group(g, _):
        second.wait(g)
        turned = second_in[pl.ds(g * 8, 8)].reshape(k, LO * CH).T
        cell = lanes_of(cell_in, g, PROWS)
        for l in range(LO):
            sum_ref[...] += lax.dot_general(
                one_hot(cell[l] & (CHI - 1), 0, CHI),
                spread(turned[l * CH : (l + 1) * CH], cell[l] >> 8),
                NT,
                preferred_element_type=F32,
            )
        return 0

    lax.fori_loop(0, 4, second_group, 0)
    mean = (sum_ref[...] / jnp.maximum(count_ref[...], 1.0)).T.astype(BF)
    mean_ref[...] = mean.reshape(BANDS, CH, CHI)

    def give_group(g, _):
        cell = lanes_of(cell_in, g, PROWS)
        means_of = mean_ref[...].reshape(C, CHI)
        for l in range(LO):
            product = jnp.dot(
                means_of, one_hot(cell[l] & (CHI - 1), 0, CHI), preferred_element_type=F32
            )
            turned_ref[l * CH : (l + 1) * CH, :] = gather_low(
                product, cell[l] >> 8, CH
            ).astype(BF)
        back_out[pl.ds(g * 8, 8)] = turned_ref[...].T.reshape(8, PROWS, LO * CH)
        back.start(g)
        return 0

    lax.fori_loop(0, 4, give_group, 0)
    means.start()
    means.wait()

    for n in range(BANDS):
        table_out[n] = gelu(
            jnp.dot(weights_ref[n, 4 * CH :, :], mean_in[...].reshape(C, CHI), preferred_element_type=F32)
        )
    tables.start()

    def take_group(g, _):
        back.wait(g)
        turned_ref[...] = back_in[pl.ds(g * 8, 8)].reshape(k, LO * CH).T
        for half_of in range(2):
            for j in range(half_of * 4, half_of * 4 + 4):
                product = jnp.dot(
                    turned_ref[...],
                    one_hot(p_row_ref[j : j + 1, :], g * k, k),
                    preferred_element_type=F32,
                )
                part = gather_low(product, p_low_ref[j : j + 1, :], CH)
                before = jnp.where(g == 0, 0.0, point_out[j].astype(F32))
                point_out[j] = (before + part).astype(BF)

            @pl.when(g == 3)
            def _():
                points.start_half(half_of)

        return 0

    point_out[...] = jnp.zeros_like(point_out)
    lax.fori_loop(0, 4, take_group, 0)
    points.wait()

    def project_for(step, _):
        n = (mine + step) % BANDS
        result_out[n] = gelu(
            jnp.dot(
                weights_ref[n, 4 * CH :, :],
                point_in[...].reshape(C, PATCH),
                preferred_element_type=F32,
            )
        )

        @pl.when(step != BANDS)
        def _():
            results.copy(step).start()

        return 0

    lax.fori_loop(1, BANDS + 1, project_for, 0)
    result_in[mine] = result_out[mine]
    results.wait()
    tables.wait()
    for each in (landings, first, cells, second, back):
        each.finish()
    for each in (gather, patches, blocks, stats, means, tables, points, results):
        each.finish()


def settle_kernel(block_in, table_in, result_in, block_ref, coarse_ref, unpooled_ref):
    for n in range(BANDS):
        block_ref[:, n * PATCH : (n + 1) * PATCH] = block_in[n]
        coarse_ref[:, n * CHI : (n + 1) * CHI] = table_in[n]
        unpooled_ref[:, n * PATCH : (n + 1) * PATCH] = result_in[n]


def on_device(feats, hilbert_pos, ln_attn, w_qkv, w_proj, ln_pool, w_pool, cell_of):
    small = lambda: pltpu.VMEM((BANDS, PATCH), jnp.int32)
    table = lambda: pltpu.VMEM((GROUPS, 4, TAB), jnp.int32)
    half = lambda *dims: pltpu.VMEM(dims, BF)
    full = lambda *dims: pltpu.VMEM(dims, F32)
    settle = pl.pallas_call(
        settle_kernel,
        out_shape=[
            jax.ShapeDtypeStruct((CH, POINTS), BF),
            jax.ShapeDtypeStruct((CH2, CELLS), BF),
            jax.ShapeDtypeStruct((CH2, POINTS), BF),
        ],
        in_specs=[INSIDE] * 3,
        out_specs=[INSIDE] * 3,
        compiler_params=pltpu.CompilerParams(vmem_limit_bytes=60 * 1024 * 1024),
    )
    return tuple(
        settle(*pl.pallas_call(
            kernel,
            out_shape=[
                jax.ShapeDtypeStruct((BANDS, CH, PATCH), BF),
                jax.ShapeDtypeStruct((BANDS, CH2, CHI), BF),
                jax.ShapeDtypeStruct((BANDS, CH2, PATCH), BF),
            ],
            in_specs=[INSIDE] * 8,
            out_specs=[INSIDE] * 3,
            scratch_shapes=[
                half(6 * CH, C),
                small(), small(), small(), small(),
                table(), table(), table(), table(),
                half(LO * CH, POINTS),
                half(GROUPS, HROWS, LO * CH), half(GROUPS, HROWS, LO * CH),
                full(PATCH, LO * CH),
                half(BANDS, PATCH // LO, LO * CH), half(BANDS, PATCH // LO, LO * CH),
                half(BANDS, 6 * CH, C),
                half(C, PATCH), half(C, PATCH), half(C, PATCH), half(C, PATCH), half(C, PATCH),
                half(PATCH, C), half(2, C, PATCH), half(2, 2 * HD, PATCH),
                full(2, PATCH, COLS), full(2, 8, COLS), half(2, PATCH, COLS),
                half(BANDS, CH, PATCH), full(2, PATCH), full(BANDS, 2, PATCH),
                half(GROUPS, PROWS, LO * CH), half(GROUPS, PROWS, LO * CH),
                full(CHI, LO * CH), full(CHI, LO * CH),
                half(BANDS, CH, CHI), half(BANDS, CH, CHI), half(BANDS, CH2, CHI),
                half(LO * CH, 8 * PROWS),
                half(GROUPS, PROWS, LO * CH), half(GROUPS, PROWS, LO * CH),
                half(BANDS, CH, PATCH), half(BANDS, CH, PATCH), half(BANDS, CH2, PATCH),
                pltpu.SemaphoreType.DMA((5, GROUPS)), pltpu.SemaphoreType.DMA((5, GROUPS)),
                pltpu.SemaphoreType.DMA((8, BANDS)), pltpu.SemaphoreType.DMA((8, BANDS)),
            ],
            compiler_params=pltpu.CompilerParams(
                collective_id=0, has_side_effects=True, vmem_limit_bytes=56 * 1024 * 1024
            ),
        )(
            feats,
            hilbert_pos.reshape(1, POINTS),
            cell_of.reshape(1, POINTS),
            w_qkv.transpose(0, 2, 1).reshape(-1, C),
            w_proj,
            w_pool.T,
            ln_attn.reshape(1, C),
            ln_pool.reshape(1, C),
        ))
    )


def solution(mesh):
    in_specs = (
        P("narrow", "wide"),
        P("wide"),
        P(),
        P(None, None, "narrow"),
        P("narrow", None),
        P(),
        P(None, "narrow"),
        P("wide"),
    )
    out_specs = (P("narrow", "wide"), P("narrow", "wide"), P("narrow", "wide"))
    return jax.shard_map(
        on_device, mesh=mesh, in_specs=in_specs, out_specs=out_specs, check_vma=False
    )
```

```python
import jax
import jax.numpy as jnp
import numpy as np
from jax import lax
from jax.experimental import pallas as pl
from jax.experimental.pallas import tpu as pltpu
from jax.sharding import PartitionSpec as P

HD = 16
HEADS = 16
C = 256
C2 = 512
PATCH = 1024
POINTS = 8192
GROUPS = 32
BANDS = 8
CH = C // BANDS
CH2 = C2 // BANDS
LO = 8
TAB = 128
OWN = 1
SET = 4
SETS = GROUPS // SET
INSIDE = pl.BlockSpec(memory_space=pltpu.VMEM)
COLS = 512
HROWS = 64
PROWS = 48
CELLS = 2048
CHI = CELLS // LO
BF = jnp.bfloat16
F32 = jnp.float32
NT = (((1,), (1,)), ((), ()))
SCORE = float(HD**-0.5 * np.log2(np.e))


def shape(dims, dtype):
    return jax.ShapeDtypeStruct(dims, dtype)


def one_hot(row, first, count):
    numbers = lax.broadcasted_iota(jnp.int32, (count, row.shape[1]), 0)
    return jnp.where(numbers == row - first, 1.0, 0.0).astype(BF)


def spread(values, low):
    wide = values.astype(F32)
    return jnp.concatenate([jnp.where(low == l, wide, 0.0).astype(BF) for l in range(LO)], axis=0)


def gather_low(product, low, channels):
    total = jnp.where(low == 0, product[:channels], 0.0)
    for l in range(1, LO):
        total += jnp.where(low == l, product[l * channels : (l + 1) * channels], 0.0)
    return total


def slot_of(goal):
    me = lax.axis_index("wide")
    up = ((goal >> 2) - (me >> 2)) & 7
    across = ((goal & 3) - (me & 3)) & 3
    back = jnp.where((up == 0) | (up > 4), 1, 0)
    return jnp.where(up == 0, 0, jnp.abs(up - 4)) * 8 + across * 2 + back


def partner(t, sign):
    me = lax.axis_index("wide")
    group, across, back = t // 8, t % 8 // 2, t % 2
    up = (1 - back) * (4 - group) + back * ((group + 3) // 4 * 4 + group)
    return (me // 4 + sign * up + 8) % 8 * 4 + (me % 4 + sign * across + 4) % 4


def rank_points(rows, bits, goal_ref, row_ref, low_ref):
    k = 512
    before = lax.broadcasted_iota(jnp.int32, (k, k), 0) < lax.broadcasted_iota(jnp.int32, (k, k), 1)
    before = jnp.where(before, 1.0, 0.0).astype(BF)
    goals = [slot_of(goal_ref[:, j * k : (j + 1) * k] >> bits) for j in range(POINTS // k)]
    hot = jnp.concatenate([one_hot(goal, 0, GROUPS) for goal in goals], axis=0)
    running = jnp.dot(hot, before, preferred_element_type=F32)
    carry = jnp.zeros((GROUPS, 1), F32)
    for j, goal in enumerate(goals):
        at = slice(j * k % PATCH, j * k % PATCH + k)
        of = slice(j * k // PATCH, j * k // PATCH + 1)
        member = lax.broadcasted_iota(jnp.int32, (GROUPS, k), 0) == goal
        ranks = running[j * GROUPS : (j + 1) * GROUPS]
        rank = jnp.sum(jnp.where(member, ranks + carry, 0.0), axis=0, keepdims=True).astype(jnp.int32)
        carry = carry + ranks[:, k - 1 :] + jnp.where(member[:, k - 1 :], 1.0, 0.0)
        low = jnp.zeros_like(rank)
        for l in range(1, LO):
            low += jnp.where(rank >= l * rows, 1, 0)
        row_ref[of, at] = goal * rows + rank - low * rows
        low_ref[of, at] = low


def make_table(rows, bits, value_ref, row_ref, low_ref, table_ref):
    k = 512
    table = jnp.zeros((GROUPS * 4, 2 * TAB), F32)
    for j in range(POINTS // k):
        at = slice(j * k % PATCH, j * k % PATCH + k)
        of = slice(j * k // PATCH, j * k // PATCH + 1)
        values = value_ref[:, j * k : (j + 1) * k]
        goal, low = slot_of(values >> bits), low_ref[of, at]
        value = (values & ((1 << bits) - 1)) + 1
        lane = row_ref[of, at] - goal * rows + (low & 1) * (TAB // 2)
        which = lax.broadcasted_iota(jnp.int32, (TAB, k), 0) == lane
        parts = [
            jnp.where(which, part.astype(F32), 0.0) for part in (value >> 7, value & 127)
        ]
        marks = jnp.concatenate(parts, axis=0).astype(BF)
        table += lax.dot_general(
            one_hot(goal * 4 + (low >> 1), 0, GROUPS * 4), marks, NT, preferred_element_type=F32
        )
    table = (table[:, :TAB] * 128.0 + table[:, TAB:]).astype(jnp.int32) - 1
    for t in range(GROUPS):
        table_ref[t] = table[t * 4 : (t + 1) * 4]


def place(row_ref, spread_ref, first, count):
    total = jnp.zeros((count, spread_ref.shape[0]), F32)
    for j in range(BANDS):
        total += lax.dot_general(
            one_hot(row_ref[j : j + 1, :], first, count),
            spread_ref[:, j * PATCH : (j + 1) * PATCH],
            NT,
            preferred_element_type=F32,
        )
    return total


def statistics(wide):
    average = jnp.mean(wide, axis=0, keepdims=True)
    centred = wide - average
    spread_of = jnp.mean(centred * centred, axis=0, keepdims=True)
    return average, lax.rsqrt(spread_of + 1e-05)


def normalise(wide, average, scale, gain):
    return ((wide - average) * scale * gain).astype(BF)


def remote(src, dst, send_sem, recv_sem, wide, narrow):
    return pltpu.make_async_remote_copy(
        src_ref=src,
        dst_ref=dst,
        send_sem=send_sem,
        recv_sem=recv_sem,
        device_id={"wide": wide, "narrow": narrow},
        device_id_type=pl.DeviceIdType.MESH,
    )


class Wide:
    def __init__(self, src, dst, send_sem, recv_sem, sign):
        self.src, self.dst, self.send_sem, self.recv_sem, self.sign = src, dst, send_sem, recv_sem, sign

    def each(self, first, count, act):
        def one(i, _):
            t = first + i

            @pl.when(t != OWN)
            def _():
                act(
                    remote(
                        self.src.at[t],
                        self.dst.at[t],
                        self.send_sem.at[t],
                        self.recv_sem.at[t],
                        partner(t, self.sign),
                        lax.axis_index("narrow"),
                    )
                )

            return 0

        lax.fori_loop(0, count, one, 0)

    def start(self, group):
        self.each(group * SET, SET, lambda copy: copy.start())

        @pl.when(group == OWN // SET)
        def _():
            self.dst[OWN] = self.src[OWN]

    def wait(self, group):
        self.each(group * SET, SET, lambda copy: copy.wait_recv())

    def finish(self):
        self.each(0, GROUPS, lambda copy: copy.wait_send())


class Narrow:
    def __init__(self, src, dst, send_sem, recv_sem, whole=False):
        self.src, self.dst, self.send_sem, self.recv_sem = src, dst, send_sem, recv_sem
        self.whole = whole

    def copy(self, step):
        me = lax.axis_index("narrow")
        goal = (me + step) % BANDS
        return remote(
            self.src if self.whole else self.src.at[goal],
            self.dst.at[me],
            self.send_sem.at[step],
            self.recv_sem.at[step],
            lax.axis_index("wide"),
            goal,
        )

    def start(self):
        me = lax.axis_index("narrow")
        lax.fori_loop(1, BANDS, lambda s, _: self.copy(s).start() or 0, 0)
        self.dst[me] = self.src[...] if self.whole else self.src[me]

    def start_half(self, half):
        me = lax.axis_index("narrow")

        def one(i, _):
            step = (half * 4 + i - me + BANDS) % BANDS

            @pl.when(step != 0)
            def _():
                self.copy(step).start()

            return 0

        lax.fori_loop(0, 4, one, 0)

        @pl.when(me // 4 == half)
        def _():
            self.dst[me] = self.src[me]

    def wait(self):
        me = lax.axis_index("narrow")

        def one(step, _):
            landed = self.dst.at[(me - step + BANDS) % BANDS]
            remote(
                landed,
                landed,
                self.send_sem.at[step],
                self.recv_sem.at[step],
                lax.axis_index("wide"),
                me,
            ).wait_recv()
            return 0

        lax.fori_loop(1, BANDS, one, 0)

    def finish(self):
        lax.fori_loop(1, BANDS, lambda s, _: self.copy(s).wait_send() or 0, 0)


def attend(q_ref, k_ref, v_ref, att_ref, key_ref, query_ref, value_ref, score_ref, top_ref, prob_ref):
    key_ref[...] = k_ref[...].T
    query_ref[...] = jnp.zeros_like(query_ref)
    value_ref[...] = jnp.ones_like(value_ref)
    parts = PATCH // COLS

    def head_rows(h):
        return pl.ds(pl.multiple_of(h * HD, HD), HD)

    def score(h, part, slot):
        if part == 0:
            query_ref[h % 2, head_rows((h + HEADS - 2) % HEADS), :] = jnp.zeros((HD, PATCH), BF)
            query_ref[h % 2, head_rows(h), :] = q_ref[head_rows(h), :]
        scores = jnp.dot(
            key_ref[...],
            query_ref[h % 2, :, part * COLS : (part + 1) * COLS],
            preferred_element_type=F32,
        )
        score_ref[slot] = scores
        top_ref[slot] = jnp.broadcast_to(jnp.max(scores, axis=0, keepdims=True), (8, COLS))

    score(0, 0, 0)

    def two_heads(pair, _):
        for unit in range(2 * parts):
            h, part, slot = pair * 2 + unit // parts, unit % parts, unit % 2
            after = unit + 1
            score(jnp.minimum(pair * 2 + after // parts, HEADS - 1), after % parts, after % 2)
            prob_ref[slot] = jnp.exp2((score_ref[slot] - top_ref[slot][:1]) * SCORE).astype(BF)
            value_ref[h % 2, :HD, :] = v_ref[head_rows(h), :]
            sums = jnp.dot(value_ref[h % 2], prob_ref[slot], preferred_element_type=F32)
            att_ref[head_rows(h), part * COLS : (part + 1) * COLS] = (sums[:HD] / sums[HD:]).astype(BF)
        return 0

    lax.fori_loop(0, HEADS // 2, two_heads, 0)


def gelu(value):
    return (value * (1.0 + lax.erf(value * (0.5**0.5))) * 0.5).astype(BF)


def lanes_of(table_ref, group, rows):
    halves = [
        jnp.concatenate([table_ref[group * SET + i][:, at : at + rows] for i in range(SET)], axis=1)
        for at in (0, TAB // 2)
    ]
    return [halves[l % 2][l // 2 : l // 2 + 1] for l in range(LO)]


def kernel(
    feats_ref, hilbert_ref, cell_ref, qkv_ref, proj_ref, pool_ref, gain_ref, gain2_ref,
    block_in, table_in, result_in,
    own_ref,
    row_ref, low_ref, p_row_ref, p_low_ref,
    land_out, land_in, cell_out, cell_in,
    spread_ref, first_out, first_in, acc_ref,
    patch_out, patch_in, weights_ref,
    x_ref, q_ref, k_ref, v_ref, att_ref, key_ref, query_ref, value_ref, score_ref, top_ref, prob_ref,
    block_out, stat_out, stat_in, second_out, second_in,
    sum_ref, count_ref, mean_ref, mean_in, table_out,
    turned_ref, back_out, back_in, point_out, point_in, result_out,
    wide_send, wide_recv, narrow_send, narrow_recv,
):
    me = lax.axis_index("wide")
    mine = lax.axis_index("narrow")

    def wide(number, src, dst, sign=1):
        return Wide(src, dst, wide_send.at[number], wide_recv.at[number], sign)

    def narrow(number, src, dst, whole=False):
        return Narrow(src, dst, narrow_send.at[number], narrow_recv.at[number], whole)

    landings = wide(0, land_out, land_in)
    first = wide(1, first_out, first_in)
    cells = wide(2, cell_out, cell_in)
    second = wide(3, second_out, second_in)
    back = wide(4, back_out, back_in, -1)
    gather = narrow(0, own_ref, weights_ref, True)
    patches = narrow(1, patch_out, patch_in)
    blocks = narrow(2, block_out, block_in)
    stats = narrow(5, stat_out, stat_in, True)
    points = [narrow(6 + i, point_out.at[i], point_in.at[i]) for i in range(2)]
    results = [narrow(8 + i, result_out.at[i], result_in.at[i]) for i in range(2)]
    means = narrow(3, mean_ref, mean_in)
    tables = narrow(4, table_out, table_in)

    barrier = pltpu.get_barrier_semaphore()

    def greet_wide(t, _):
        pl.semaphore_signal(
            barrier,
            inc=1,
            device_id={"wide": (me + t) % GROUPS, "narrow": mine},
            device_id_type=pl.DeviceIdType.MESH,
        )
        return 0

    def greet_narrow(t, _):
        pl.semaphore_signal(
            barrier,
            inc=1,
            device_id={"wide": me, "narrow": (mine + t) % BANDS},
            device_id_type=pl.DeviceIdType.MESH,
        )
        return 0

    lax.fori_loop(1, GROUPS, greet_wide, 0)
    lax.fori_loop(1, BANDS, greet_narrow, 0)

    own_ref[: 3 * CH, :] = qkv_ref[...]
    own_ref[3 * CH : 4 * CH, :] = proj_ref[...]
    own_ref[4 * CH :, :] = pool_ref[...]

    rank_points(HROWS, 13, hilbert_ref, row_ref, low_ref)
    for j in range(BANDS):
        at = slice(j * PATCH, (j + 1) * PATCH)
        spread_ref[:, at] = spread(feats_ref[:, at], low_ref[j : j + 1, :])

    def first_block(g, _):
        count = SET * HROWS
        chunk = place(row_ref, spread_ref, g * count, count).astype(BF)
        first_out[pl.ds(g * SET, SET)] = chunk.reshape(SET, HROWS, LO * CH)

        @pl.when(g == 0)
        def _():
            pl.semaphore_wait(barrier, GROUPS + BANDS - 2)

        first.start(g)

        @pl.when(g == 1)
        def _():
            make_table(HROWS, 13, hilbert_ref, row_ref, low_ref, land_out)
            lax.fori_loop(0, SETS, lambda i, _: landings.start(i) or 0, 0)

        return 0

    lax.fori_loop(0, SETS, first_block, 0)
    gather.start()
    rank_points(PROWS, 11, cell_ref, p_row_ref, p_low_ref)
    make_table(PROWS, 11, cell_ref, p_row_ref, p_low_ref, cell_out)

    def first_group(g, _):
        landings.wait(g)
        first.wait(g)
        k = SET * HROWS
        turned = first_in[pl.ds(g * SET, SET)].reshape(k, LO * CH).T
        landing = lanes_of(land_in, g, HROWS)
        for l in range(LO):
            spread_ref[:, l * k : (l + 1) * k] = spread(
                turned[l * CH : (l + 1) * CH], (landing[l] >> 7) & 7
            )
        rows = [(each >> 10) * 128 + (each & 127) for each in landing]
        for m in range(2):
            total = jnp.zeros((512, LO * CH), F32)
            for l in range(LO):
                total += lax.dot_general(
                    one_hot(rows[l], m * 512, 512),
                    spread_ref[:, l * k : (l + 1) * k],
                    NT,
                    preferred_element_type=F32,
                )
            at = slice(m * 512, (m + 1) * 512)
            total = jnp.where(g == 0, total, total + acc_ref[at, :])
            acc_ref[at, :] = total

            @pl.when(g == SETS - 1)
            def _():
                patch_out[m * 4 : (m + 1) * 4] = total.astype(BF).reshape(4, PATCH // LO, LO * CH)
                patches.start_half(m)

        return 0

    lax.fori_loop(0, SETS, first_group, 0)
    lax.fori_loop(0, SETS, lambda i, _: cells.start(i) or 0, 0)
    gather.wait()
    patches.wait()

    for n in range(BANDS):
        turned = patch_in[n].T
        for l in range(LO):
            x_ref[n * CH : (n + 1) * CH, l * 128 : (l + 1) * 128] = turned[l * CH : (l + 1) * CH]
    gains = jnp.broadcast_to(gain_ref[...], (8, C)).T[:, :1]
    wide_x = x_ref[...].astype(F32)
    normed = normalise(wide_x, *statistics(wide_x), gains)

    def weight(start):
        return jnp.concatenate([weights_ref[n, start : start + CH, :] for n in range(BANDS)], axis=0)

    def project(t):
        return jnp.dot(weight(t * CH), normed, preferred_element_type=F32).astype(BF)

    q_ref[...] = project(0)
    k_ref[...] = project(1)
    v_ref[...] = project(2)
    attend(
        q_ref, k_ref, v_ref, att_ref, key_ref, query_ref, value_ref, score_ref, top_ref, prob_ref
    )
    added = jnp.dot(weight(3 * CH).T, att_ref[...], preferred_element_type=F32)
    block = (x_ref[...].astype(F32) + added).astype(BF)
    block_out[...] = block.reshape(BANDS, CH, PATCH)
    blocks.start()
    average, scale = statistics(block.astype(F32))
    stat_out[:1, :] = average
    stat_out[1:, :] = scale
    stats.start()
    stats.wait()
    blocks.wait()

    k = SET * PROWS
    gains2 = jnp.broadcast_to(gain2_ref[...], (8, C)).T[:, :1].reshape(BANDS, CH, 1)
    gain2 = jnp.zeros((CH, 1), F32)
    for n in range(BANDS):
        gain2 = jnp.where(mine == n, gains2[n], gain2)
    for j in range(BANDS):
        at = slice(j * PATCH, (j + 1) * PATCH)
        pooled = normalise(
            block_in[j].astype(F32), stat_in[j, :1, :], stat_in[j, 1:, :], gain2
        )
        spread_ref[:, at] = spread(pooled, p_low_ref[j : j + 1, :])

    def second_block(g, _):
        chunk = place(p_row_ref, spread_ref, g * k, k).astype(BF)
        second_out[pl.ds(g * SET, SET)] = chunk.reshape(SET, PROWS, LO * CH)
        second.start(g)
        return 0

    lax.fori_loop(0, SETS, second_block, 0)
    sum_ref[...] = jnp.zeros_like(sum_ref)
    count_ref[...] = jnp.zeros_like(count_ref)

    def count_group(g, _):
        cells.wait(g)
        cell = lanes_of(cell_in, g, PROWS)
        ones = jnp.ones((CH, k), F32)
        for l in range(LO):
            count_ref[...] += lax.dot_general(
                one_hot(cell[l] & (CHI - 1), 0, CHI),
                spread(ones, cell[l] >> 8),
                NT,
                preferred_element_type=F32,
            )
        return 0

    lax.fori_loop(0, SETS, count_group, 0)

    def second_group(g, _):
        second.wait(g)
        turned = second_in[pl.ds(g * SET, SET)].reshape(k, LO * CH).T
        cell = lanes_of(cell_in, g, PROWS)
        for l in range(LO):
            sum_ref[...] += lax.dot_general(
                one_hot(cell[l] & (CHI - 1), 0, CHI),
                spread(turned[l * CH : (l + 1) * CH], cell[l] >> 8),
                NT,
                preferred_element_type=F32,
            )
        return 0

    lax.fori_loop(0, SETS, second_group, 0)
    mean = (sum_ref[...] / jnp.maximum(count_ref[...], 1.0)).T.astype(BF)
    mean_ref[...] = mean.reshape(BANDS, CH, CHI)

    def give_group(g, _):
        cell = lanes_of(cell_in, g, PROWS)
        means_of = mean_ref[...].reshape(C, CHI)
        for l in range(LO):
            product = jnp.dot(
                means_of, one_hot(cell[l] & (CHI - 1), 0, CHI), preferred_element_type=F32
            )
            turned_ref[l * CH : (l + 1) * CH, :] = gather_low(
                product, cell[l] >> 8, CH
            ).astype(BF)
        back_out[pl.ds(g * SET, SET)] = turned_ref[...].T.reshape(SET, PROWS, LO * CH)
        back.start(g)
        return 0

    lax.fori_loop(0, SETS, give_group, 0)
    means.start()
    means.wait()

    for n in range(BANDS):
        table_out[n] = gelu(
            jnp.dot(weights_ref[n, 4 * CH :, :], mean_in[...].reshape(C, CHI), preferred_element_type=F32)
        )
    tables.start()

    def take_group(g, _):
        back.wait(g)
        turned_ref[...] = back_in[pl.ds(g * SET, SET)].reshape(k, LO * CH).T
        for part in range(2):
            columns = slice(part * COLS, (part + 1) * COLS)
            for j in range(BANDS):
                product = jnp.dot(
                    turned_ref[...],
                    one_hot(p_row_ref[j : j + 1, columns], g * k, k),
                    preferred_element_type=F32,
                )
                taken = gather_low(product, p_low_ref[j : j + 1, columns], CH)
                before = jnp.where(g == 0, 0.0, point_out[part, j].astype(F32))
                point_out[part, j] = (before + taken).astype(BF)

            @pl.when(g == SETS - 1)
            def _():
                points[part].start()

        return 0

    point_out[...] = jnp.zeros_like(point_out)
    lax.fori_loop(0, SETS, take_group, 0)

    for part in range(2):
        points[part].wait()

        def project_for(step, _):
            n = (mine + step) % BANDS
            result_out[part, n] = gelu(
                jnp.dot(
                    weights_ref[n, 4 * CH :, :],
                    point_in[part].reshape(C, COLS),
                    preferred_element_type=F32,
                )
            )

            @pl.when(step != BANDS)
            def _():
                results[part].copy(step).start()

            return 0

        lax.fori_loop(1, BANDS + 1, project_for, 0)
        result_in[part, mine] = result_out[part, mine]
    for part in range(2):
        results[part].wait()
    tables.wait()
    for each in (landings, first, cells, second, back):
        each.finish()
    for each in (gather, patches, blocks, stats, means, tables, *points, *results):
        each.finish()


def settle_kernel(block_in, table_in, result_in, block_ref, coarse_ref, unpooled_ref):
    for n in range(BANDS):
        block_ref[:, n * PATCH : (n + 1) * PATCH] = block_in[n]
        coarse_ref[:, n * CHI : (n + 1) * CHI] = table_in[n]
        for part in range(2):
            at = slice(n * PATCH + part * COLS, n * PATCH + (part + 1) * COLS)
            unpooled_ref[:, at] = result_in[part, n]


def on_device(feats, hilbert_pos, ln_attn, w_qkv, w_proj, ln_pool, w_pool, cell_of):
    small = lambda: pltpu.VMEM((BANDS, PATCH), jnp.int32)
    table = lambda: pltpu.VMEM((GROUPS, 4, TAB), jnp.int32)
    half = lambda *dims: pltpu.VMEM(dims, BF)
    full = lambda *dims: pltpu.VMEM(dims, F32)
    settle = pl.pallas_call(
        settle_kernel,
        out_shape=[
            jax.ShapeDtypeStruct((CH, POINTS), BF),
            jax.ShapeDtypeStruct((CH2, CELLS), BF),
            jax.ShapeDtypeStruct((CH2, POINTS), BF),
        ],
        in_specs=[INSIDE] * 3,
        out_specs=[INSIDE] * 3,
        compiler_params=pltpu.CompilerParams(vmem_limit_bytes=60 * 1024 * 1024),
    )
    return tuple(
        settle(*pl.pallas_call(
            kernel,
            out_shape=[
                jax.ShapeDtypeStruct((BANDS, CH, PATCH), BF),
                jax.ShapeDtypeStruct((BANDS, CH2, CHI), BF),
                jax.ShapeDtypeStruct((2, BANDS, CH2, COLS), BF),
            ],
            in_specs=[INSIDE] * 8,
            out_specs=[INSIDE] * 3,
            scratch_shapes=[
                half(6 * CH, C),
                small(), small(), small(), small(),
                table(), table(), table(), table(),
                half(LO * CH, POINTS),
                half(GROUPS, HROWS, LO * CH), half(GROUPS, HROWS, LO * CH),
                full(PATCH, LO * CH),
                half(BANDS, PATCH // LO, LO * CH), half(BANDS, PATCH // LO, LO * CH),
                half(BANDS, 6 * CH, C),
                half(C, PATCH), half(C, PATCH), half(C, PATCH), half(C, PATCH), half(C, PATCH),
                half(PATCH, C), half(2, C, PATCH), half(2, 2 * HD, PATCH),
                full(2, PATCH, COLS), full(2, 8, COLS), half(2, PATCH, COLS),
                half(BANDS, CH, PATCH), full(2, PATCH), full(BANDS, 2, PATCH),
                half(GROUPS, PROWS, LO * CH), half(GROUPS, PROWS, LO * CH),
                full(CHI, LO * CH), full(CHI, LO * CH),
                half(BANDS, CH, CHI), half(BANDS, CH, CHI), half(BANDS, CH2, CHI),
                half(LO * CH, SET * PROWS),
                half(GROUPS, PROWS, LO * CH), half(GROUPS, PROWS, LO * CH),
                half(2, BANDS, CH, COLS), half(2, BANDS, CH, COLS), half(2, BANDS, CH2, COLS),
                pltpu.SemaphoreType.DMA((5, GROUPS)), pltpu.SemaphoreType.DMA((5, GROUPS)),
                pltpu.SemaphoreType.DMA((10, BANDS)), pltpu.SemaphoreType.DMA((10, BANDS)),
            ],
            compiler_params=pltpu.CompilerParams(
                collective_id=0, has_side_effects=True, vmem_limit_bytes=56 * 1024 * 1024
            ),
        )(
            feats,
            hilbert_pos.reshape(1, POINTS),
            cell_of.reshape(1, POINTS),
            w_qkv.transpose(0, 2, 1).reshape(-1, C),
            w_proj,
            w_pool.T,
            ln_attn.reshape(1, C),
            ln_pool.reshape(1, C),
        ))
    )


def solution(mesh):
    in_specs = (
        P("narrow", "wide"),
        P("wide"),
        P(),
        P(None, None, "narrow"),
        P("narrow", None),
        P(),
        P(None, "narrow"),
        P("wide"),
    )
    out_specs = (P("narrow", "wide"), P("narrow", "wide"), P("narrow", "wide"))
    return jax.shard_map(
        on_device, mesh=mesh, in_specs=in_specs, out_specs=out_specs, check_vma=False
    )
```

```python
import jax
import jax.numpy as jnp
import numpy as np
from jax import lax
from jax.experimental import pallas as pl
from jax.experimental.pallas import tpu as pltpu
from jax.sharding import PartitionSpec as P

HD = 16
HEADS = 16
C = 256
C2 = 512
PATCH = 1024
POINTS = 8192
GROUPS = 32
BANDS = 8
CH = C // BANDS
CH2 = C2 // BANDS
LO = 8
TAB = 128
OWN = 1
SET = 4
SETS = GROUPS // SET
POOL_SET = 8
POOL_SETS = GROUPS // POOL_SET
INSIDE = pl.BlockSpec(memory_space=pltpu.VMEM)
COLS = 512
HROWS = 64
PROWS = 48
CELLS = 2048
CHI = CELLS // LO
BF = jnp.bfloat16
F32 = jnp.float32
NT = (((1,), (1,)), ((), ()))
SCORE = float(HD**-0.5 * np.log2(np.e))


def shape(dims, dtype):
    return jax.ShapeDtypeStruct(dims, dtype)


def one_hot(row, first, count):
    numbers = lax.broadcasted_iota(jnp.int32, (count, row.shape[1]), 0)
    return jnp.where(numbers == row - first, 1.0, 0.0).astype(BF)


def spread(values, low):
    wide = values.astype(F32)
    return jnp.concatenate([jnp.where(low == l, wide, 0.0).astype(BF) for l in range(LO)], axis=0)


def gather_low(product, low, channels):
    total = jnp.where(low == 0, product[:channels], 0.0)
    for l in range(1, LO):
        total += jnp.where(low == l, product[l * channels : (l + 1) * channels], 0.0)
    return total


def slot_of(goal):
    me = lax.axis_index("wide")
    up = ((goal >> 2) - (me >> 2)) & 7
    across = ((goal & 3) - (me & 3)) & 3
    back = jnp.where((up == 0) | (up > 4), 1, 0)
    return jnp.where(up == 0, 0, jnp.abs(up - 4)) * 8 + across * 2 + back


def partner(t, sign):
    me = lax.axis_index("wide")
    group, across, back = t // 8, t % 8 // 2, t % 2
    up = (1 - back) * (4 - group) + back * ((group + 3) // 4 * 4 + group)
    return (me // 4 + sign * up + 8) % 8 * 4 + (me % 4 + sign * across + 4) % 4


def rank_points(rows, bits, goal_ref, row_ref, low_ref):
    k = 512
    before = lax.broadcasted_iota(jnp.int32, (k, k), 0) < lax.broadcasted_iota(jnp.int32, (k, k), 1)
    before = jnp.where(before, 1.0, 0.0).astype(BF)
    goals = [slot_of(goal_ref[:, j * k : (j + 1) * k] >> bits) for j in range(POINTS // k)]
    hot = jnp.concatenate([one_hot(goal, 0, GROUPS) for goal in goals], axis=0)
    running = jnp.dot(hot, before, preferred_element_type=F32)
    carry = jnp.zeros((GROUPS, 1), F32)
    for j, goal in enumerate(goals):
        at = slice(j * k % PATCH, j * k % PATCH + k)
        of = slice(j * k // PATCH, j * k // PATCH + 1)
        member = lax.broadcasted_iota(jnp.int32, (GROUPS, k), 0) == goal
        ranks = running[j * GROUPS : (j + 1) * GROUPS]
        rank = jnp.sum(jnp.where(member, ranks + carry, 0.0), axis=0, keepdims=True).astype(jnp.int32)
        carry = carry + ranks[:, k - 1 :] + jnp.where(member[:, k - 1 :], 1.0, 0.0)
        low = jnp.zeros_like(rank)
        for l in range(1, LO):
            low += jnp.where(rank >= l * rows, 1, 0)
        row_ref[of, at] = goal * rows + rank - low * rows
        low_ref[of, at] = low


def make_table(rows, bits, value_ref, row_ref, low_ref, table_ref):
    k = 512
    table = jnp.zeros((GROUPS * 4, 2 * TAB), F32)
    for j in range(POINTS // k):
        at = slice(j * k % PATCH, j * k % PATCH + k)
        of = slice(j * k // PATCH, j * k // PATCH + 1)
        values = value_ref[:, j * k : (j + 1) * k]
        goal, low = slot_of(values >> bits), low_ref[of, at]
        value = (values & ((1 << bits) - 1)) + 1
        lane = row_ref[of, at] - goal * rows + (low & 1) * (TAB // 2)
        which = lax.broadcasted_iota(jnp.int32, (TAB, k), 0) == lane
        parts = [
            jnp.where(which, part.astype(F32), 0.0) for part in (value >> 7, value & 127)
        ]
        marks = jnp.concatenate(parts, axis=0).astype(BF)
        table += lax.dot_general(
            one_hot(goal * 4 + (low >> 1), 0, GROUPS * 4), marks, NT, preferred_element_type=F32
        )
    table = (table[:, :TAB] * 128.0 + table[:, TAB:]).astype(jnp.int32) - 1
    for t in range(GROUPS):
        table_ref[t] = table[t * 4 : (t + 1) * 4]


def place(row_ref, spread_ref, first, count):
    total = jnp.zeros((count, spread_ref.shape[0]), F32)
    for j in range(BANDS):
        total += lax.dot_general(
            one_hot(row_ref[j : j + 1, :], first, count),
            spread_ref[:, j * PATCH : (j + 1) * PATCH],
            NT,
            preferred_element_type=F32,
        )
    return total


def statistics(wide):
    average = jnp.mean(wide, axis=0, keepdims=True)
    centred = wide - average
    spread_of = jnp.mean(centred * centred, axis=0, keepdims=True)
    return average, lax.rsqrt(spread_of + 1e-05)


def normalise(wide, average, scale, gain):
    return ((wide - average) * scale * gain).astype(BF)


def remote(src, dst, send_sem, recv_sem, wide, narrow):
    return pltpu.make_async_remote_copy(
        src_ref=src,
        dst_ref=dst,
        send_sem=send_sem,
        recv_sem=recv_sem,
        device_id={"wide": wide, "narrow": narrow},
        device_id_type=pl.DeviceIdType.MESH,
    )


class Wide:
    def __init__(self, size, src, dst, send_sem, recv_sem, sign):
        self.src, self.dst, self.send_sem, self.recv_sem, self.sign = src, dst, send_sem, recv_sem, sign
        self.size = size

    def each(self, first, count, act):
        def one(i, _):
            t = first + i

            @pl.when(t != OWN)
            def _():
                act(
                    remote(
                        self.src.at[t],
                        self.dst.at[t],
                        self.send_sem.at[t],
                        self.recv_sem.at[t],
                        partner(t, self.sign),
                        lax.axis_index("narrow"),
                    )
                )

            return 0

        lax.fori_loop(0, count, one, 0)

    def start(self, group):
        self.each(group * self.size, self.size, lambda copy: copy.start())

        @pl.when(group == 0)
        def _():
            self.dst[OWN] = self.src[OWN]

    def wait(self, group):
        self.each(group * self.size, self.size, lambda copy: copy.wait_recv())

    def finish(self):
        self.each(0, GROUPS, lambda copy: copy.wait_send())


class Narrow:
    def __init__(self, src, dst, send_sem, recv_sem, whole=False):
        self.src, self.dst, self.send_sem, self.recv_sem = src, dst, send_sem, recv_sem
        self.whole = whole

    def copy(self, step):
        me = lax.axis_index("narrow")
        goal = (me + step) % BANDS
        return remote(
            self.src if self.whole else self.src.at[goal],
            self.dst.at[me],
            self.send_sem.at[step],
            self.recv_sem.at[step],
            lax.axis_index("wide"),
            goal,
        )

    def start(self):
        me = lax.axis_index("narrow")
        lax.fori_loop(1, BANDS, lambda s, _: self.copy(s).start() or 0, 0)
        self.dst[me] = self.src[...] if self.whole else self.src[me]

    def start_half(self, half):
        me = lax.axis_index("narrow")

        def one(i, _):
            step = (half * 4 + i - me + BANDS) % BANDS

            @pl.when(step != 0)
            def _():
                self.copy(step).start()

            return 0

        lax.fori_loop(0, 4, one, 0)

        @pl.when(me // 4 == half)
        def _():
            self.dst[me] = self.src[me]

    def wait(self):
        me = lax.axis_index("narrow")

        def one(step, _):
            landed = self.dst.at[(me - step + BANDS) % BANDS]
            remote(
                landed,
                landed,
                self.send_sem.at[step],
                self.recv_sem.at[step],
                lax.axis_index("wide"),
                me,
            ).wait_recv()
            return 0

        lax.fori_loop(1, BANDS, one, 0)

    def finish(self):
        lax.fori_loop(1, BANDS, lambda s, _: self.copy(s).wait_send() or 0, 0)


def attend(q_ref, k_ref, v_ref, att_ref, key_ref, query_ref, value_ref, score_ref, top_ref, prob_ref):
    key_ref[...] = k_ref[...].T
    query_ref[...] = jnp.zeros_like(query_ref)
    value_ref[...] = jnp.ones_like(value_ref)
    parts = PATCH // COLS

    def head_rows(h):
        return pl.ds(pl.multiple_of(h * HD, HD), HD)

    def score(h, part, slot):
        if part == 0:
            query_ref[h % 2, head_rows((h + HEADS - 2) % HEADS), :] = jnp.zeros((HD, PATCH), BF)
            query_ref[h % 2, head_rows(h), :] = q_ref[head_rows(h), :]
        scores = jnp.dot(
            key_ref[...],
            query_ref[h % 2, :, part * COLS : (part + 1) * COLS],
            preferred_element_type=F32,
        )
        score_ref[slot] = scores
        top_ref[slot] = jnp.broadcast_to(jnp.max(scores, axis=0, keepdims=True), (8, COLS))

    score(0, 0, 0)

    def two_heads(pair, _):
        for unit in range(2 * parts):
            h, part, slot = pair * 2 + unit // parts, unit % parts, unit % 2
            after = unit + 1
            score(jnp.minimum(pair * 2 + after // parts, HEADS - 1), after % parts, after % 2)
            prob_ref[slot] = jnp.exp2((score_ref[slot] - top_ref[slot][:1]) * SCORE).astype(BF)
            value_ref[h % 2, :HD, :] = v_ref[head_rows(h), :]
            sums = jnp.dot(value_ref[h % 2], prob_ref[slot], preferred_element_type=F32)
            att_ref[head_rows(h), part * COLS : (part + 1) * COLS] = (sums[:HD] / sums[HD:]).astype(BF)
        return 0

    lax.fori_loop(0, HEADS // 2, two_heads, 0)


def gelu(value):
    return (value * (1.0 + lax.erf(value * (0.5**0.5))) * 0.5).astype(BF)


def lanes_of(table_ref, group, size, rows):
    halves = [
        jnp.concatenate([table_ref[group * size + i][:, at : at + rows] for i in range(size)], axis=1)
        for at in (0, TAB // 2)
    ]
    return [halves[l % 2][l // 2 : l // 2 + 1] for l in range(LO)]


def kernel(
    feats_ref, hilbert_ref, cell_ref, qkv_ref, proj_ref, pool_ref, gain_ref, gain2_ref,
    block_in, table_in, result_in,
    own_ref,
    row_ref, low_ref, p_row_ref, p_low_ref,
    land_out, land_in, cell_out, cell_in,
    spread_ref, first_out, first_in, acc_ref,
    patch_out, patch_in, weights_ref,
    x_ref, q_ref, k_ref, v_ref, att_ref, key_ref, query_ref, value_ref, score_ref, top_ref, prob_ref,
    block_out, stat_out, stat_in, second_out, second_in,
    sum_ref, count_ref, mean_ref, mean_in, table_out,
    turned_ref, back_out, back_in, point_out, point_in, result_out,
    wide_send, wide_recv, narrow_send, narrow_recv,
):
    me = lax.axis_index("wide")
    mine = lax.axis_index("narrow")

    def wide(number, size, src, dst, sign=1):
        return Wide(size, src, dst, wide_send.at[number], wide_recv.at[number], sign)

    def narrow(number, src, dst, whole=False):
        return Narrow(src, dst, narrow_send.at[number], narrow_recv.at[number], whole)

    landings = wide(0, SET, land_out, land_in)
    first = wide(1, SET, first_out, first_in)
    cells = wide(2, POOL_SET, cell_out, cell_in)
    second = wide(3, POOL_SET, second_out, second_in)
    back = wide(4, POOL_SET, back_out, back_in, -1)
    gather = narrow(0, own_ref, weights_ref, True)
    patches = narrow(1, patch_out, patch_in)
    blocks = narrow(2, block_out, block_in)
    stats = narrow(5, stat_out, stat_in, True)
    points = [narrow(6 + i, point_out.at[i], point_in.at[i]) for i in range(2)]
    results = [narrow(8 + i, result_out.at[i], result_in.at[i]) for i in range(2)]
    means = narrow(3, mean_ref, mean_in)
    tables = narrow(4, table_out, table_in)

    barrier = pltpu.get_barrier_semaphore()

    def greet_wide(t, _):
        pl.semaphore_signal(
            barrier,
            inc=1,
            device_id={"wide": (me + t) % GROUPS, "narrow": mine},
            device_id_type=pl.DeviceIdType.MESH,
        )
        return 0

    def greet_narrow(t, _):
        pl.semaphore_signal(
            barrier,
            inc=1,
            device_id={"wide": me, "narrow": (mine + t) % BANDS},
            device_id_type=pl.DeviceIdType.MESH,
        )
        return 0

    lax.fori_loop(1, GROUPS, greet_wide, 0)
    lax.fori_loop(1, BANDS, greet_narrow, 0)

    own_ref[: 3 * CH, :] = qkv_ref[...]
    own_ref[3 * CH : 4 * CH, :] = proj_ref[...]
    own_ref[4 * CH :, :] = pool_ref[...]

    rank_points(HROWS, 13, hilbert_ref, row_ref, low_ref)
    for j in range(BANDS):
        at = slice(j * PATCH, (j + 1) * PATCH)
        spread_ref[:, at] = spread(feats_ref[:, at], low_ref[j : j + 1, :])

    def first_block(g, _):
        count = SET * HROWS
        chunk = place(row_ref, spread_ref, g * count, count).astype(BF)
        first_out[pl.ds(g * SET, SET)] = chunk.reshape(SET, HROWS, LO * CH)

        @pl.when(g == 0)
        def _():
            pl.semaphore_wait(barrier, GROUPS + BANDS - 2)

        first.start(g)

        @pl.when(g == 1)
        def _():
            make_table(HROWS, 13, hilbert_ref, row_ref, low_ref, land_out)
            lax.fori_loop(0, SETS, lambda i, _: landings.start(i) or 0, 0)

        return 0

    lax.fori_loop(0, SETS, first_block, 0)
    gather.start()
    rank_points(PROWS, 11, cell_ref, p_row_ref, p_low_ref)
    make_table(PROWS, 11, cell_ref, p_row_ref, p_low_ref, cell_out)

    def first_group(g, _):
        landings.wait(g)
        first.wait(g)
        k = SET * HROWS
        turned = first_in[pl.ds(g * SET, SET)].reshape(k, LO * CH).T
        landing = lanes_of(land_in, g, SET, HROWS)
        for l in range(LO):
            spread_ref[:, l * k : (l + 1) * k] = spread(
                turned[l * CH : (l + 1) * CH], (landing[l] >> 7) & 7
            )
        rows = [(each >> 10) * 128 + (each & 127) for each in landing]
        for m in range(2):
            total = jnp.zeros((512, LO * CH), F32)
            for l in range(LO):
                total += lax.dot_general(
                    one_hot(rows[l], m * 512, 512),
                    spread_ref[:, l * k : (l + 1) * k],
                    NT,
                    preferred_element_type=F32,
                )
            at = slice(m * 512, (m + 1) * 512)
            total = jnp.where(g == 0, total, total + acc_ref[at, :])
            acc_ref[at, :] = total

            @pl.when(g == SETS - 1)
            def _():
                patch_out[m * 4 : (m + 1) * 4] = total.astype(BF).reshape(4, PATCH // LO, LO * CH)
                patches.start_half(m)

        return 0

    lax.fori_loop(0, SETS, first_group, 0)
    lax.fori_loop(0, POOL_SETS, lambda i, _: cells.start(i) or 0, 0)
    gather.wait()
    patches.wait()

    for n in range(BANDS):
        turned = patch_in[n].T
        for l in range(LO):
            x_ref[n * CH : (n + 1) * CH, l * 128 : (l + 1) * 128] = turned[l * CH : (l + 1) * CH]
    gains = jnp.broadcast_to(gain_ref[...], (8, C)).T[:, :1]
    wide_x = x_ref[...].astype(F32)
    normed = normalise(wide_x, *statistics(wide_x), gains)

    def weight(start):
        return jnp.concatenate([weights_ref[n, start : start + CH, :] for n in range(BANDS)], axis=0)

    def project(t):
        return jnp.dot(weight(t * CH), normed, preferred_element_type=F32).astype(BF)

    q_ref[...] = project(0)
    k_ref[...] = project(1)
    v_ref[...] = project(2)
    attend(
        q_ref, k_ref, v_ref, att_ref, key_ref, query_ref, value_ref, score_ref, top_ref, prob_ref
    )
    added = jnp.dot(weight(3 * CH).T, att_ref[...], preferred_element_type=F32)
    block = (x_ref[...].astype(F32) + added).astype(BF)
    block_out[...] = block.reshape(BANDS, CH, PATCH)
    blocks.start()
    average, scale = statistics(block.astype(F32))
    stat_out[:1, :] = average
    stat_out[1:, :] = scale
    stats.start()
    stats.wait()
    blocks.wait()

    k = POOL_SET * PROWS
    gains2 = jnp.broadcast_to(gain2_ref[...], (8, C)).T[:, :1].reshape(BANDS, CH, 1)
    gain2 = jnp.zeros((CH, 1), F32)
    for n in range(BANDS):
        gain2 = jnp.where(mine == n, gains2[n], gain2)
    for j in range(BANDS):
        at = slice(j * PATCH, (j + 1) * PATCH)
        pooled = normalise(
            block_in[j].astype(F32), stat_in[j, :1, :], stat_in[j, 1:, :], gain2
        )
        spread_ref[:, at] = spread(pooled, p_low_ref[j : j + 1, :])

    def second_block(g, _):
        chunk = place(p_row_ref, spread_ref, g * k, k).astype(BF)
        second_out[pl.ds(g * POOL_SET, POOL_SET)] = chunk.reshape(POOL_SET, PROWS, LO * CH)
        second.start(g)
        return 0

    lax.fori_loop(0, POOL_SETS, second_block, 0)
    sum_ref[...] = jnp.zeros_like(sum_ref)
    count_ref[...] = jnp.zeros_like(count_ref)

    def count_group(g, _):
        cells.wait(g)
        cell = lanes_of(cell_in, g, POOL_SET, PROWS)
        ones = jnp.ones((CH, k), F32)
        for l in range(LO):
            count_ref[...] += lax.dot_general(
                one_hot(cell[l] & (CHI - 1), 0, CHI),
                spread(ones, cell[l] >> 8),
                NT,
                preferred_element_type=F32,
            )
        return 0

    lax.fori_loop(0, POOL_SETS, count_group, 0)

    def second_group(g, _):
        second.wait(g)
        turned = second_in[pl.ds(g * POOL_SET, POOL_SET)].reshape(k, LO * CH).T
        cell = lanes_of(cell_in, g, POOL_SET, PROWS)
        for l in range(LO):
            sum_ref[...] += lax.dot_general(
                one_hot(cell[l] & (CHI - 1), 0, CHI),
                spread(turned[l * CH : (l + 1) * CH], cell[l] >> 8),
                NT,
                preferred_element_type=F32,
            )
        return 0

    lax.fori_loop(0, POOL_SETS, second_group, 0)
    mean = (sum_ref[...] / jnp.maximum(count_ref[...], 1.0)).T.astype(BF)
    mean_ref[...] = mean.reshape(BANDS, CH, CHI)

    def give_group(g, _):
        cell = lanes_of(cell_in, g, POOL_SET, PROWS)
        means_of = mean_ref[...].reshape(C, CHI)
        for l in range(LO):
            product = jnp.dot(
                means_of, one_hot(cell[l] & (CHI - 1), 0, CHI), preferred_element_type=F32
            )
            turned_ref[l * CH : (l + 1) * CH, :] = gather_low(
                product, cell[l] >> 8, CH
            ).astype(BF)
        back_out[pl.ds(g * POOL_SET, POOL_SET)] = turned_ref[...].T.reshape(POOL_SET, PROWS, LO * CH)
        back.start(g)
        return 0

    lax.fori_loop(0, POOL_SETS, give_group, 0)
    means.start()

    def take_group(g, _):
        back.wait(g)
        turned_ref[...] = back_in[pl.ds(g * POOL_SET, POOL_SET)].reshape(k, LO * CH).T
        for part in range(2):
            columns = slice(part * COLS, (part + 1) * COLS)
            for j in range(BANDS):
                product = jnp.dot(
                    turned_ref[...],
                    one_hot(p_row_ref[j : j + 1, columns], g * k, k),
                    preferred_element_type=F32,
                )
                taken = gather_low(product, p_low_ref[j : j + 1, columns], CH)
                before = jnp.where(g == 0, 0.0, point_out[part, j].astype(F32))
                point_out[part, j] = (before + taken).astype(BF)

            @pl.when(g == POOL_SETS - 1)
            def _():
                points[part].start()

        return 0

    point_out[...] = jnp.zeros_like(point_out)
    lax.fori_loop(0, POOL_SETS, take_group, 0)
    means.wait()

    for n in range(BANDS):
        table_out[n] = gelu(
            jnp.dot(weights_ref[n, 4 * CH :, :], mean_in[...].reshape(C, CHI), preferred_element_type=F32)
        )
    tables.start()

    for part in range(2):
        points[part].wait()

        def project_for(step, _):
            n = (mine + step) % BANDS
            result_out[part, n] = gelu(
                jnp.dot(
                    weights_ref[n, 4 * CH :, :],
                    point_in[part].reshape(C, COLS),
                    preferred_element_type=F32,
                )
            )

            @pl.when(step != BANDS)
            def _():
                results[part].copy(step).start()

            return 0

        lax.fori_loop(1, BANDS + 1, project_for, 0)
        result_in[part, mine] = result_out[part, mine]
    for part in range(2):
        results[part].wait()
    tables.wait()
    for each in (landings, first, cells, second, back):
        each.finish()
    for each in (gather, patches, blocks, stats, means, tables, *points, *results):
        each.finish()


def settle_kernel(block_in, table_in, result_in, block_ref, coarse_ref, unpooled_ref):
    for n in range(BANDS):
        block_ref[:, n * PATCH : (n + 1) * PATCH] = block_in[n]
        coarse_ref[:, n * CHI : (n + 1) * CHI] = table_in[n]
        for part in range(2):
            at = slice(n * PATCH + part * COLS, n * PATCH + (part + 1) * COLS)
            unpooled_ref[:, at] = result_in[part, n]


def on_device(feats, hilbert_pos, ln_attn, w_qkv, w_proj, ln_pool, w_pool, cell_of):
    small = lambda: pltpu.VMEM((BANDS, PATCH), jnp.int32)
    table = lambda: pltpu.VMEM((GROUPS, 4, TAB), jnp.int32)
    half = lambda *dims: pltpu.VMEM(dims, BF)
    full = lambda *dims: pltpu.VMEM(dims, F32)
    settle = pl.pallas_call(
        settle_kernel,
        out_shape=[
            jax.ShapeDtypeStruct((CH, POINTS), BF),
            jax.ShapeDtypeStruct((CH2, CELLS), BF),
            jax.ShapeDtypeStruct((CH2, POINTS), BF),
        ],
        in_specs=[INSIDE] * 3,
        out_specs=[INSIDE] * 3,
        compiler_params=pltpu.CompilerParams(vmem_limit_bytes=60 * 1024 * 1024),
    )
    return tuple(
        settle(*pl.pallas_call(
            kernel,
            out_shape=[
                jax.ShapeDtypeStruct((BANDS, CH, PATCH), BF),
                jax.ShapeDtypeStruct((BANDS, CH2, CHI), BF),
                jax.ShapeDtypeStruct((2, BANDS, CH2, COLS), BF),
            ],
            in_specs=[INSIDE] * 8,
            out_specs=[INSIDE] * 3,
            scratch_shapes=[
                half(6 * CH, C),
                small(), small(), small(), small(),
                table(), table(), table(), table(),
                half(LO * CH, POINTS),
                half(GROUPS, HROWS, LO * CH), half(GROUPS, HROWS, LO * CH),
                full(PATCH, LO * CH),
                half(BANDS, PATCH // LO, LO * CH), half(BANDS, PATCH // LO, LO * CH),
                half(BANDS, 6 * CH, C),
                half(C, PATCH), half(C, PATCH), half(C, PATCH), half(C, PATCH), half(C, PATCH),
                half(PATCH, C), half(2, C, PATCH), half(2, 2 * HD, PATCH),
                full(2, PATCH, COLS), full(2, 8, COLS), half(2, PATCH, COLS),
                half(BANDS, CH, PATCH), full(2, PATCH), full(BANDS, 2, PATCH),
                half(GROUPS, PROWS, LO * CH), half(GROUPS, PROWS, LO * CH),
                full(CHI, LO * CH), full(CHI, LO * CH),
                half(BANDS, CH, CHI), half(BANDS, CH, CHI), half(BANDS, CH2, CHI),
                half(LO * CH, POOL_SET * PROWS),
                half(GROUPS, PROWS, LO * CH), half(GROUPS, PROWS, LO * CH),
                half(2, BANDS, CH, COLS), half(2, BANDS, CH, COLS), half(2, BANDS, CH2, COLS),
                pltpu.SemaphoreType.DMA((5, GROUPS)), pltpu.SemaphoreType.DMA((5, GROUPS)),
                pltpu.SemaphoreType.DMA((10, BANDS)), pltpu.SemaphoreType.DMA((10, BANDS)),
            ],
            compiler_params=pltpu.CompilerParams(
                collective_id=0, has_side_effects=True, vmem_limit_bytes=56 * 1024 * 1024
            ),
        )(
            feats,
            hilbert_pos.reshape(1, POINTS),
            cell_of.reshape(1, POINTS),
            w_qkv.transpose(0, 2, 1).reshape(-1, C),
            w_proj,
            w_pool.T,
            ln_attn.reshape(1, C),
            ln_pool.reshape(1, C),
        ))
    )


def solution(mesh):
    in_specs = (
        P("narrow", "wide"),
        P("wide"),
        P(),
        P(None, None, "narrow"),
        P("narrow", None),
        P(),
        P(None, "narrow"),
        P("wide"),
    )
    out_specs = (P("narrow", "wide"), P("narrow", "wide"), P("narrow", "wide"))
    return jax.shard_map(
        on_device, mesh=mesh, in_specs=in_specs, out_specs=out_specs, check_vma=False
    )
```

```python
import jax
import jax.numpy as jnp
import numpy as np
from jax import lax
from jax.experimental import pallas as pl
from jax.experimental.pallas import tpu as pltpu
from jax.sharding import PartitionSpec as P

HD = 16
HEADS = 16
C = 256
C2 = 512
PATCH = 1024
POINTS = 8192
GROUPS = 32
BANDS = 8
CH = C // BANDS
CH2 = C2 // BANDS
LO = 8
TAB = 128
OWN = 1
INSIDE = pl.BlockSpec(memory_space=pltpu.VMEM)
COLS = 512
HROWS = 64
PROWS = 48
CELLS = 2048
CHI = CELLS // LO
BF = jnp.bfloat16
F32 = jnp.float32
NT = (((1,), (1,)), ((), ()))
SCORE = float(HD**-0.5 * np.log2(np.e))


def shape(dims, dtype):
    return jax.ShapeDtypeStruct(dims, dtype)


def one_hot(row, first, count):
    numbers = lax.broadcasted_iota(jnp.int32, (count, row.shape[1]), 0)
    return jnp.where(numbers == row - first, 1.0, 0.0).astype(BF)


def spread(values, low):
    wide = values.astype(F32)
    return jnp.concatenate([jnp.where(low == l, wide, 0.0).astype(BF) for l in range(LO)], axis=0)


def gather_low(product, low, channels):
    total = jnp.where(low == 0, product[:channels], 0.0)
    for l in range(1, LO):
        total += jnp.where(low == l, product[l * channels : (l + 1) * channels], 0.0)
    return total


def slot_of(goal):
    me = lax.axis_index("wide")
    up = ((goal >> 2) - (me >> 2)) & 7
    across = ((goal & 3) - (me & 3)) & 3
    back = jnp.where((up == 0) | (up > 4), 1, 0)
    return jnp.where(up == 0, 0, jnp.abs(up - 4)) * 8 + across * 2 + back


def partner(t, sign):
    me = lax.axis_index("wide")
    group, across, back = t // 8, t % 8 // 2, t % 2
    up = (1 - back) * (4 - group) + back * ((group + 3) // 4 * 4 + group)
    return (me // 4 + sign * up + 8) % 8 * 4 + (me % 4 + sign * across + 4) % 4


def rank_points(rows, bits, goal_ref, row_ref, low_ref):
    k = 512
    before = lax.broadcasted_iota(jnp.int32, (k, k), 0) < lax.broadcasted_iota(jnp.int32, (k, k), 1)
    before = jnp.where(before, 1.0, 0.0).astype(BF)
    goals = [slot_of(goal_ref[:, j * k : (j + 1) * k] >> bits) for j in range(POINTS // k)]
    hot = jnp.concatenate([one_hot(goal, 0, GROUPS) for goal in goals], axis=0)
    running = jnp.dot(hot, before, preferred_element_type=F32)
    carry = jnp.zeros((GROUPS, 1), F32)
    for j, goal in enumerate(goals):
        at = slice(j * k % PATCH, j * k % PATCH + k)
        of = slice(j * k // PATCH, j * k // PATCH + 1)
        member = lax.broadcasted_iota(jnp.int32, (GROUPS, k), 0) == goal
        ranks = running[j * GROUPS : (j + 1) * GROUPS]
        rank = jnp.sum(jnp.where(member, ranks + carry, 0.0), axis=0, keepdims=True).astype(jnp.int32)
        carry = carry + ranks[:, k - 1 :] + jnp.where(member[:, k - 1 :], 1.0, 0.0)
        low = jnp.zeros_like(rank)
        for l in range(1, LO):
            low += jnp.where(rank >= l * rows, 1, 0)
        row_ref[of, at] = goal * rows + rank - low * rows
        low_ref[of, at] = low


def make_table(rows, bits, value_ref, row_ref, low_ref, table_ref):
    k = 512
    table = jnp.zeros((GROUPS * 4, 2 * TAB), F32)
    for j in range(POINTS // k):
        at = slice(j * k % PATCH, j * k % PATCH + k)
        of = slice(j * k // PATCH, j * k // PATCH + 1)
        values = value_ref[:, j * k : (j + 1) * k]
        goal, low = slot_of(values >> bits), low_ref[of, at]
        value = (values & ((1 << bits) - 1)) + 1
        lane = row_ref[of, at] - goal * rows + (low & 1) * (TAB // 2)
        which = lax.broadcasted_iota(jnp.int32, (TAB, k), 0) == lane
        parts = [
            jnp.where(which, part.astype(F32), 0.0) for part in (value >> 7, value & 127)
        ]
        marks = jnp.concatenate(parts, axis=0).astype(BF)
        table += lax.dot_general(
            one_hot(goal * 4 + (low >> 1), 0, GROUPS * 4), marks, NT, preferred_element_type=F32
        )
    table = (table[:, :TAB] * 128.0 + table[:, TAB:]).astype(jnp.int32) - 1
    for t in range(GROUPS):
        table_ref[t] = table[t * 4 : (t + 1) * 4]


def place(row_ref, spread_ref, first, count):
    total = jnp.zeros((count, spread_ref.shape[0]), F32)
    for j in range(BANDS):
        total += lax.dot_general(
            one_hot(row_ref[j : j + 1, :], first, count),
            spread_ref[:, j * PATCH : (j + 1) * PATCH],
            NT,
            preferred_element_type=F32,
        )
    return total


def statistics(wide):
    average = jnp.mean(wide, axis=0, keepdims=True)
    centred = wide - average
    spread_of = jnp.mean(centred * centred, axis=0, keepdims=True)
    return average, lax.rsqrt(spread_of + 1e-05)


def normalise(wide, average, scale, gain):
    return ((wide - average) * scale * gain).astype(BF)


def remote(src, dst, send_sem, recv_sem, wide, narrow):
    return pltpu.make_async_remote_copy(
        src_ref=src,
        dst_ref=dst,
        send_sem=send_sem,
        recv_sem=recv_sem,
        device_id={"wide": wide, "narrow": narrow},
        device_id_type=pl.DeviceIdType.MESH,
    )


class Wide:
    def __init__(self, src, dst, send_sem, recv_sem, sign):
        self.src, self.dst, self.send_sem, self.recv_sem, self.sign = src, dst, send_sem, recv_sem, sign

    def each(self, first, count, act):
        def one(i, _):
            t = first + i

            @pl.when(t != OWN)
            def _():
                act(
                    remote(
                        self.src.at[t],
                        self.dst.at[t],
                        self.send_sem.at[t],
                        self.recv_sem.at[t],
                        partner(t, self.sign),
                        lax.axis_index("narrow"),
                    )
                )

            return 0

        lax.fori_loop(0, count, one, 0)

    def start(self, group):
        self.each(group * 8, 8, lambda copy: copy.start())

        @pl.when(group == OWN // 8)
        def _():
            self.dst[OWN] = self.src[OWN]

    def wait(self, group):
        self.each(group * 8, 8, lambda copy: copy.wait_recv())

    def finish(self):
        self.each(0, GROUPS, lambda copy: copy.wait_send())


class Narrow:
    def __init__(self, src, dst, send_sem, recv_sem, whole=False):
        self.src, self.dst, self.send_sem, self.recv_sem = src, dst, send_sem, recv_sem
        self.whole = whole

    def copy(self, step):
        me = lax.axis_index("narrow")
        goal = (me + step) % BANDS
        return remote(
            self.src if self.whole else self.src.at[goal],
            self.dst.at[me],
            self.send_sem.at[step],
            self.recv_sem.at[step],
            lax.axis_index("wide"),
            goal,
        )

    def start(self):
        me = lax.axis_index("narrow")
        lax.fori_loop(1, BANDS, lambda s, _: self.copy(s).start() or 0, 0)
        self.dst[me] = self.src[...] if self.whole else self.src[me]

    def start_half(self, half):
        me = lax.axis_index("narrow")

        def one(i, _):
            step = (half * 4 + i - me + BANDS) % BANDS

            @pl.when(step != 0)
            def _():
                self.copy(step).start()

            return 0

        lax.fori_loop(0, 4, one, 0)

        @pl.when(me // 4 == half)
        def _():
            self.dst[me] = self.src[me]

    def wait(self):
        me = lax.axis_index("narrow")

        def one(step, _):
            landed = self.dst.at[(me - step + BANDS) % BANDS]
            remote(
                landed,
                landed,
                self.send_sem.at[step],
                self.recv_sem.at[step],
                lax.axis_index("wide"),
                me,
            ).wait_recv()
            return 0

        lax.fori_loop(1, BANDS, one, 0)

    def finish(self):
        lax.fori_loop(1, BANDS, lambda s, _: self.copy(s).wait_send() or 0, 0)


def attend(q_ref, k_ref, v_ref, att_ref, key_ref, query_ref, value_ref, score_ref, top_ref, prob_ref):
    key_ref[...] = k_ref[...].T
    query_ref[...] = jnp.zeros_like(query_ref)
    value_ref[...] = jnp.ones_like(value_ref)
    parts = PATCH // COLS

    def head_rows(h):
        return pl.ds(pl.multiple_of(h * HD, HD), HD)

    def score(h, part, slot):
        if part == 0:
            query_ref[h % 2, head_rows((h + HEADS - 2) % HEADS), :] = jnp.zeros((HD, PATCH), BF)
            query_ref[h % 2, head_rows(h), :] = q_ref[head_rows(h), :]
        scores = jnp.dot(
            key_ref[...],
            query_ref[h % 2, :, part * COLS : (part + 1) * COLS],
            preferred_element_type=F32,
        )
        score_ref[slot] = scores
        top_ref[slot] = jnp.broadcast_to(jnp.max(scores, axis=0, keepdims=True), (8, COLS))

    score(0, 0, 0)

    def two_heads(pair, _):
        for unit in range(2 * parts):
            h, part, slot = pair * 2 + unit // parts, unit % parts, unit % 2
            after = unit + 1
            score(jnp.minimum(pair * 2 + after // parts, HEADS - 1), after % parts, after % 2)
            prob_ref[slot] = jnp.exp2((score_ref[slot] - top_ref[slot][:1]) * SCORE).astype(BF)
            value_ref[h % 2, :HD, :] = v_ref[head_rows(h), :]
            sums = jnp.dot(value_ref[h % 2], prob_ref[slot], preferred_element_type=F32)
            att_ref[head_rows(h), part * COLS : (part + 1) * COLS] = (sums[:HD] / sums[HD:]).astype(BF)
        return 0

    lax.fori_loop(0, HEADS // 2, two_heads, 0)


def gelu(value):
    return (value * (1.0 + lax.erf(value * (0.5**0.5))) * 0.5).astype(BF)


def lanes_of(table_ref, group, rows):
    halves = [
        jnp.concatenate([table_ref[group * 8 + i][:, at : at + rows] for i in range(8)], axis=1)
        for at in (0, TAB // 2)
    ]
    return [halves[l % 2][l // 2 : l // 2 + 1] for l in range(LO)]


def kernel(
    feats_ref, hilbert_ref, cell_ref, qkv_ref, proj_ref, pool_ref, gain_ref, gain2_ref,
    block_in, table_in, result_in,
    own_ref,
    row_ref, low_ref, p_row_ref, p_low_ref,
    land_out, land_in, cell_out, cell_in,
    spread_ref, first_out, first_in, acc_ref,
    patch_out, patch_in, weights_ref,
    x_ref, q_ref, k_ref, v_ref, att_ref, key_ref, query_ref, value_ref, score_ref, top_ref, prob_ref,
    block_out, stat_out, stat_in, second_out, second_in,
    sum_ref, count_ref, mean_ref, mean_in, table_out,
    turned_ref, back_out, back_in, point_out, point_in, result_out,
    wide_send, wide_recv, narrow_send, narrow_recv,
):
    me = lax.axis_index("wide")
    mine = lax.axis_index("narrow")

    def wide(number, src, dst, sign=1):
        return Wide(src, dst, wide_send.at[number], wide_recv.at[number], sign)

    def narrow(number, src, dst, whole=False):
        return Narrow(src, dst, narrow_send.at[number], narrow_recv.at[number], whole)

    landings = wide(0, land_out, land_in)
    first = wide(1, first_out, first_in)
    cells = wide(2, cell_out, cell_in)
    second = wide(3, second_out, second_in)
    back = wide(4, back_out, back_in, -1)
    gather = narrow(0, own_ref, weights_ref, True)
    patches = narrow(1, patch_out, patch_in)
    blocks = narrow(2, block_out, block_in)
    stats = narrow(5, stat_out, stat_in, True)
    points = narrow(6, point_out, point_in)
    results = narrow(7, result_out, result_in)
    means = narrow(3, mean_ref, mean_in)
    tables = narrow(4, table_out, table_in)

    barrier = pltpu.get_barrier_semaphore()

    def greet_wide(t, _):
        pl.semaphore_signal(
            barrier,
            inc=1,
            device_id={"wide": (me + t) % GROUPS, "narrow": mine},
            device_id_type=pl.DeviceIdType.MESH,
        )
        return 0

    def greet_narrow(t, _):
        pl.semaphore_signal(
            barrier,
            inc=1,
            device_id={"wide": me, "narrow": (mine + t) % BANDS},
            device_id_type=pl.DeviceIdType.MESH,
        )
        return 0

    lax.fori_loop(1, GROUPS, greet_wide, 0)
    lax.fori_loop(1, BANDS, greet_narrow, 0)

    own_ref[: 3 * CH, :] = qkv_ref[...]
    own_ref[3 * CH : 4 * CH, :] = proj_ref[...]
    own_ref[4 * CH :, :] = pool_ref[...]

    rank_points(HROWS, 13, hilbert_ref, row_ref, low_ref)
    for j in range(BANDS):
        at = slice(j * PATCH, (j + 1) * PATCH)
        spread_ref[:, at] = spread(feats_ref[:, at], low_ref[j : j + 1, :])

    def first_block(g, _):
        chunk = place(row_ref, spread_ref, g * 512, 512).astype(BF)
        first_out[pl.ds(g * 8, 8)] = chunk.reshape(8, HROWS, LO * CH)

        @pl.when(g == 0)
        def _():
            pl.semaphore_wait(barrier, GROUPS + BANDS - 2)

        first.start(g)

        @pl.when(g == 0)
        def _():
            make_table(HROWS, 13, hilbert_ref, row_ref, low_ref, land_out)
            lax.fori_loop(0, 4, lambda i, _: landings.start(i) or 0, 0)

        return 0

    lax.fori_loop(0, 4, first_block, 0)
    gather.start()
    rank_points(PROWS, 11, cell_ref, p_row_ref, p_low_ref)
    make_table(PROWS, 11, cell_ref, p_row_ref, p_low_ref, cell_out)

    def first_group(g, _):
        landings.wait(g)
        first.wait(g)
        k = 8 * HROWS
        turned = first_in[pl.ds(g * 8, 8)].reshape(k, LO * CH).T
        landing = lanes_of(land_in, g, HROWS)
        for l in range(LO):
            spread_ref[:, l * k : (l + 1) * k] = spread(
                turned[l * CH : (l + 1) * CH], (landing[l] >> 7) & 7
            )
        rows = [(each >> 10) * 128 + (each & 127) for each in landing]
        for m in range(2):
            total = jnp.zeros((512, LO * CH), F32)
            for l in range(LO):
                total += lax.dot_general(
                    one_hot(rows[l], m * 512, 512),
                    spread_ref[:, l * k : (l + 1) * k],
                    NT,
                    preferred_element_type=F32,
                )
            at = slice(m * 512, (m + 1) * 512)
            total = jnp.where(g == 0, total, total + acc_ref[at, :])
            acc_ref[at, :] = total

            @pl.when(g == 3)
            def _():
                patch_out[m * 4 : (m + 1) * 4] = total.astype(BF).reshape(4, PATCH // LO, LO * CH)
                patches.start_half(m)

        return 0

    lax.fori_loop(0, 4, first_group, 0)
    lax.fori_loop(0, 4, lambda i, _: cells.start(i) or 0, 0)
    gather.wait()
    patches.wait()

    for n in range(BANDS):
        turned = patch_in[n].T
        for l in range(LO):
            x_ref[n * CH : (n + 1) * CH, l * 128 : (l + 1) * 128] = turned[l * CH : (l + 1) * CH]
    gains = jnp.broadcast_to(gain_ref[...], (8, C)).T[:, :1]
    wide_x = x_ref[...].astype(F32)
    normed = normalise(wide_x, *statistics(wide_x), gains)

    def weight(start):
        return jnp.concatenate([weights_ref[n, start : start + CH, :] for n in range(BANDS)], axis=0)

    def project(t):
        return jnp.dot(weight(t * CH), normed, preferred_element_type=F32).astype(BF)

    q_ref[...] = project(0)
    k_ref[...] = project(1)
    v_ref[...] = project(2)
    attend(
        q_ref, k_ref, v_ref, att_ref, key_ref, query_ref, value_ref, score_ref, top_ref, prob_ref
    )
    added = jnp.dot(weight(3 * CH).T, att_ref[...], preferred_element_type=F32)
    block = (x_ref[...].astype(F32) + added).astype(BF)
    block_out[...] = block.reshape(BANDS, CH, PATCH)
    blocks.start()
    average, scale = statistics(block.astype(F32))
    stat_out[:1, :] = average
    stat_out[1:, :] = scale
    stats.start()
    stats.wait()
    blocks.wait()

    gains2 = jnp.broadcast_to(gain2_ref[...], (8, C)).T[:, :1].reshape(BANDS, CH, 1)
    gain2 = jnp.zeros((CH, 1), F32)
    for n in range(BANDS):
        gain2 = jnp.where(mine == n, gains2[n], gain2)
    for j in range(BANDS):
        at = slice(j * PATCH, (j + 1) * PATCH)
        pooled = normalise(
            block_in[j].astype(F32), stat_in[j, :1, :], stat_in[j, 1:, :], gain2
        )
        spread_ref[:, at] = spread(pooled, p_low_ref[j : j + 1, :])

    def second_block(g, _):
        chunk = place(p_row_ref, spread_ref, g * 384, 384).astype(BF)
        second_out[pl.ds(g * 8, 8)] = chunk.reshape(8, PROWS, LO * CH)
        second.start(g)
        return 0

    lax.fori_loop(0, 4, second_block, 0)
    sum_ref[...] = jnp.zeros_like(sum_ref)
    count_ref[...] = jnp.zeros_like(count_ref)
    k = 8 * PROWS

    def count_group(g, _):
        cells.wait(g)
        cell = lanes_of(cell_in, g, PROWS)
        ones = jnp.ones((CH, k), F32)
        for l in range(LO):
            count_ref[...] += lax.dot_general(
                one_hot(cell[l] & (CHI - 1), 0, CHI),
                spread(ones, cell[l] >> 8),
                NT,
                preferred_element_type=F32,
            )
        return 0

    lax.fori_loop(0, 4, count_group, 0)

    def second_group(g, _):
        second.wait(g)
        turned = second_in[pl.ds(g * 8, 8)].reshape(k, LO * CH).T
        cell = lanes_of(cell_in, g, PROWS)
        for l in range(LO):
            sum_ref[...] += lax.dot_general(
                one_hot(cell[l] & (CHI - 1), 0, CHI),
                spread(turned[l * CH : (l + 1) * CH], cell[l] >> 8),
                NT,
                preferred_element_type=F32,
            )
        return 0

    lax.fori_loop(0, 4, second_group, 0)
    mean = (sum_ref[...] / jnp.maximum(count_ref[...], 1.0)).T.astype(BF)
    mean_ref[...] = mean.reshape(BANDS, CH, CHI)

    def give_group(g, _):
        cell = lanes_of(cell_in, g, PROWS)
        means_of = mean_ref[...].reshape(C, CHI)
        for l in range(LO):
            product = jnp.dot(
                means_of, one_hot(cell[l] & (CHI - 1), 0, CHI), preferred_element_type=F32
            )
            turned_ref[l * CH : (l + 1) * CH, :] = gather_low(
                product, cell[l] >> 8, CH
            ).astype(BF)
        back_out[pl.ds(g * 8, 8)] = turned_ref[...].T.reshape(8, PROWS, LO * CH)
        back.start(g)
        return 0

    lax.fori_loop(0, 4, give_group, 0)
    means.start()

    def take_group(g, _):
        back.wait(g)
        turned_ref[...] = back_in[pl.ds(g * 8, 8)].reshape(k, LO * CH).T
        for half_of in range(2):
            for j in range(half_of * 4, half_of * 4 + 4):
                product = jnp.dot(
                    turned_ref[...],
                    one_hot(p_row_ref[j : j + 1, :], g * k, k),
                    preferred_element_type=F32,
                )
                part = gather_low(product, p_low_ref[j : j + 1, :], CH)
                before = jnp.where(g == 0, 0.0, point_out[j].astype(F32))
                point_out[j] = (before + part).astype(BF)

            @pl.when(g == 3)
            def _():
                points.start_half(half_of)

        return 0

    point_out[...] = jnp.zeros_like(point_out)
    lax.fori_loop(0, 4, take_group, 0)
    means.wait()

    for n in range(BANDS):
        table_out[n] = gelu(
            jnp.dot(weights_ref[n, 4 * CH :, :], mean_in[...].reshape(C, CHI), preferred_element_type=F32)
        )
    tables.start()
    points.wait()

    def project_for(step, _):
        n = (mine + step) % BANDS
        result_out[n] = gelu(
            jnp.dot(
                weights_ref[n, 4 * CH :, :],
                point_in[...].reshape(C, PATCH),
                preferred_element_type=F32,
            )
        )

        @pl.when(step != BANDS)
        def _():
            results.copy(step).start()

        return 0

    lax.fori_loop(1, BANDS + 1, project_for, 0)
    result_in[mine] = result_out[mine]
    results.wait()
    tables.wait()
    for each in (landings, first, cells, second, back):
        each.finish()
    for each in (gather, patches, blocks, stats, means, tables, points, results):
        each.finish()


def settle_kernel(block_in, table_in, result_in, block_ref, coarse_ref, unpooled_ref):
    for n in range(BANDS):
        block_ref[:, n * PATCH : (n + 1) * PATCH] = block_in[n]
        coarse_ref[:, n * CHI : (n + 1) * CHI] = table_in[n]
        unpooled_ref[:, n * PATCH : (n + 1) * PATCH] = result_in[n]


def on_device(feats, hilbert_pos, ln_attn, w_qkv, w_proj, ln_pool, w_pool, cell_of):
    small = lambda: pltpu.VMEM((BANDS, PATCH), jnp.int32)
    table = lambda: pltpu.VMEM((GROUPS, 4, TAB), jnp.int32)
    half = lambda *dims: pltpu.VMEM(dims, BF)
    full = lambda *dims: pltpu.VMEM(dims, F32)
    settle = pl.pallas_call(
        settle_kernel,
        out_shape=[
            jax.ShapeDtypeStruct((CH, POINTS), BF),
            jax.ShapeDtypeStruct((CH2, CELLS), BF),
            jax.ShapeDtypeStruct((CH2, POINTS), BF),
        ],
        in_specs=[INSIDE] * 3,
        out_specs=[INSIDE] * 3,
        compiler_params=pltpu.CompilerParams(vmem_limit_bytes=60 * 1024 * 1024),
    )
    return tuple(
        settle(*pl.pallas_call(
            kernel,
            out_shape=[
                jax.ShapeDtypeStruct((BANDS, CH, PATCH), BF),
                jax.ShapeDtypeStruct((BANDS, CH2, CHI), BF),
                jax.ShapeDtypeStruct((BANDS, CH2, PATCH), BF),
            ],
            in_specs=[INSIDE] * 8,
            out_specs=[INSIDE] * 3,
            scratch_shapes=[
                half(6 * CH, C),
                small(), small(), small(), small(),
                table(), table(), table(), table(),
                half(LO * CH, POINTS),
                half(GROUPS, HROWS, LO * CH), half(GROUPS, HROWS, LO * CH),
                full(PATCH, LO * CH),
                half(BANDS, PATCH // LO, LO * CH), half(BANDS, PATCH // LO, LO * CH),
                half(BANDS, 6 * CH, C),
                half(C, PATCH), half(C, PATCH), half(C, PATCH), half(C, PATCH), half(C, PATCH),
                half(PATCH, C), half(2, C, PATCH), half(2, 2 * HD, PATCH),
                full(2, PATCH, COLS), full(2, 8, COLS), half(2, PATCH, COLS),
                half(BANDS, CH, PATCH), full(2, PATCH), full(BANDS, 2, PATCH),
                half(GROUPS, PROWS, LO * CH), half(GROUPS, PROWS, LO * CH),
                full(CHI, LO * CH), full(CHI, LO * CH),
                half(BANDS, CH, CHI), half(BANDS, CH, CHI), half(BANDS, CH2, CHI),
                half(LO * CH, 8 * PROWS),
                half(GROUPS, PROWS, LO * CH), half(GROUPS, PROWS, LO * CH),
                half(BANDS, CH, PATCH), half(BANDS, CH, PATCH), half(BANDS, CH2, PATCH),
                pltpu.SemaphoreType.DMA((5, GROUPS)), pltpu.SemaphoreType.DMA((5, GROUPS)),
                pltpu.SemaphoreType.DMA((8, BANDS)), pltpu.SemaphoreType.DMA((8, BANDS)),
            ],
            compiler_params=pltpu.CompilerParams(
                collective_id=0, has_side_effects=True, vmem_limit_bytes=56 * 1024 * 1024
            ),
        )(
            feats,
            hilbert_pos.reshape(1, POINTS),
            cell_of.reshape(1, POINTS),
            w_qkv.transpose(0, 2, 1).reshape(-1, C),
            w_proj,
            w_pool.T,
            ln_attn.reshape(1, C),
            ln_pool.reshape(1, C),
        ))
    )


def solution(mesh):
    in_specs = (
        P("narrow", "wide"),
        P("wide"),
        P(),
        P(None, None, "narrow"),
        P("narrow", None),
        P(),
        P(None, "narrow"),
        P("wide"),
    )
    out_specs = (P("narrow", "wide"), P("narrow", "wide"), P("narrow", "wide"))
    return jax.shard_map(
        on_device, mesh=mesh, in_specs=in_specs, out_specs=out_specs, check_vma=False
    )
```
